128 devices in a mesh: group: 4 (over x), local: 32 (over z, y, core).
Axes of the slice: x: 4, y: 4, z: 4, core: 2. Of those that a mesh axis runs over, the one named last changes fastest.
Arguments:
- x_q: bfloat16 [2048, 4096], P(('group', 'local')), may hold values from -6 to 6
- x_scale: float32 [2048, 32], P(('group', 'local')), may hold values from 0.25 to 4, as said below
- cotangent: bfloat16 [2048, 4096], P(('group', 'local')), may hold values from -6 to 6
- gates: bfloat16 [2048, 8], P(('group', 'local')), may hold values from 0.049804688 to 0.5
- experts: int32 [2048, 8], P(('group', 'local')), may hold values from 0 to 63, as said below
- replicas: int32 [2048, 8], P(('group', 'local')), may hold values from 0 to 1, as said below
- slots: int32 [2048, 8], P(('group', 'local')), may hold values from 0 to 255, as said below
- w_gate_q: bfloat16 [8192, 32, 768], P('group', 'local'), may hold values from -0.09375 to 0.09375
- w_up_q: bfloat16 [8192, 32, 768], P('group', 'local'), may hold values from -0.09375 to 0.09375
- w_down_q: bfloat16 [8192, 32, 768], P('group', 'local'), may hold values from -0.21875 to 0.21875
- gate_scales: float32 [64, 32, 6], P('group', 'local'), may hold values from 0.5 to 2, as said below
- up_scales: float32 [64, 32, 6], P('group', 'local'), may hold values from 0.5 to 2, as said below
- down_scales: float32 [64, 32, 6], P('group', 'local'), may hold values from 0.5 to 2, as said below
Outputs:
- grad_tokens: bfloat16 [2048, 4096], P(('group', 'local'))
- grad_gates: bfloat16 [2048, 8], P(('group', 'local'))
- grad_gate: bfloat16 [8192, 32, 768], P('group', 'local')
- grad_up: bfloat16 [8192, 32, 768], P('group', 'local')
- grad_down: bfloat16 [8192, 32, 768], P('group', 'local')
The draws below stay inside these ranges and needn't reach their ends.
Inputs may be any that keep to these rules, and one draw needn't show every extreme that they name: Each token names 8 distinct experts; no expert is named more than 2 * 2 times by the tokens of one device (aligned blocks of 16 tokens). `replicas`: the copies of the tokens of one device reach one replica device at most 2 times; in every block some replica device receives exactly 2. `slots`: the slot of a copy is the number of earlier copies, in token order and then choice order, that go to the same replica device. `x_scale`: every entry is a power of two. `gate_scales`: every entry is a power of two. `up_scales`: every entry is a power of two. `down_scales`: every entry is a power of two.
All inputs are finite; a program needn't handle non-finite values.
Results may differ from the reference program's by a relative error of at most 0.0075.
Values may be sent and summed in bfloat16 or wider, within the bound.
No kernel may reach another device: no remote copies, remote signals or barrier semaphores. Data moves between devices by JAX's collectives and lax.ppermute only.
A program may use at most 128 MiB of HBM per device.

```python
import math
import jax
import jax.numpy as jnp
from jax import lax

D = 4096
H = 768
TOP = 8
TOK_DEV = 16
SETS = 2
EXPERTS = 64
TOKENS = 2048
PAIR = 2
CAP = 192
N_LOCAL = 32
DEVICES = 128


def route_all(key):
    key = jax.random.fold_in(key, 11)
    k_pop, k_noise, k_coin = jax.random.split(key, 3)
    blocks = TOKENS // TOK_DEV
    spread = 4096
    popular = jax.random.permutation(k_pop, EXPERTS).astype(jnp.int32)
    base = 2 * spread // (popular + 1)
    noise = jax.random.randint(k_noise, (blocks, TOK_DEV, EXPERTS), 0, spread).astype(jnp.int32)
    coins = jax.random.randint(k_coin, (blocks, TOK_DEV, TOP), 0, 2).astype(jnp.int32)
    limit = 2 * PAIR
    ids = jnp.arange(EXPERTS, dtype=jnp.int32)
    sides = jnp.arange(2, dtype=jnp.int32)

    def one_block(noise_block, coin_block):

        def step(carry, inputs):
            count, side_count = carry
            noise_row, coin_row = inputs
            score = (base + noise_row) * EXPERTS + ids
            score = jnp.where(count < limit, score, -1)
            chosen = lax.top_k(score, TOP)[1].astype(jnp.int32)
            first = side_count[chosen, 0]
            second = side_count[chosen, 1]
            side = jnp.where(first < second, 0, jnp.where(second < first, 1, coin_row)).astype(jnp.int32)
            hit = (chosen[:, None] == ids[None, :]).astype(jnp.int32)
            side_hot = (side[:, None] == sides[None, :]).astype(jnp.int32)
            count = count + jnp.sum(hit, axis=0)
            side_count = side_count + jnp.sum(hit[:, :, None] * side_hot[:, None, :], axis=0)
            return ((count, side_count), (chosen, side))
        start = (jnp.zeros((EXPERTS,), jnp.int32), jnp.zeros((EXPERTS, 2), jnp.int32))
        return lax.scan(step, start, (noise_block, coin_block))[1]
    chosen, side = jax.vmap(one_block)(noise, coins)
    experts = chosen.reshape(TOKENS, TOP)
    replicas = side.reshape(TOKENS, TOP)
    expert_flat = experts.reshape(-1)
    target = (2 * (expert_flat // N_LOCAL) + replicas.reshape(-1)) * N_LOCAL + expert_flat % N_LOCAL
    onehot = (target[:, None] == jnp.arange(DEVICES, dtype=jnp.int32)[None, :]).astype(jnp.int32)
    earlier = jnp.cumsum(onehot, axis=0) - onehot
    slots = jnp.sum(earlier * onehot, axis=1).reshape(TOKENS, TOP).astype(jnp.int32)
    return (experts, replicas, slots)


def draw_experts(key, part):
    return route_all(key)[0]


def draw_replicas(key, part):
    return route_all(key)[1]


def draw_slots(key, part):
    return route_all(key)[2]


def draw_x_scale(key, part):
    levels = jnp.array([0.25, 0.5, 1.0, 2.0, 4.0], jnp.float32)
    pick = jax.random.randint(jax.random.fold_in(key, 21), (TOKENS, D // 128), 0, 5)
    return levels[pick]


def block_scales(key, salt):
    levels = jnp.array([0.5, 1.0, 2.0], jnp.float32)
    pick = jax.random.randint(jax.random.fold_in(key, salt), (SETS * D // 128, N_LOCAL, H // 128), 0, 3)
    return levels[pick]


def draw_gate_scales(key, part):
    return block_scales(key, 31)


def draw_up_scales(key, part):
    return block_scales(key, 32)


def draw_down_scales(key, part):
    return block_scales(key, 33)


def level_of(own_key, dims, cuts, low, high):
    loudness = 1.0
    for position, shards_of in cuts:
        steps = jax.random.uniform(jax.random.fold_in(jax.random.fold_in(own_key, 6), position), (shards_of,), jnp.float32, low / len(cuts), high / len(cuts))
        loudness = loudness * jnp.repeat(jnp.exp(steps), dims[position] // shards_of).reshape((-1,) + (1,) * (len(dims) - 1 - position))
    return loudness


def bell_draw(key, extent, scale, bound, cuts=(), kind=jnp.bfloat16):
    factor_of = level_of(key, extent, cuts, -0.22, 0.18) if cuts else 1.0
    drawn = jax.random.normal(key, extent, jnp.float32) * scale * factor_of
    return jnp.minimum(jnp.maximum(drawn, -bound), bound).astype(kind)


def setup_inputs(seed: int = 0) -> dict:
    arg_keys = jax.random.split(jax.random.key(seed), 14)
    x_q = bell_draw(arg_keys[0], (TOKENS, D), 1.0, 6.0, ((0, 128),))
    x_scale = draw_x_scale(jax.random.fold_in(arg_keys[13], 71), 0)
    cotangent = bell_draw(arg_keys[2], (TOKENS, D), 1.0, 6.0, ((0, 128),))
    gates = jnp.clip(jnp.exp(math.log(0.5) - 2.306499 * jax.random.uniform(arg_keys[3], (TOKENS, TOP), jnp.float32) ** level_of(arg_keys[3], (TOKENS, TOP), ((0, 128),), -0.2, 0.2)), 0.049804688, 0.5).astype(jnp.bfloat16)
    experts = draw_experts(jax.random.fold_in(arg_keys[13], 71), 0)
    replicas = draw_replicas(jax.random.fold_in(arg_keys[13], 71), 0)
    slots = draw_slots(jax.random.fold_in(arg_keys[13], 71), 0)
    w_gate_q = bell_draw(arg_keys[7], (SETS * D, N_LOCAL, H), D ** -0.5, 0.09375, ((0, 4), (1, 32)))
    w_up_q = bell_draw(arg_keys[8], (SETS * D, N_LOCAL, H), D ** -0.5, 0.09375, ((0, 4), (1, 32)))
    w_down_q = bell_draw(arg_keys[9], (SETS * D, N_LOCAL, H), H ** -0.5, 0.21875, ((0, 4), (1, 32)))
    gate_scales = draw_gate_scales(jax.random.fold_in(arg_keys[13], 71), 0)
    up_scales = draw_up_scales(jax.random.fold_in(arg_keys[13], 71), 0)
    down_scales = draw_down_scales(jax.random.fold_in(arg_keys[13], 71), 0)
    return dict(x_q=x_q, x_scale=x_scale, cotangent=cotangent, gates=gates, experts=experts, replicas=replicas, slots=slots, w_gate_q=w_gate_q, w_up_q=w_up_q, w_down_q=w_down_q, gate_scales=gate_scales, up_scales=up_scales, down_scales=down_scales)


def contract_rows(left, right):
    return lax.dot_general(left, right, (((0,), (0,)), ((), ())), preferred_element_type=jnp.float32)


def contract_last(left, right):
    return lax.dot_general(left, right, (((1,), (1,)), ((), ())), preferred_element_type=jnp.float32)


def expert_backward(rows_x, rows_dy, rows_gate, w_gate, w_up, w_down):
    act_a = jnp.dot(rows_x, w_gate, preferred_element_type=jnp.float32)
    act_b = jnp.dot(rows_x, w_up, preferred_element_type=jnp.float32)
    sigma = jax.nn.sigmoid(act_a)
    silu_a = act_a * sigma
    hidden = (silu_a * act_b).astype(jnp.bfloat16)
    output = contract_last(hidden, w_down)
    grad_gate_rows = jnp.sum(rows_dy.astype(jnp.float32) * output, axis=1).astype(jnp.bfloat16)
    scaled = (rows_gate.astype(jnp.float32)[:, None] * rows_dy.astype(jnp.float32)).astype(jnp.bfloat16)
    d_hidden = jnp.dot(scaled, w_down, preferred_element_type=jnp.float32)
    d_gate_act = (d_hidden * act_b * sigma * (1.0 + act_a * (1.0 - sigma))).astype(jnp.bfloat16)
    d_up_act = (d_hidden * silu_a).astype(jnp.bfloat16)
    grad_rows = (contract_last(d_gate_act, w_gate) + contract_last(d_up_act, w_up)).astype(jnp.bfloat16)
    term_gate = contract_rows(rows_x, d_gate_act).astype(jnp.bfloat16)
    term_up = contract_rows(rows_x, d_up_act).astype(jnp.bfloat16)
    term_down = contract_rows(scaled, hidden).astype(jnp.bfloat16)
    return grad_rows, grad_gate_rows, term_gate, term_up, term_down


def expert_weight(quant, scales, set_index, local_index):
    blocks = quant.reshape(SETS, D, N_LOCAL, H)
    block = blocks[set_index, :, local_index, :]
    scale_blocks = scales.reshape(SETS, D // 128, N_LOCAL, H // 128)
    scale = scale_blocks[set_index, :, local_index, :]
    scale = jnp.repeat(jnp.repeat(scale, 128, axis=0), 128, axis=1)
    return (block.astype(jnp.float32) * scale).astype(jnp.bfloat16)


def reference(x_q, x_scale, cotangent, gates, experts, replicas, slots, w_gate_q, w_up_q, w_down_q, gate_scales, up_scales, down_scales):
    tokens = (x_q.astype(jnp.float32) * jnp.repeat(x_scale, 128, axis=1)).astype(jnp.bfloat16)
    copies = TOKENS * TOP
    expert_flat = experts.reshape(-1).astype(jnp.int32)
    replica_flat = replicas.reshape(-1).astype(jnp.int32)
    slot_flat = slots.reshape(-1).astype(jnp.int32)
    target = (2 * (expert_flat // N_LOCAL) + replica_flat) * N_LOCAL + expert_flat % N_LOCAL
    place = jnp.where(slot_flat < CAP, target * CAP + slot_flat, DEVICES * CAP).astype(jnp.int32)
    table = jnp.full((DEVICES * CAP,), copies, jnp.int32).at[place].set(jnp.arange(copies, dtype=jnp.int32), mode="drop")
    table = table.reshape(DEVICES, CAP)
    token_ext = jnp.concatenate([tokens, jnp.zeros((1, D), jnp.bfloat16)], axis=0)
    cot_ext = jnp.concatenate([cotangent, jnp.zeros((1, D), jnp.bfloat16)], axis=0)
    gate_ext = jnp.concatenate([gates.reshape(-1), jnp.zeros((1,), jnp.bfloat16)], axis=0)

    def one_expert(index):
        set_index = (index // N_LOCAL).astype(jnp.int32)
        local_index = (index % N_LOCAL).astype(jnp.int32)
        w_gate = expert_weight(w_gate_q, gate_scales, set_index, local_index)
        w_up = expert_weight(w_up_q, up_scales, set_index, local_index)
        w_down = expert_weight(w_down_q, down_scales, set_index, local_index)
        results = []
        for replica in range(2):
            device = ((2 * set_index + replica) * N_LOCAL + local_index).astype(jnp.int32)
            copy_ids = table[device]
            results.append(expert_backward(token_ext[copy_ids // TOP], cot_ext[copy_ids // TOP], gate_ext[copy_ids], w_gate, w_up, w_down))
        grads = [(results[0][m].astype(jnp.float32) + results[1][m].astype(jnp.float32)).astype(jnp.bfloat16) for m in (2, 3, 4)]
        return jnp.stack([results[0][0], results[1][0]]), jnp.stack([results[0][1], results[1][1]]), grads[0], grads[1], grads[2]

    dx_all, dg_all, g_gate, g_up, g_down = lax.map(one_expert, jnp.arange(EXPERTS, dtype=jnp.int32))
    index_e = jnp.arange(EXPERTS, dtype=jnp.int32)
    devices = jnp.stack([(2 * (index_e // N_LOCAL) + rep) * N_LOCAL + index_e % N_LOCAL for rep in range(2)], axis=1).astype(jnp.int32)
    copy_ids = table[devices].reshape(-1)
    dx_copies = jnp.zeros((copies + 1, D), jnp.bfloat16).at[copy_ids].set(dx_all.reshape(-1, D))
    dg_copies = jnp.zeros((copies + 1,), jnp.bfloat16).at[copy_ids].set(dg_all.reshape(-1))
    grad_tokens = dx_copies[:copies].reshape(TOKENS, TOP, D).astype(jnp.float32).sum(axis=1).astype(jnp.bfloat16)
    grad_gates = dg_copies[:copies].reshape(TOKENS, TOP)

    def relayout(grad):
        return grad.reshape(SETS, N_LOCAL, D, H).transpose(0, 2, 1, 3).reshape(SETS * D, N_LOCAL, H)

    return grad_tokens, grad_gates, relayout(g_gate), relayout(g_up), relayout(g_down)
```

```python
import functools

import jax
import jax.numpy as jnp
from jax import lax
from jax.experimental import pallas as pl
from jax.experimental.pallas import tpu as pltpu
from jax.sharding import PartitionSpec as P

CAP = 192
META = 128
CODE, SLOT, GATE = 0, 8, 16
BF = jnp.bfloat16
F32 = jnp.float32
VMEM_LIMIT = 48 * 1024 * 1024

ROWS = (((0,), (0,)), ((), ()))
LAST = (((1,), (1,)), ((), ()))


def dot(left, right, dims=(((1,), (0,)), ((), ()))):
    return lax.dot_general(left, right, dims, preferred_element_type=F32)


def call(kernel, outs, args, flops=0, moved=0, **kw):
    return pl.pallas_call(
        kernel,
        out_shape=outs,
        compiler_params=pltpu.CompilerParams(vmem_limit_bytes=VMEM_LIMIT),
        cost_estimate=pl.CostEstimate(flops=flops, bytes_accessed=moved, transcendentals=0),
        **kw,
    )(*args)


SMEM = pl.BlockSpec(memory_space=pltpu.SMEM)
VMEM = pl.BlockSpec(memory_space=pltpu.VMEM)


def prepare_kernel(place_ref, xq_ref, xs_ref, dy_ref, meta_ref, same_x, other_x, same_dy, other_dy):
    half = xq_ref.shape[1] // 2
    blocks = half // 128
    first = lax.rem(place_ref[0], 2) == 0
    for c in range(blocks):
        low, high = c * 128, half + c * 128
        x_low = (xq_ref[:, low : low + 128].astype(F32) * xs_ref[:, c : c + 1]).astype(BF)
        x_high = (
            xq_ref[:, high : high + 128].astype(F32) * xs_ref[:, blocks + c : blocks + c + 1]
        ).astype(BF)
        same_x[:, low : low + 128] = jnp.where(first, x_low, x_high)
        other_x[:, low : low + 128] = jnp.where(first, x_high, x_low)
    same_x[:, half:] = meta_ref[...]
    other_x[:, half:] = meta_ref[...]
    dy_low, dy_high = dy_ref[:, :half], dy_ref[:, half:]
    same_dy[...] = jnp.where(first, dy_low, dy_high)
    other_dy[...] = jnp.where(first, dy_high, dy_low)


def matches(meta, k, base, count):
    lane = lax.broadcasted_iota(jnp.int32, (meta.shape[0], count), 1).astype(F32)
    code = meta[:, CODE + k : CODE + k + 1] - base
    return (code == lane) | (code - 64.0 == lane)


def owner_of_row(rows, count, per):
    row = lax.broadcasted_iota(jnp.int32, (rows, count), 0)
    lane = lax.broadcasted_iota(jnp.int32, (rows, count), 1)
    return lax.div(row, per) == lane


def pack_x_kernel(n_local, top, place_ref, b0, b1, b2, b3, out_ref, pick_ref, gated_ref, meta_out):
    half = b0.shape[1] - META
    tokens = jnp.concatenate([b[...] for b in (b0, b1, b2, b3)], axis=0)
    meta = tokens[:, half:].astype(F32)
    count = tokens.shape[0]
    base = (1 + lax.div(place_ref[0], 2) * n_local).astype(F32)
    named = jnp.zeros((count, n_local), F32)
    gate = jnp.zeros((count, n_local), F32)
    for k in range(top):
        hit = matches(meta, k, base, n_local) & (meta[:, SLOT + k : SLOT + k + 1] < CAP)
        named = jnp.where(hit, 1.0, named)
        gate = jnp.where(hit, meta[:, GATE + k : GATE + k + 1], gate)
    row = lax.broadcasted_iota(jnp.int32, (count, count), 0)
    col = lax.broadcasted_iota(jnp.int32, (count, count), 1)
    before = jnp.where(col < row, 1.0, 0.0).astype(BF)
    rank = jnp.where(named > 0.0, dot(before, named.astype(BF)), -1.0)
    rows = out_ref.shape[0]
    per = rows // n_local
    spread = jnp.where(owner_of_row(rows, n_local, per), 1.0, 0.0).astype(BF)
    rank_rows = dot(spread, rank.astype(BF), LAST)
    gate_rows = dot(spread, gate.astype(BF), LAST)
    position = lax.rem(lax.broadcasted_iota(jnp.int32, (rows, count), 0), per).astype(F32)
    hit = rank_rows == position
    pick = jnp.where(hit, 1.0, 0.0).astype(BF)
    pick_ref[...] = pick
    gated_ref[...] = jnp.where(hit, gate_rows, 0.0).astype(BF)
    meta_out[...] = meta.astype(BF)
    out_ref[...] = dot(pick, tokens).astype(BF)


def pack_dy_kernel(gated_ref, b0, b1, b2, b3, out_ref):
    tokens = jnp.concatenate([b[...] for b in (b0, b1, b2, b3)], axis=0)
    out_ref[...] = dot(gated_ref[...], tokens).astype(BF)


def forward_kernel(
    n_local, top, place_ref, x_ref, meta_ref, wg_ref, wu_ref, kept_ref, part_ref, send_ref, slot_ref
):
    step = pl.program_id(0)
    hidden = wg_ref.shape[1]

    @pl.when(step == 0)
    def _():
        meta = meta_ref[...].astype(F32)
        own = (1 + lax.div(place_ref[0], 2) * n_local + place_ref[1]).astype(F32)
        target = jnp.full((meta.shape[0], 1), -1.0, F32)
        for k in range(top):
            code = meta[:, CODE + k : CODE + k + 1]
            slot = meta[:, SLOT + k : SLOT + k + 1]
            target = jnp.where(code == own, slot, target)
            target = jnp.where(code == own + 64.0, slot + CAP, target)
        lane = lax.broadcasted_iota(jnp.int32, slot_ref.shape, 1).astype(F32)
        slot_ref[...] = jnp.where(lane == target, 1.0, 0.0).astype(BF)
        part_ref[...] = jnp.zeros_like(part_ref)

    kept = dot(slot_ref[...], x_ref[...], ROWS).astype(BF)
    kept_ref[...] = kept
    part_ref[:, :hidden] += dot(kept, wg_ref[...])
    part_ref[:, hidden:] += dot(kept, wu_ref[...])

    @pl.when(step == pl.num_programs(0) - 1)
    def _():
        send_ref[...] = part_ref[...].astype(BF)


def down_kernel(slot_ref, dy_ref, v_ref, kept_ref, part_ref, send_ref):
    step = pl.program_id(0)

    @pl.when(step == 0)
    def _():
        part_ref[...] = jnp.zeros_like(part_ref)

    kept = dot(slot_ref[...], dy_ref[...], ROWS).astype(BF)
    kept_ref[...] = kept
    part_ref[...] += dot(kept, v_ref[...])

    @pl.when(step == pl.num_programs(0) - 1)
    def _():
        send_ref[...] = part_ref[...].astype(BF)


def backward_kernel(
    ab_ref, ab_in, dh_ref, dh_in, slot_ref, wg_ref, wu_ref, da_out, db_out, hid_out, dx_ref, wide
):
    step = pl.program_id(0)
    hidden = wg_ref.shape[1]
    chunk = wg_ref.shape[0]
    width = dx_ref.shape[1] - META

    @pl.when(step == 0)
    def _():
        ab = ab_ref[...] + ab_in[...].astype(F32)
        d_hidden = dh_ref[...] + dh_in[...].astype(F32)
        act_a, act_b = ab[:, :hidden], ab[:, hidden:]
        sigma = jax.nn.sigmoid(act_a)
        silu_a = act_a * sigma
        hid = (silu_a * act_b).astype(BF)
        d_a = (d_hidden * act_b * sigma * (1.0 + act_a * (1.0 - sigma))).astype(BF)
        d_b = (d_hidden * silu_a).astype(BF)
        da_out[...] = d_a
        db_out[...] = d_b
        hid_out[...] = hid
        wide[:, :hidden] = dot(slot_ref[...], d_a).astype(BF)
        wide[:, hidden:] = dot(slot_ref[...], d_b).astype(BF)
        grad = jnp.sum(hid.astype(F32) * d_hidden, axis=1, keepdims=True)
        high = grad.astype(BF).astype(F32)
        lane = lax.broadcasted_iota(jnp.int32, (grad.shape[0], META), 1)
        both = jnp.where(lane == 0, high, jnp.where(lane == 1, grad - high, 0.0)).astype(BF)
        dx_ref[:, width:] = dot(slot_ref[...], both).astype(BF)

    dx = dot(wide[:, :hidden], wg_ref[...], LAST) + dot(wide[:, hidden:], wu_ref[...], LAST)
    dx_ref[:, pl.ds(pl.multiple_of(step * chunk, chunk), chunk)] = dx.astype(BF)


def combine_kernel(n_local, top, place_ref, ret_ref, pick_ref, meta_ref, *outs):
    width = ret_ref.shape[1] - META
    pick = pick_ref[...]
    meta = meta_ref[...].astype(F32)
    total = dot(pick, ret_ref[:, :width], ROWS).astype(BF)
    rows = ret_ref.shape[0]
    owner = owner_of_row(rows, n_local, rows // n_local)
    grads = ret_ref[:, width:].astype(F32)
    high = jnp.where(owner, grads[:, 0:1], 0.0).astype(BF)
    low = jnp.where(owner, grads[:, 1:2], 0.0).astype(BF)
    by_expert = dot(pick, high, ROWS) + dot(pick, low, ROWS)
    base = (1 + lax.div(place_ref[0], 2) * n_local).astype(F32)
    lane = lax.broadcasted_iota(jnp.int32, meta.shape, 1)
    tail = jnp.zeros(meta.shape, F32)
    for k in range(top):
        hit = matches(meta, k, base, n_local) & (meta[:, SLOT + k : SLOT + k + 1] < CAP)
        value = jnp.sum(jnp.where(hit, by_expert, 0.0), axis=1, keepdims=True)
        tail = jnp.where(lane == k, value / meta[:, GATE + k : GATE + k + 1], tail)
    tail = tail.astype(BF)
    block = outs[0].shape[0]
    for m, out in enumerate(outs):
        out[:, :width] = total[m * block : (m + 1) * block]
        out[:, width:] = tail[m * block : (m + 1) * block]


def finish_kernel(place_ref, b0, b1, b2, b3, tokens_ref, gates_ref):
    half = tokens_ref.shape[1] // 2
    first = lax.rem(place_ref[0], 2) == 0
    own = b0[...].astype(F32) + b2[...].astype(F32)
    other = b1[:, :half].astype(F32) + b3[:, :half].astype(F32)
    mine = own[:, :half]
    tokens_ref[:, :half] = jnp.where(first, mine, other).astype(BF)
    tokens_ref[:, half:] = jnp.where(first, other, mine).astype(BF)
    gates_ref[...] = own[:, half : half + gates_ref.shape[1]].astype(BF)


def dequant_half(quant, scales):
    scale = jnp.repeat(jnp.repeat(scales[:, 0, :], 128, axis=0), 128, axis=1)
    return (quant[:, 0, :].astype(F32) * scale).astype(BF)


def shape(*dims, dtype=BF):
    return jax.ShapeDtypeStruct(dims, dtype)


def shards(
    x_q,
    x_scale,
    cotangent,
    gates,
    experts,
    replicas,
    slots,
    w_gate_q,
    w_up_q,
    w_down_q,
    gate_scales,
    up_scales,
    down_scales,
):
    n_group = lax.axis_size("group")
    n_local = lax.axis_size("local")
    tok, width = x_q.shape
    top = experts.shape[1]
    half = width // 2
    hidden = w_gate_q.shape[2]
    column = n_group * tok
    rows = n_local * n_group * 4
    kept = 2 * CAP
    wide = half + META
    place = jnp.stack([lax.axis_index("group"), lax.axis_index("local")]).astype(jnp.int32)

    def across(block, apart):
        return lax.ppermute(block, "group", [(i, i ^ apart) for i in range(n_group)])

    def spread(block):
        return lax.all_to_all(block, "local", split_axis=0, concat_axis=0, tiled=True)

    meta = jnp.concatenate(
        [
            (1 + experts + 64 * replicas).astype(BF),
            slots.astype(BF),
            gates,
            jnp.zeros((tok, META - 3 * top), BF),
        ],
        axis=1,
    )
    same_x, other_x, same_dy, other_dy = call(
        prepare_kernel,
        (shape(tok, wide), shape(tok, wide), shape(tok, half), shape(tok, half)),
        (place, x_q, x_scale, cotangent, meta),
        moved=tok * width * 8,
        in_specs=[SMEM] + [VMEM] * 4,
        out_specs=[VMEM] * 4,
    )
    near_x = [same_x, across(other_x, 1), across(same_x, 2), across(other_x, 3)]
    near_dy = [same_dy, across(other_dy, 1), across(same_dy, 2), across(other_dy, 3)]
    packed_x, pick, gated, column_meta = call(
        functools.partial(pack_x_kernel, n_local, top),
        (shape(rows, wide), shape(rows, column), shape(rows, column), shape(column, META)),
        (place, *near_x),
        flops=2 * rows * column * wide,
        moved=2 * rows * wide,
        in_specs=[SMEM] + [VMEM] * 4,
        out_specs=[VMEM] * 4,
    )
    packed_dy = call(
        pack_dy_kernel,
        shape(rows, half),
        (gated, *near_dy),
        flops=2 * rows * column * half,
        moved=2 * rows * half,
        in_specs=[VMEM] * 5,
        out_specs=VMEM,
    )
    w_gate = dequant_half(w_gate_q, gate_scales)
    w_up = dequant_half(w_up_q, up_scales)
    w_down = dequant_half(w_down_q, down_scales)
    got_x = spread(packed_x)
    got_x, packed_dy = lax.optimization_barrier((got_x, packed_dy))
    got_dy = spread(packed_dy)

    chunk = 512
    steps = half // chunk
    whole = lambda *dims: pl.BlockSpec(dims, lambda i: (0,) * len(dims))
    rows_x, part_ab, send_ab, slot_of = call(
        functools.partial(forward_kernel, n_local, top),
        (
            shape(kept, half),
            shape(kept, 2 * hidden, dtype=F32),
            shape(kept, 2 * hidden),
            shape(rows, kept),
        ),
        (place, got_x, got_x, w_gate, w_up),
        flops=4 * kept * half * hidden,
        moved=4 * half * hidden + 4 * rows * half,
        grid=(steps,),
        in_specs=[
            SMEM,
            pl.BlockSpec((rows, chunk), lambda i: (0, i)),
            pl.BlockSpec((rows, META), lambda i: (0, half // META)),
            pl.BlockSpec((chunk, hidden), lambda i: (i, 0)),
            pl.BlockSpec((chunk, hidden), lambda i: (i, 0)),
        ],
        out_specs=[
            pl.BlockSpec((kept, chunk), lambda i: (0, i)),
            whole(kept, 2 * hidden),
            whole(kept, 2 * hidden),
            whole(rows, kept),
        ],
    )
    their_ab = across(send_ab, 1)
    rows_dy, part_dh, send_dh = call(
        down_kernel,
        (shape(kept, half), shape(kept, hidden, dtype=F32), shape(kept, hidden)),
        (slot_of, got_dy, w_down),
        flops=2 * kept * half * hidden,
        moved=2 * half * hidden + 4 * rows * half,
        grid=(steps,),
        in_specs=[
            whole(rows, kept),
            pl.BlockSpec((rows, chunk), lambda i: (0, i)),
            pl.BlockSpec((chunk, hidden), lambda i: (i, 0)),
        ],
        out_specs=[
            pl.BlockSpec((kept, chunk), lambda i: (0, i)),
            whole(kept, hidden),
            whole(kept, hidden),
        ],
    )
    their_dh = across(send_dh, 1)
    d_a, d_b, hid, dx = call(
        backward_kernel,
        (shape(kept, hidden), shape(kept, hidden), shape(kept, hidden), shape(rows, wide)),
        (part_ab, their_ab, part_dh, their_dh, slot_of, w_gate, w_up),
        flops=4 * rows * half * hidden,
        moved=4 * half * hidden + 2 * rows * half,
        grid=(steps,),
        in_specs=[
            whole(kept, 2 * hidden),
            whole(kept, 2 * hidden),
            whole(kept, hidden),
            whole(kept, hidden),
            whole(rows, kept),
            pl.BlockSpec((chunk, hidden), lambda i: (i, 0)),
            pl.BlockSpec((chunk, hidden), lambda i: (i, 0)),
        ],
        out_specs=[
            whole(kept, hidden),
            whole(kept, hidden),
            whole(kept, hidden),
            whole(rows, wide),
        ],
        scratch_shapes=[pltpu.VMEM((rows, 2 * hidden), BF)],
    )
    returned = spread(dx)
    grads = [
        dot(left, right, ROWS).astype(BF)
        for left, right in ((rows_x, d_a), (rows_x, d_b), (rows_dy, hid))
    ]
    blocks = call(
        functools.partial(combine_kernel, n_local, top),
        tuple(shape(tok, wide) for _ in range(n_group)),
        (place, returned, pick, column_meta),
        flops=2 * rows * column * half,
        moved=2 * rows * half,
        in_specs=[SMEM] + [VMEM] * 3,
        out_specs=[VMEM] * n_group,
    )
    back = [blocks[0]] + [across(blocks[m], m) for m in range(1, n_group)]
    grad_tokens, grad_gates = call(
        finish_kernel,
        (shape(tok, width), shape(tok, top)),
        (place, *back),
        moved=tok * width * 6,
        in_specs=[SMEM] + [VMEM] * 4,
        out_specs=[VMEM] * 2,
    )
    return (
        grad_tokens,
        grad_gates,
        grads[0][:, None, :],
        grads[1][:, None, :],
        grads[2][:, None, :],
    )


def solution(mesh):
    by_token = P(("group", "local"), None)
    by_expert = P("group", "local", None)
    return jax.shard_map(
        shards,
        mesh=mesh,
        in_specs=(by_token,) * 7 + (by_expert,) * 6,
        out_specs=(by_token,) * 2 + (by_expert,) * 3,
        check_vma=False,
    )
```

```python
import functools

import jax
import jax.numpy as jnp
from jax import lax
from jax.experimental import pallas as pl
from jax.experimental.pallas import tpu as pltpu
from jax.sharding import PartitionSpec as P

CAP = 192
META = 128
CODE, SLOT, GATE = 0, 8, 16
BF = jnp.bfloat16
F32 = jnp.float32
MIB = 1024 * 1024

ROWS = (((0,), (0,)), ((), ()))
LAST = (((1,), (1,)), ((), ()))


def dot(left, right, dims=(((1,), (0,)), ((), ()))):
    return lax.dot_general(left, right, dims, preferred_element_type=F32)


def call(kernel, outs, args, limit, flops=0, moved=0, **kw):
    return pl.pallas_call(
        kernel,
        out_shape=outs,
        compiler_params=pltpu.CompilerParams(vmem_limit_bytes=limit * MIB),
        cost_estimate=pl.CostEstimate(flops=flops, bytes_accessed=moved, transcendentals=0),
        **kw,
    )(*args)


SMEM = pl.BlockSpec(memory_space=pltpu.SMEM)


def whole(*dims):
    return pl.BlockSpec(dims, lambda i: (0,) * len(dims))


def placed(source, offset):
    lane = lax.broadcasted_iota(jnp.int32, (source.shape[0], META), 1)
    row = lax.broadcasted_iota(jnp.int32, (source.shape[0], META), 0)
    return dot(source.astype(BF), jnp.where(lane == row + offset, 1.0, 0.0).astype(BF), ROWS)


def prepare_kernel(
    place_ref, xq_ref, xs_ref, dy_ref, e_ref, r_ref, s_ref, g_ref, same_x, other_x, same_dy, other_dy
):
    half = xq_ref.shape[1] // 2
    blocks = half // 128
    first = lax.rem(place_ref[0], 2) == 0
    code = (1 + e_ref[...] + 64 * r_ref[...]).astype(F32)
    meta = placed(code, CODE) + placed(s_ref[...].astype(F32), SLOT) + placed(g_ref[...], GATE)
    same_x[:, half:] = meta.astype(BF)
    other_x[:, half:] = meta.astype(BF)
    for c in range(blocks):
        low, high = c * 128, half + c * 128
        x_low = (xq_ref[:, low : low + 128].astype(F32) * xs_ref[:, c : c + 1]).astype(BF)
        x_high = (
            xq_ref[:, high : high + 128].astype(F32) * xs_ref[:, blocks + c : blocks + c + 1]
        ).astype(BF)
        same_x[:, low : low + 128] = jnp.where(first, x_low, x_high)
        other_x[:, low : low + 128] = jnp.where(first, x_high, x_low)
    dy_low, dy_high = dy_ref[:, :half], dy_ref[:, half:]
    same_dy[...] = jnp.where(first, dy_low, dy_high)
    other_dy[...] = jnp.where(first, dy_high, dy_low)


def matches(meta, k, base, count):
    lane = lax.broadcasted_iota(jnp.int32, (meta.shape[0], count), 1).astype(F32)
    code = meta[:, CODE + k : CODE + k + 1] - base
    return (code == lane) | (code - 64.0 == lane)


def owner_of_row(rows, count, per, start=0):
    row = lax.broadcasted_iota(jnp.int32, (rows, count), 0) + start
    lane = lax.broadcasted_iota(jnp.int32, (rows, count), 1)
    return lax.div(row, per) == lane


def pack_x_kernel(
    n_local, top, per, place_ref, b0, b1, b2, b3, out_ref, pick_ref, gated_ref, meta_out, tokens, ranks, gates
):
    step = pl.program_id(0)
    half = b0.shape[1] - META
    count = tokens.shape[0]

    @pl.when(step == 0)
    def _():
        block = b0.shape[0]
        for m, b in enumerate((b0, b1, b2, b3)):
            tokens[m * block : (m + 1) * block] = b[...]
        meta_out[...] = tokens[:, half:]
        meta = tokens[:, half:].astype(F32)
        base = (1 + lax.div(place_ref[0], 2) * n_local).astype(F32)
        named = jnp.zeros((count, n_local), F32)
        gate = jnp.zeros((count, n_local), F32)
        for k in range(top):
            hit = matches(meta, k, base, n_local) & (meta[:, SLOT + k : SLOT + k + 1] < CAP)
            named = jnp.where(hit, 1.0, named)
            gate = jnp.where(hit, meta[:, GATE + k : GATE + k + 1], gate)
        row = lax.broadcasted_iota(jnp.int32, (count, count), 0)
        col = lax.broadcasted_iota(jnp.int32, (count, count), 1)
        before = jnp.where(col < row, 1.0, 0.0).astype(BF)
        ranks[...] = jnp.where(named > 0.0, dot(before, named.astype(BF)), -1.0).astype(BF)
        gates[...] = gate.astype(BF)

    rows = out_ref.shape[0]
    spread = jnp.where(owner_of_row(rows, n_local, per, step * rows), 1.0, 0.0).astype(BF)
    rank_rows = dot(spread, ranks[...], LAST)
    gate_rows = dot(spread, gates[...], LAST)
    position = lax.rem(lax.broadcasted_iota(jnp.int32, (rows, count), 0), per).astype(F32)
    hit = rank_rows == position
    pick = jnp.where(hit, 1.0, 0.0).astype(BF)
    pick_ref[...] = pick
    gated_ref[...] = jnp.where(hit, gate_rows, 0.0).astype(BF)
    out_ref[...] = dot(pick, tokens[...]).astype(BF)


def pack_dy_kernel(gated_ref, b0, b1, b2, b3, out_ref):
    tokens = jnp.concatenate([b[...] for b in (b0, b1, b2, b3)], axis=0)
    out_ref[...] = dot(gated_ref[...], tokens).astype(BF)


def dequant(quant_ref, scales_ref, out_ref, first_row, first_col, at_col=0):
    rows, cols = quant_ref.shape
    for c in range(cols // 128):
        for r in range(rows // 128):
            scale = scales_ref[first_col + c, first_row + r]
            factor = jnp.full((1, 16, 128), scale, F32).astype(BF)
            block = quant_ref[r * 128 : (r + 1) * 128, c * 128 : (c + 1) * 128]
            out_ref[r * 128 : (r + 1) * 128, at_col + c * 128 : at_col + (c + 1) * 128] = (
                block.reshape(8, 16, 128) * factor
            ).reshape(128, 128)


def forward_kernel(
    n_local, top, place_ref, sg_ref, su_ref, x_ref, wg_ref, wu_ref,
    kept_ref, a_ref, b_ref, send_ref, slot_ref, wg, wu,
):
    step = pl.program_id(0)
    half = kept_ref.shape[1]
    blocks = wg_ref.shape[1] // 128

    @pl.when(step == 0)
    def _():
        lane = lax.broadcasted_iota(jnp.int32, (2 * top, META), 1)
        row = lax.broadcasted_iota(jnp.int32, (2 * top, META), 0)
        turn = jnp.where(lane == row, 1.0, 0.0).astype(BF)
        meta = dot(turn, x_ref[:, half:], LAST)
        own = (1 + lax.div(place_ref[0], 2) * n_local + place_ref[1]).astype(F32)
        target = jnp.full((1, meta.shape[1]), -1.0, F32)
        for k in range(top):
            code = meta[CODE + k : CODE + k + 1]
            slot = meta[SLOT + k : SLOT + k + 1]
            target = jnp.where(code == own, slot, target)
            target = jnp.where(code == own + 64.0, slot + CAP, target)
        row = lax.broadcasted_iota(jnp.int32, slot_ref.shape, 0).astype(F32)
        slot_ref[...] = jnp.where(row == target, 1.0, 0.0).astype(BF)
        kept_ref[...] = dot(slot_ref[...], x_ref[:, :half]).astype(BF)

    dequant(wg_ref, sg_ref, wg, 0, step * blocks)
    dequant(wu_ref, su_ref, wu, 0, step * blocks)
    part_a = dot(kept_ref[...], wg[...])
    a_ref[...] = part_a
    send_ref[0] = part_a.astype(BF)
    part_b = dot(kept_ref[...], wu[...])
    b_ref[...] = part_b
    send_ref[1] = part_b.astype(BF)


def down_kernel(sv_ref, slot_ref, dy_ref, v_ref, kept_ref, part_ref, send_ref, v):
    step = pl.program_id(0)

    @pl.when(step == 0)
    def _():
        kept_ref[...] = dot(slot_ref[...], dy_ref[...]).astype(BF)

    dequant(v_ref, sv_ref, v, 0, step * (v_ref.shape[1] // 128))
    part = dot(kept_ref[...], v[...])
    part_ref[...] = part
    send_ref[...] = part.astype(BF)


def backward_kernel(
    sg_ref, su_ref, a_ref, b_ref, ab_in, dh_ref, dh_in, slot_ref, wg_ref, wu_ref,
    da_out, db_out, hid_out, dx_ref, wide, both, wcat,
):
    step = pl.program_id(0)
    hidden = wg_ref.shape[1]
    chunk = wg_ref.shape[0]
    width = dx_ref.shape[1] - META
    block = 64

    @pl.when(step == 0)
    def _():
        for r in range(0, a_ref.shape[0], block):
            at = slice(r, r + block)
            d_hidden = dh_ref[at] + dh_in[at].astype(F32)
            act_a = a_ref[at] + ab_in[0, at].astype(F32)
            act_b = b_ref[at] + ab_in[1, at].astype(F32)
            sigma = jax.nn.sigmoid(act_a)
            silu_a = act_a * sigma
            hid = (silu_a * act_b).astype(BF)
            hid_out[at] = hid
            d_a = d_hidden * act_b * sigma * (1.0 + act_a * (1.0 - sigma))
            da_out[at] = d_a.astype(BF)
            db_out[at] = (d_hidden * silu_a).astype(BF)
            grad = jnp.sum(hid.astype(F32) * d_hidden, axis=1, keepdims=True)
            high = grad.astype(BF).astype(F32)
            lane = lax.broadcasted_iota(jnp.int32, (block, META), 1)
            pair = jnp.where(lane == 0, high, jnp.where(lane == 1, grad - high, 0.0))
            both[at] = pair.astype(BF)
        wide[:, :hidden] = dot(slot_ref[...], da_out[...], ROWS).astype(BF)
        wide[:, hidden:] = dot(slot_ref[...], db_out[...], ROWS).astype(BF)
        dx_ref[:, width:] = dot(slot_ref[...], both[...], ROWS).astype(BF)

    rows = chunk // 128
    dequant(wg_ref, sg_ref, wcat, step * rows, 0)
    dequant(wu_ref, su_ref, wcat, step * rows, 0, hidden)
    dx = dot(wide[...], wcat[...], LAST)
    dx_ref[:, pl.ds(pl.multiple_of(step * chunk, chunk), chunk)] = dx.astype(BF)


def combine_kernel(n_local, top, place_ref, ret_ref, pick_ref, meta_ref, *outs):
    width = ret_ref.shape[1] - META
    pick = pick_ref[...]
    meta = meta_ref[...].astype(F32)
    total = dot(pick, ret_ref[:, :width], ROWS).astype(BF)
    rows = ret_ref.shape[0]
    owner = owner_of_row(rows, n_local, rows // n_local)
    grads = ret_ref[:, width:].astype(F32)
    high = jnp.where(owner, grads[:, 0:1], 0.0).astype(BF)
    low = jnp.where(owner, grads[:, 1:2], 0.0).astype(BF)
    by_expert = dot(pick, high, ROWS) + dot(pick, low, ROWS)
    base = (1 + lax.div(place_ref[0], 2) * n_local).astype(F32)
    lane = lax.broadcasted_iota(jnp.int32, meta.shape, 1)
    tail = jnp.zeros(meta.shape, F32)
    for k in range(top):
        hit = matches(meta, k, base, n_local) & (meta[:, SLOT + k : SLOT + k + 1] < CAP)
        value = jnp.sum(jnp.where(hit, by_expert, 0.0), axis=1, keepdims=True)
        tail = jnp.where(lane == k, value / meta[:, GATE + k : GATE + k + 1], tail)
    tail = tail.astype(BF)
    block = outs[0].shape[0]
    for m, out in enumerate(outs):
        out[:, :width] = total[m * block : (m + 1) * block]
        out[:, width:] = tail[m * block : (m + 1) * block]


def finish_kernel(place_ref, b0, b1, b2, b3, tokens_ref, gates_ref):
    half = tokens_ref.shape[1] // 2
    first = lax.rem(place_ref[0], 2) == 0
    own = b0[...].astype(F32) + b2[...].astype(F32)
    other = b1[:, :half].astype(F32) + b3[:, :half].astype(F32)
    mine = own[:, :half]
    tokens_ref[:, :half] = jnp.where(first, mine, other).astype(BF)
    tokens_ref[:, half:] = jnp.where(first, other, mine).astype(BF)
    lane = lax.broadcasted_iota(jnp.int32, (gates_ref.shape[0], META), 1)
    row = lax.broadcasted_iota(jnp.int32, (gates_ref.shape[0], META), 0)
    turn = jnp.where(lane == row, 1.0, 0.0).astype(BF)
    gates_ref[...] = dot(turn, own[:, half:].astype(BF), LAST).astype(BF)


def shape(*dims, dtype=BF):
    return jax.ShapeDtypeStruct(dims, dtype)


def shards(
    x_q,
    x_scale,
    cotangent,
    gates,
    experts,
    replicas,
    slots,
    w_gate_q,
    w_up_q,
    w_down_q,
    gate_scales,
    up_scales,
    down_scales,
):
    n_group = lax.axis_size("group")
    n_local = lax.axis_size("local")
    tok, width = x_q.shape
    top = experts.shape[1]
    half = width // 2
    hidden = w_gate_q.shape[2]
    column = n_group * tok
    rows = n_local * n_group * 4
    kept = 2 * CAP
    wide = half + META
    place = jnp.stack([lax.axis_index("group"), lax.axis_index("local")]).astype(jnp.int32)

    def across(block, apart):
        return lax.ppermute(block, "group", [(i, i ^ apart) for i in range(n_group)])

    def spread(block):
        return lax.all_to_all(block, "local", split_axis=0, concat_axis=0, tiled=True)

    same_x, other_x, same_dy, other_dy = call(
        prepare_kernel,
        (shape(tok, wide), shape(tok, wide), shape(tok, half), shape(tok, half)),
        (place, x_q, x_scale, cotangent, experts.T, replicas.T, slots.T, gates.T),
        limit=63,
        moved=tok * width * 8,
        grid=(1,),
        in_specs=[SMEM, whole(tok, width), whole(*x_scale.shape), whole(tok, width)]
        + [whole(top, tok)] * 4,
        out_specs=[whole(tok, wide)] * 2 + [whole(tok, half)] * 2,
    )
    near_x = [same_x, across(other_x, 1), across(same_x, 2), across(other_x, 3)]
    near_dy = [same_dy, across(other_dy, 1), across(same_dy, 2), across(other_dy, 3)]
    part = rows // 4
    by_row = lambda *dims: pl.BlockSpec(dims, lambda i: (i, 0))
    packed_x, pick, gated, column_meta = call(
        functools.partial(pack_x_kernel, n_local, top, rows // n_local),
        (shape(rows, wide), shape(rows, column), shape(rows, column), shape(column, META)),
        (place, *near_x),
        flops=2 * rows * column * wide,
        limit=24,
        moved=2 * rows * wide,
        grid=(4,),
        in_specs=[SMEM] + [whole(tok, wide)] * 4,
        out_specs=[by_row(part, wide), by_row(part, column), by_row(part, column), whole(column, META)],
        scratch_shapes=[
            pltpu.VMEM((column, wide), BF),
            pltpu.VMEM((column, n_local), BF),
            pltpu.VMEM((column, n_local), BF),
        ],
    )
    packed_dy = call(
        pack_dy_kernel,
        shape(rows, half),
        (gated, *near_dy),
        flops=2 * rows * column * half,
        limit=24,
        moved=2 * rows * half,
        grid=(4,),
        in_specs=[by_row(part, column)] + [whole(tok, half)] * 4,
        out_specs=by_row(part, half),
    )
    got_x = spread(packed_x)
    got_x, packed_dy = lax.optimization_barrier((got_x, packed_dy))
    got_dy = spread(packed_dy)

    weights = [w[:, 0, :] for w in (w_gate_q, w_up_q, w_down_q)]
    scales = [s[:, 0, :].T for s in (gate_scales, up_scales, down_scales)]
    cols = 256
    steps = hidden // cols
    by_col = lambda *dims: pl.BlockSpec(dims, lambda i: (0, i))
    rows_x, part_a, part_b, send_ab, slot_of = call(
        functools.partial(forward_kernel, n_local, top),
        (
            shape(kept, half),
            shape(kept, hidden, dtype=F32),
            shape(kept, hidden, dtype=F32),
            shape(2, kept, hidden),
            shape(kept, rows),
        ),
        (place, scales[0], scales[1], got_x, weights[0], weights[1]),
        flops=4 * kept * half * hidden,
        limit=63,
        moved=4 * half * hidden + 4 * rows * half,
        grid=(steps,),
        in_specs=[SMEM, SMEM, SMEM, whole(rows, wide), by_col(half, cols), by_col(half, cols)],
        out_specs=[
            whole(kept, half),
            by_col(kept, cols),
            by_col(kept, cols),
            pl.BlockSpec((2, kept, cols), lambda i: (0, 0, i)),
            whole(kept, rows),
        ],
        scratch_shapes=[pltpu.VMEM((half, cols), BF)] * 2,
    )
    their_ab = across(send_ab, 1)
    rows_dy, part_dh, send_dh = call(
        down_kernel,
        (shape(kept, half), shape(kept, hidden, dtype=F32), shape(kept, hidden)),
        (scales[2], slot_of, got_dy, weights[2]),
        flops=2 * kept * half * hidden,
        limit=63,
        moved=2 * half * hidden + 4 * rows * half,
        grid=(steps,),
        in_specs=[SMEM, whole(kept, rows), whole(rows, half), by_col(half, cols)],
        out_specs=[whole(kept, half), by_col(kept, cols), by_col(kept, cols)],
        scratch_shapes=[pltpu.VMEM((half, cols), BF)],
    )
    their_dh = across(send_dh, 1)
    chunk = 512
    d_a, d_b, hid, dx = call(
        backward_kernel,
        (shape(kept, hidden), shape(kept, hidden), shape(kept, hidden), shape(rows, wide)),
        (
            scales[0], scales[1], part_a, part_b, their_ab, part_dh, their_dh, slot_of,
            weights[0], weights[1],
        ),
        flops=4 * rows * half * hidden,
        limit=63,
        moved=4 * half * hidden + 2 * rows * half,
        grid=(half // chunk,),
        in_specs=[SMEM, SMEM]
        + [whole(kept, hidden), whole(kept, hidden), whole(2, kept, hidden)]
        + [whole(kept, hidden), whole(kept, hidden), whole(kept, rows)]
        + [by_row(chunk, hidden)] * 2,
        out_specs=[whole(kept, hidden)] * 3 + [whole(rows, wide)],
        scratch_shapes=[
            pltpu.VMEM((rows, 2 * hidden), BF),
            pltpu.VMEM((kept, META), BF),
            pltpu.VMEM((chunk, 2 * hidden), BF),
        ],
    )
    returned = spread(dx)
    grads = [
        dot(left, right, ROWS).astype(BF)
        for left, right in ((rows_x, d_a), (rows_x, d_b), (rows_dy, hid))
    ]
    blocks = call(
        functools.partial(combine_kernel, n_local, top),
        tuple(shape(tok, wide) for _ in range(n_group)),
        (place, returned, pick, column_meta),
        flops=2 * rows * column * half,
        limit=24,
        moved=2 * rows * half,
        grid=(1,),
        in_specs=[SMEM, whole(rows, wide), whole(rows, column), whole(column, META)],
        out_specs=[whole(tok, wide)] * n_group,
    )
    back = [blocks[0]] + [across(blocks[m], m) for m in range(1, n_group)]
    grad_tokens, grad_gates = call(
        finish_kernel,
        (shape(tok, width), shape(top, tok)),
        (place, *back),
        limit=24,
        moved=tok * width * 6,
        grid=(1,),
        in_specs=[SMEM] + [whole(tok, wide)] * 4,
        out_specs=[whole(tok, width), whole(top, tok)],
    )
    return (
        grad_tokens,
        grad_gates.T,
        grads[0][:, None, :],
        grads[1][:, None, :],
        grads[2][:, None, :],
    )


def solution(mesh):
    by_token = P(("group", "local"), None)
    by_expert = P("group", "local", None)
    return jax.shard_map(
        shards,
        mesh=mesh,
        in_specs=(by_token,) * 7 + (by_expert,) * 6,
        out_specs=(by_token,) * 2 + (by_expert,) * 3,
        check_vma=False,
    )
```

```python
import functools

import jax
import jax.numpy as jnp
from jax import lax
from jax.experimental import pallas as pl
from jax.experimental.pallas import tpu as pltpu
from jax.sharding import PartitionSpec as P

CAP = 192
META = 128
CODE, SLOT, GATE = 0, 8, 16
BF = jnp.bfloat16
F32 = jnp.float32
MIB = 1024 * 1024
LIMIT = 24
LIMIT_FORWARD = 50
LIMIT_DOWN = 50
LIMIT_BACKWARD = 50

ROWS = (((0,), (0,)), ((), ()))
LAST = (((1,), (1,)), ((), ()))


def dot(left, right, dims=(((1,), (0,)), ((), ()))):
    return lax.dot_general(left, right, dims, preferred_element_type=F32)


def call(kernel, outs, args, limit, flops=0, moved=0, **kw):
    return pl.pallas_call(
        kernel,
        out_shape=outs,
        compiler_params=pltpu.CompilerParams(vmem_limit_bytes=limit * MIB),
        cost_estimate=pl.CostEstimate(flops=flops, bytes_accessed=moved, transcendentals=0),
        **kw,
    )(*args)


SMEM = pl.BlockSpec(memory_space=pltpu.SMEM)
VMEM = pl.BlockSpec(memory_space=pltpu.VMEM)
HBM = pl.BlockSpec(memory_space=pltpu.HBM)
SEMS = pltpu.SemaphoreType.DMA


def whole(*dims):
    return pl.BlockSpec(dims, lambda i: (0,) * len(dims))


def placed(source, offset):
    lane = lax.broadcasted_iota(jnp.int32, (source.shape[0], META), 1)
    row = lax.broadcasted_iota(jnp.int32, (source.shape[0], META), 0)
    return dot(source.astype(BF), jnp.where(lane == row + offset, 1.0, 0.0).astype(BF), ROWS)


def prepare_kernel(
    xq_ref, xs_ref, dy_ref, e_ref, r_ref, s_ref, g_ref, same_x, other_x, same_dy, other_dy
):
    half = xq_ref.shape[1] // 2
    blocks = half // 128
    first = lax.rem(lax.axis_index("group"), 2) == 0
    code = (1 + e_ref[...] + 64 * r_ref[...]).astype(F32)
    meta = placed(code, CODE) + placed(s_ref[...].astype(F32), SLOT) + placed(g_ref[...], GATE)
    same_x[:, half:] = meta.astype(BF)
    other_x[:, half:] = meta.astype(BF)
    for c in range(blocks):
        low, high = c * 128, half + c * 128
        x_low = (xq_ref[:, low : low + 128].astype(F32) * xs_ref[:, c : c + 1]).astype(BF)
        x_high = (
            xq_ref[:, high : high + 128].astype(F32) * xs_ref[:, blocks + c : blocks + c + 1]
        ).astype(BF)
        same_x[:, low : low + 128] = jnp.where(first, x_low, x_high)
        other_x[:, low : low + 128] = jnp.where(first, x_high, x_low)
    dy_low, dy_high = dy_ref[:, :half], dy_ref[:, half:]
    same_dy[...] = jnp.where(first, dy_low, dy_high)
    other_dy[...] = jnp.where(first, dy_high, dy_low)


def matches(meta, k, base, count):
    lane = lax.broadcasted_iota(jnp.int32, (meta.shape[0], count), 1).astype(F32)
    code = meta[:, CODE + k : CODE + k + 1] - base
    return (code == lane) | (code - 64.0 == lane)


def owner_of_row(rows, count, per, start=0):
    row = lax.broadcasted_iota(jnp.int32, (rows, count), 0) + start
    lane = lax.broadcasted_iota(jnp.int32, (rows, count), 1)
    return lax.div(row, per) == lane


def pack_x_kernel(
    n_local, top, per, b0, b1, b2, b3, out_hbm, pick_ref, gated_ref, meta_out, tokens, out, sems
):
    half = b0.shape[1] - META
    count = tokens.shape[0]
    block = b0.shape[0]
    for m, b in enumerate((b0, b1, b2, b3)):
        tokens[m * block : (m + 1) * block] = b[...]
    meta_out[...] = tokens[:, half:]
    lane = lax.broadcasted_iota(jnp.int32, (4 * top, META), 1)
    row = lax.broadcasted_iota(jnp.int32, (4 * top, META), 0)
    turn = jnp.where(lane == row, 1.0, 0.0).astype(BF)
    meta = dot(turn, tokens[:, half:], LAST)
    base = (1 + lax.div(lax.axis_index("group"), 2) * n_local).astype(F32)
    expert = lax.broadcasted_iota(jnp.int32, (n_local, count), 0).astype(F32) + base
    named = jnp.zeros((n_local, count), F32)
    gate = jnp.zeros((n_local, count), F32)
    for k in range(top):
        code = meta[CODE + k : CODE + k + 1]
        kept = meta[SLOT + k : SLOT + k + 1] < CAP
        hit = ((code == expert) | (code - 64.0 == expert)) & kept
        named = jnp.where(hit, 1.0, named)
        gate = jnp.where(hit, meta[GATE + k : GATE + k + 1], gate)
    row = lax.broadcasted_iota(jnp.int32, (count, count), 0)
    col = lax.broadcasted_iota(jnp.int32, (count, count), 1)
    before = jnp.where(row < col, 1.0, 0.0).astype(BF)
    rank = jnp.where(named > 0.0, dot(named.astype(BF), before), -1.0)
    position = lax.broadcasted_iota(jnp.int32, (per, count), 0).astype(F32)
    part = out.shape[0] // sems.shape[0]
    copies = []
    for j in range(n_local):
        at = slice(j * per, (j + 1) * per)
        hit = rank[j : j + 1] == position
        pick_ref[at] = jnp.where(hit, 1.0, 0.0).astype(BF)
        gated_ref[at] = jnp.where(hit, gate[j : j + 1], 0.0).astype(BF)
        if (j + 1) * per % part == 0:
            at = slice((j + 1) * per - part, (j + 1) * per)
            out[at] = dot(pick_ref[at], tokens[...]).astype(BF)
            copies.append(
                pltpu.make_async_copy(out.at[at], out_hbm.at[at], sems.at[len(copies)])
            )
            copies[-1].start()
    for copy in copies:
        copy.wait()


def pack_dy_kernel(gated_ref, b0, b1, b2, b3, out_hbm, out, sems):
    tokens = jnp.concatenate([b[...] for b in (b0, b1, b2, b3)], axis=0)
    part = out.shape[0] // sems.shape[0]
    copies = []
    for i in range(sems.shape[0]):
        at = slice(i * part, (i + 1) * part)
        out[at] = dot(gated_ref[at], tokens).astype(BF)
        copies.append(pltpu.make_async_copy(out.at[at], out_hbm.at[at], sems.at[i]))
        copies[-1].start()
    for copy in copies:
        copy.wait()


def dequant(quant_ref, scales_ref, out_ref, row, col, rows, cols, at_col=0):
    for c in range(cols // 128):
        for r in range(rows // 128):
            top, left = row + r * 128, col + c * 128
            factor = jnp.full((1, 16, 128), scales_ref[left // 128, top // 128], F32).astype(BF)
            block = quant_ref[top : top + 128, left : left + 128].reshape(8, 16, 128) * factor
            out_ref[r * 128 : (r + 1) * 128, at_col + c * 128 : at_col + (c + 1) * 128] = (
                block.reshape(128, 128)
            )


def fetch(source, target, sems, pieces):
    copies = [
        pltpu.make_async_copy(source.at[piece], target.at[piece], sems.at[i])
        for i, piece in enumerate(pieces)
    ]
    for copy in copies:
        copy.start()
    return copies


def columns(count, size):
    return [(slice(None), slice(c, c + size)) for c in range(0, count, size)]


def forward_kernel(
    n_local, top, cols, sg_ref, su_ref, x_ref, wg_hbm, wu_hbm,
    kept_hbm, send_ref, slot_ref, kept, wg_raw, wu_raw, wg, wu, sems_g, sems_u, sem_k,
):
    half, hidden = wg_raw.shape
    ready_g = fetch(wg_hbm, wg_raw, sems_g, columns(hidden, cols))
    ready_u = fetch(wu_hbm, wu_raw, sems_u, columns(hidden, cols))
    lane = lax.broadcasted_iota(jnp.int32, (2 * top, META), 1)
    row = lax.broadcasted_iota(jnp.int32, (2 * top, META), 0)
    turn = jnp.where(lane == row, 1.0, 0.0).astype(BF)
    meta = dot(turn, x_ref[:, half:], LAST)
    own = (
        1 + lax.div(lax.axis_index("group"), 2) * n_local + lax.axis_index("local")
    ).astype(F32)
    target = jnp.full((1, meta.shape[1]), -1.0, F32)
    for k in range(top):
        code = meta[CODE + k : CODE + k + 1]
        slot = meta[SLOT + k : SLOT + k + 1]
        target = jnp.where(code == own, slot, target)
        target = jnp.where(code == own + 64.0, slot + CAP, target)
    row = lax.broadcasted_iota(jnp.int32, slot_ref.shape, 0).astype(F32)
    slot_ref[...] = jnp.where(row == target, 1.0, 0.0).astype(BF)
    for c in range(0, half, 512):
        kept[:, c : c + 512] = dot(slot_ref[...], x_ref[:, c : c + 512]).astype(BF)
    save = pltpu.make_async_copy(kept, kept_hbm, sem_k)
    save.start()
    for i, c in enumerate(range(0, hidden, cols)):
        at = slice(c, c + cols)
        ready_g[i].wait()
        dequant(wg_raw, sg_ref, wg, 0, c, half, cols)
        send_ref[0, :, at] = dot(kept[...], wg[...]).astype(BF)
        ready_u[i].wait()
        dequant(wu_raw, su_ref, wu, 0, c, half, cols)
        send_ref[1, :, at] = dot(kept[...], wu[...]).astype(BF)
    save.wait()


def down_kernel(
    cols, sv_ref, slot_ref, dy_ref, v_hbm, kept_hbm, send_ref, kept, v_raw, v, sems_v, sem_k
):
    half, hidden = v_raw.shape
    ready = fetch(v_hbm, v_raw, sems_v, columns(hidden, cols))
    for c in range(0, half, 512):
        kept[:, c : c + 512] = dot(slot_ref[...], dy_ref[:, c : c + 512]).astype(BF)
    save = pltpu.make_async_copy(kept, kept_hbm, sem_k)
    save.start()
    for i, c in enumerate(range(0, hidden, cols)):
        ready[i].wait()
        dequant(v_raw, sv_ref, v, 0, c, half, cols)
        send_ref[:, c : c + cols] = dot(kept[...], v[...]).astype(BF)
    save.wait()


def backward_kernel(
    chunk, sg_ref, su_ref, ab_ref, ab_in, dh_ref, dh_in, slot_ref, wg_hbm, wu_hbm,
    d_hbm, dx_hbm, d_all, wide, both, wg_raw, wu_raw, wcat, dx, sems_g, sems_u, sems_x, sem_d,
):
    half, hidden = wg_raw.shape
    pieces = [slice(c, c + chunk) for c in range(0, half, chunk)]
    ready_g = fetch(wg_hbm, wg_raw, sems_g, pieces)
    ready_u = fetch(wu_hbm, wu_raw, sems_u, pieces)
    block = 64
    for r in range(0, dh_ref.shape[0], block):
        at = slice(r, r + block)
        d_hidden = dh_ref[at].astype(F32) + dh_in[at].astype(F32)
        act_a = ab_ref[0, at].astype(F32) + ab_in[0, at].astype(F32)
        act_b = ab_ref[1, at].astype(F32) + ab_in[1, at].astype(F32)
        sigma = jax.nn.sigmoid(act_a)
        silu_a = act_a * sigma
        hid = (silu_a * act_b).astype(BF)
        d_a = d_hidden * act_b * sigma * (1.0 + act_a * (1.0 - sigma))
        d_all[0, at] = d_a.astype(BF)
        d_all[1, at] = (d_hidden * silu_a).astype(BF)
        d_all[2, at] = hid
        grad = jnp.sum(hid.astype(F32) * d_hidden, axis=1, keepdims=True)
        high = grad.astype(BF).astype(F32)
        lane = lax.broadcasted_iota(jnp.int32, (block, META), 1)
        pair = jnp.where(lane == 0, high, jnp.where(lane == 1, grad - high, 0.0))
        both[at] = pair.astype(BF)
    save = pltpu.make_async_copy(d_all, d_hbm, sem_d)
    save.start()
    wide[:, :hidden] = dot(slot_ref[...], d_all[0], ROWS).astype(BF)
    wide[:, hidden:] = dot(slot_ref[...], d_all[1], ROWS).astype(BF)
    dx[:, half:] = dot(slot_ref[...], both[...], ROWS).astype(BF)
    copies = []
    for i, c in enumerate(range(0, half, chunk)):
        ready_g[i].wait()
        ready_u[i].wait()
        dequant(wg_raw, sg_ref, wcat, c, 0, chunk, hidden, 0)
        dequant(wu_raw, su_ref, wcat, c, 0, chunk, hidden, hidden)
        dx[:, c : c + chunk] = dot(wide[...], wcat[...], LAST).astype(BF)
        stop = c + chunk if c + chunk < half else half + META
        copies.append(
            pltpu.make_async_copy(dx.at[:, c:stop], dx_hbm.at[:, c:stop], sems_x.at[i])
        )
        copies[-1].start()
    for copy in copies:
        copy.wait()
    save.wait()


def combine_kernel(n_local, top, ret_ref, pick_ref, meta_ref, *outs):
    width = ret_ref.shape[1] - META
    pick = pick_ref[...]
    meta = meta_ref[...].astype(F32)
    total = dot(pick, ret_ref[:, :width], ROWS).astype(BF)
    rows = ret_ref.shape[0]
    owner = owner_of_row(rows, n_local, rows // n_local)
    grads = ret_ref[:, width:].astype(F32)
    high = jnp.where(owner, grads[:, 0:1], 0.0).astype(BF)
    low = jnp.where(owner, grads[:, 1:2], 0.0).astype(BF)
    by_expert = dot(pick, high, ROWS) + dot(pick, low, ROWS)
    base = (1 + lax.div(lax.axis_index("group"), 2) * n_local).astype(F32)
    lane = lax.broadcasted_iota(jnp.int32, meta.shape, 1)
    tail = jnp.zeros(meta.shape, F32)
    for k in range(top):
        hit = matches(meta, k, base, n_local) & (meta[:, SLOT + k : SLOT + k + 1] < CAP)
        value = jnp.sum(jnp.where(hit, by_expert, 0.0), axis=1, keepdims=True)
        tail = jnp.where(lane == k, value / meta[:, GATE + k : GATE + k + 1], tail)
    tail = tail.astype(BF)
    block = outs[0].shape[0]
    for m, out in enumerate(outs):
        out[:, :width] = total[m * block : (m + 1) * block]
        out[:, width:] = tail[m * block : (m + 1) * block]


def finish_kernel(b0, b1, b2, b3, tokens_ref, gates_ref):
    half = tokens_ref.shape[1] // 2
    first = lax.rem(lax.axis_index("group"), 2) == 0
    own = b0[...].astype(F32) + b2[...].astype(F32)
    other = b1[:, :half].astype(F32) + b3[:, :half].astype(F32)
    mine = own[:, :half]
    tokens_ref[:, :half] = jnp.where(first, mine, other).astype(BF)
    tokens_ref[:, half:] = jnp.where(first, other, mine).astype(BF)
    lane = lax.broadcasted_iota(jnp.int32, (gates_ref.shape[0], META), 1)
    row = lax.broadcasted_iota(jnp.int32, (gates_ref.shape[0], META), 0)
    turn = jnp.where(lane == row, 1.0, 0.0).astype(BF)
    gates_ref[...] = dot(turn, own[:, half:].astype(BF), LAST).astype(BF)


def shape(*dims, dtype=BF):
    return jax.ShapeDtypeStruct(dims, dtype)


def shards(
    x_q,
    x_scale,
    cotangent,
    gates,
    experts,
    replicas,
    slots,
    w_gate_q,
    w_up_q,
    w_down_q,
    gate_scales,
    up_scales,
    down_scales,
):
    n_group = lax.axis_size("group")
    n_local = lax.axis_size("local")
    tok, width = x_q.shape
    top = experts.shape[1]
    half = width // 2
    hidden = w_gate_q.shape[2]
    column = n_group * tok
    rows = n_local * n_group * 4
    kept = 2 * CAP
    wide = half + META

    def across(block, apart):
        return lax.ppermute(block, "group", [(i, i ^ apart) for i in range(n_group)])

    def spread(block):
        return lax.all_to_all(block, "local", split_axis=0, concat_axis=0, tiled=True)

    same_x, other_x, same_dy, other_dy = call(
        prepare_kernel,
        (shape(tok, wide), shape(tok, wide), shape(tok, half), shape(tok, half)),
        (x_q, x_scale, cotangent, experts.T, replicas.T, slots.T, gates.T),
        limit=63,
        moved=tok * width * 8,
        grid=(1,),
        in_specs=[whole(tok, width), whole(*x_scale.shape), whole(tok, width)]
        + [whole(top, tok)] * 4,
        out_specs=[whole(tok, wide)] * 2 + [whole(tok, half)] * 2,
    )
    near_x = [same_x, across(other_x, 1), across(same_x, 2), across(other_x, 3)]
    near_dy = [same_dy, across(other_dy, 1), across(same_dy, 2), across(other_dy, 3)]
    packed_x, pick, gated, column_meta = call(
        functools.partial(pack_x_kernel, n_local, top, rows // n_local),
        (shape(rows, wide), shape(rows, column), shape(rows, column), shape(column, META)),
        tuple(near_x),
        limit=LIMIT,
        flops=2 * rows * column * wide,
        moved=2 * rows * wide,
        in_specs=[VMEM] * 4,
        out_specs=[HBM] + [VMEM] * 3,
        scratch_shapes=[pltpu.VMEM((column, wide), BF), pltpu.VMEM((rows, wide), BF), SEMS((4,))],
    )
    packed_dy = call(
        pack_dy_kernel,
        shape(rows, half),
        (gated, *near_dy),
        limit=LIMIT,
        flops=2 * rows * column * half,
        moved=2 * rows * half,
        in_specs=[VMEM] * 5,
        out_specs=HBM,
        scratch_shapes=[pltpu.VMEM((rows, half), BF), SEMS((4,))],
    )
    got_x = spread(packed_x)
    got_x, packed_dy = lax.optimization_barrier((got_x, packed_dy))
    got_dy = spread(packed_dy)

    weights = [w[:, 0, :] for w in (w_gate_q, w_up_q, w_down_q)]
    scales = [s[:, 0, :].T for s in (gate_scales, up_scales, down_scales)]
    cols = 256
    steps = hidden // cols
    raw = pltpu.VMEM((half, hidden), BF)
    rows_x, send_ab, slot_of = call(
        functools.partial(forward_kernel, n_local, top, cols),
        (shape(kept, half), shape(2, kept, hidden), shape(kept, rows)),
        (scales[0], scales[1], got_x, weights[0], weights[1]),
        limit=LIMIT_FORWARD,
        flops=4 * kept * half * hidden,
        moved=4 * half * hidden + 4 * rows * half,
        in_specs=[SMEM, SMEM, VMEM, HBM, HBM],
        out_specs=[HBM, VMEM, VMEM],
        scratch_shapes=[pltpu.VMEM((kept, half), BF), raw, raw]
        + [pltpu.VMEM((half, cols), BF)] * 2
        + [SEMS((steps,)), SEMS((steps,)), SEMS],
    )
    their_ab = across(send_ab, 1)
    rows_dy, send_dh = call(
        functools.partial(down_kernel, cols),
        (shape(kept, half), shape(kept, hidden)),
        (scales[2], slot_of, got_dy, weights[2]),
        limit=LIMIT_DOWN,
        flops=2 * kept * half * hidden,
        moved=2 * half * hidden + 4 * rows * half,
        in_specs=[SMEM, VMEM, VMEM, HBM],
        out_specs=[HBM, VMEM],
        scratch_shapes=[
            pltpu.VMEM((kept, half), BF), raw, pltpu.VMEM((half, cols), BF), SEMS((steps,)), SEMS,
        ],
    )
    their_dh = across(send_dh, 1)
    chunk = 512
    parts = half // chunk
    d_all, dx = call(
        functools.partial(backward_kernel, chunk),
        (shape(3, kept, hidden), shape(rows, wide)),
        (
            scales[0], scales[1], send_ab, their_ab, send_dh, their_dh, slot_of,
            weights[0], weights[1],
        ),
        limit=LIMIT_BACKWARD,
        flops=4 * rows * half * hidden,
        moved=4 * half * hidden + 2 * rows * half,
        in_specs=[SMEM, SMEM] + [VMEM] * 5 + [HBM, HBM],
        out_specs=[HBM, HBM],
        scratch_shapes=[
            pltpu.VMEM((3, kept, hidden), BF),
            pltpu.VMEM((rows, 2 * hidden), BF),
            pltpu.VMEM((kept, META), BF),
            raw,
            raw,
            pltpu.VMEM((chunk, 2 * hidden), BF),
            pltpu.VMEM((rows, wide), BF),
            SEMS((parts,)),
            SEMS((parts,)),
            SEMS((parts,)),
            SEMS,
        ],
    )
    returned = spread(dx)
    grads = [
        dot(left, right, ROWS).astype(BF)
        for left, right in ((rows_x, d_all[0]), (rows_x, d_all[1]), (rows_dy, d_all[2]))
    ]
    blocks = call(
        functools.partial(combine_kernel, n_local, top),
        tuple(shape(tok, wide) for _ in range(n_group)),
        (returned, pick, column_meta),
        flops=2 * rows * column * half,
        limit=24,
        moved=2 * rows * half,
        in_specs=[VMEM] * 3,
        out_specs=[VMEM] * n_group,
    )
    back = [blocks[0]] + [across(blocks[m], m) for m in range(1, n_group)]
    grad_tokens, grad_gates = call(
        finish_kernel,
        (shape(tok, width), shape(top, tok)),
        tuple(back),
        limit=24,
        moved=tok * width * 6,
        grid=(1,),
        in_specs=[whole(tok, wide)] * 4,
        out_specs=[whole(tok, width), whole(top, tok)],
    )
    return (
        grad_tokens,
        grad_gates.T,
        grads[0][:, None, :],
        grads[1][:, None, :],
        grads[2][:, None, :],
    )


def solution(mesh):
    by_token = P(("group", "local"), None)
    by_expert = P("group", "local", None)
    return jax.shard_map(
        shards,
        mesh=mesh,
        in_specs=(by_token,) * 7 + (by_expert,) * 6,
        out_specs=(by_token,) * 2 + (by_expert,) * 3,
        check_vma=False,
    )
```

```python
import functools

import jax
import jax.numpy as jnp
from jax import lax
from jax.experimental import pallas as pl
from jax.experimental.pallas import tpu as pltpu
from jax.sharding import PartitionSpec as P

CAP = 192
META = 128
CODE, SLOT, GATE = 0, 8, 16
BF = jnp.bfloat16
F32 = jnp.float32
MIB = 1024 * 1024
LIMIT = 24
LIMIT_DEQUANT = 16
LIMIT_FORWARD = 50
LIMIT_DOWN = 50
LIMIT_BACKWARD = 50

ROWS = (((0,), (0,)), ((), ()))
LAST = (((1,), (1,)), ((), ()))


def dot(left, right, dims=(((1,), (0,)), ((), ()))):
    return lax.dot_general(left, right, dims, preferred_element_type=F32)


def call(kernel, outs, args, limit, flops=0, moved=0, **kw):
    return pl.pallas_call(
        kernel,
        out_shape=outs,
        compiler_params=pltpu.CompilerParams(vmem_limit_bytes=limit * MIB),
        cost_estimate=pl.CostEstimate(flops=flops, bytes_accessed=moved, transcendentals=0),
        **kw,
    )(*args)


SMEM = pl.BlockSpec(memory_space=pltpu.SMEM)
VMEM = pl.BlockSpec(memory_space=pltpu.VMEM)
HBM = pl.BlockSpec(memory_space=pltpu.HBM)
SEMS = pltpu.SemaphoreType.DMA


def whole(*dims):
    return pl.BlockSpec(dims, lambda i: (0,) * len(dims))


def placed(source, offset):
    lane = lax.broadcasted_iota(jnp.int32, (source.shape[0], META), 1)
    row = lax.broadcasted_iota(jnp.int32, (source.shape[0], META), 0)
    return dot(source.astype(BF), jnp.where(lane == row + offset, 1.0, 0.0).astype(BF), ROWS)


def prepare_kernel(
    xq_ref, xs_ref, dy_ref, e_ref, r_ref, s_ref, g_ref, same_x, other_x, same_dy, other_dy
):
    half = xq_ref.shape[1] // 2
    blocks = half // 128
    first = lax.rem(lax.axis_index("group"), 2) == 0
    code = (1 + e_ref[...] + 64 * r_ref[...]).astype(F32)
    meta = placed(code, CODE) + placed(s_ref[...].astype(F32), SLOT) + placed(g_ref[...], GATE)
    same_x[:, half:] = meta.astype(BF)
    other_x[:, half:] = meta.astype(BF)
    for c in range(blocks):
        low, high = c * 128, half + c * 128
        x_low = (xq_ref[:, low : low + 128].astype(F32) * xs_ref[:, c : c + 1]).astype(BF)
        x_high = (
            xq_ref[:, high : high + 128].astype(F32) * xs_ref[:, blocks + c : blocks + c + 1]
        ).astype(BF)
        same_x[:, low : low + 128] = jnp.where(first, x_low, x_high)
        other_x[:, low : low + 128] = jnp.where(first, x_high, x_low)
    dy_low, dy_high = dy_ref[:, :half], dy_ref[:, half:]
    same_dy[...] = jnp.where(first, dy_low, dy_high)
    other_dy[...] = jnp.where(first, dy_high, dy_low)


def matches(meta, k, base, count):
    lane = lax.broadcasted_iota(jnp.int32, (meta.shape[0], count), 1).astype(F32)
    code = meta[:, CODE + k : CODE + k + 1] - base
    return (code == lane) | (code - 64.0 == lane)


def owner_of_row(rows, count, per, start=0):
    row = lax.broadcasted_iota(jnp.int32, (rows, count), 0) + start
    lane = lax.broadcasted_iota(jnp.int32, (rows, count), 1)
    return lax.div(row, per) == lane


def pack_x_kernel(
    n_local, top, per, b0, b1, b2, b3, out_hbm, pick_ref, gated_ref, meta_out, tokens, out, sems
):
    half = b0.shape[1] - META
    count = tokens.shape[0]
    block = b0.shape[0]
    for m, b in enumerate((b0, b1, b2, b3)):
        tokens[m * block : (m + 1) * block] = b[...]
    meta_out[...] = tokens[:, half:]
    lane = lax.broadcasted_iota(jnp.int32, (4 * top, META), 1)
    row = lax.broadcasted_iota(jnp.int32, (4 * top, META), 0)
    turn = jnp.where(lane == row, 1.0, 0.0).astype(BF)
    meta = dot(turn, tokens[:, half:], LAST)
    base = (1 + lax.div(lax.axis_index("group"), 2) * n_local).astype(F32)
    expert = lax.broadcasted_iota(jnp.int32, (n_local, count), 0).astype(F32) + base
    named = jnp.zeros((n_local, count), F32)
    gate = jnp.zeros((n_local, count), F32)
    for k in range(top):
        code = meta[CODE + k : CODE + k + 1]
        kept = meta[SLOT + k : SLOT + k + 1] < CAP
        hit = ((code == expert) | (code - 64.0 == expert)) & kept
        named = jnp.where(hit, 1.0, named)
        gate = jnp.where(hit, meta[GATE + k : GATE + k + 1], gate)
    row = lax.broadcasted_iota(jnp.int32, (count, count), 0)
    col = lax.broadcasted_iota(jnp.int32, (count, count), 1)
    before = jnp.where(row < col, 1.0, 0.0).astype(BF)
    rank = jnp.where(named > 0.0, dot(named.astype(BF), before), -1.0)
    position = lax.broadcasted_iota(jnp.int32, (per, count), 0).astype(F32)
    for j in range(n_local):
        at = slice(j * per, (j + 1) * per)
        hit = rank[j : j + 1] == position
        pick_ref[at] = jnp.where(hit, 1.0, 0.0).astype(BF)
        gated_ref[at] = jnp.where(hit, gate[j : j + 1], 0.0).astype(BF)
    multiply_out(pick_ref, tokens, out, out_hbm, sems)


def multiply_out(left, right, out, out_hbm, sems):
    parts = sems.shape[0]
    size = out.shape[0] // parts

    def copy(i):
        at = pl.ds(pl.multiple_of(i * size, size), size)
        return pltpu.make_async_copy(out.at[at], out_hbm.at[at], sems.at[i])

    def step(i, carry):
        at = pl.ds(pl.multiple_of(i * size, size), size)
        out[at] = dot(left[at], right[...]).astype(BF)
        copy(i).start()
        return carry

    lax.fori_loop(0, parts, step, 0)
    for i in range(parts):
        copy(i).wait()


def pack_dy_kernel(gated_ref, b0, b1, b2, b3, out_hbm, tokens, out, sems):
    block = b0.shape[0]
    for m, b in enumerate((b0, b1, b2, b3)):
        tokens[m * block : (m + 1) * block] = b[...]
    multiply_out(gated_ref, tokens, out, out_hbm, sems)


def dequant(quant_ref, scales_ref, out_ref, row, col):
    rows, cols = quant_ref.shape
    for c in range(cols // 128):
        for r in range(rows // 128):
            at = (slice(r * 128, (r + 1) * 128), slice(c * 128, (c + 1) * 128))
            factor = jnp.full((1, 16, 128), scales_ref[col + c, row + r], F32).astype(BF)
            out_ref[at] = (quant_ref[at].reshape(8, 16, 128) * factor).reshape(128, 128)


def columns(i, size):
    return (slice(None), pl.ds(pl.multiple_of(i * size, size), size))


def fetch(source, target, sems, i, size):
    at = columns(i, size)
    return pltpu.make_async_copy(source.at[at], target.at[at], sems.at[i])


def compact(slot_ref, rows_ref, kept, size=512):
    def step(i, carry):
        at = columns(i, size)
        kept[at] = dot(slot_ref[...], rows_ref[at]).astype(BF)
        return carry

    lax.fori_loop(0, kept.shape[1] // size, step, 0)


def forward_kernel(
    n_local, top, cols, sg_ref, su_ref, x_ref, wg_hbm, wu_hbm,
    kept_hbm, send_ref, slot_ref, kept, wg_raw, wu_raw, wg, wu, sems_g, sems_u, sem_k,
):
    half, hidden = wg_raw.shape
    steps = hidden // cols
    for i in range(steps):
        fetch(wg_hbm, wg_raw, sems_g, i, cols).start()
        fetch(wu_hbm, wu_raw, sems_u, i, cols).start()
    lane = lax.broadcasted_iota(jnp.int32, (2 * top, META), 1)
    row = lax.broadcasted_iota(jnp.int32, (2 * top, META), 0)
    turn = jnp.where(lane == row, 1.0, 0.0).astype(BF)
    meta = dot(turn, x_ref[:, half:], LAST)
    own = (
        1 + lax.div(lax.axis_index("group"), 2) * n_local + lax.axis_index("local")
    ).astype(F32)
    target = jnp.full((1, meta.shape[1]), -1.0, F32)
    for k in range(top):
        code = meta[CODE + k : CODE + k + 1]
        slot = meta[SLOT + k : SLOT + k + 1]
        target = jnp.where(code == own, slot, target)
        target = jnp.where(code == own + 64.0, slot + CAP, target)
    row = lax.broadcasted_iota(jnp.int32, slot_ref.shape, 0).astype(F32)
    slot_ref[...] = jnp.where(row == target, 1.0, 0.0).astype(BF)
    compact(slot_ref, x_ref, kept)
    save = pltpu.make_async_copy(kept, kept_hbm, sem_k)
    save.start()

    def step(i, carry):
        at = columns(i, cols)
        fetch(wg_hbm, wg_raw, sems_g, i, cols).wait()
        fetch(wu_hbm, wu_raw, sems_u, i, cols).wait()
        dequant(wg_raw.at[at], sg_ref, wg, 0, i * (cols // 128))
        dequant(wu_raw.at[at], su_ref, wu, 0, i * (cols // 128))
        send_ref[(0, *at)] = dot(kept[...], wg[...]).astype(BF)
        send_ref[(1, *at)] = dot(kept[...], wu[...]).astype(BF)
        return carry

    lax.fori_loop(0, steps, step, 0)
    save.wait()


def down_kernel(
    cols, sv_ref, slot_ref, dy_ref, v_hbm, kept_hbm, send_ref, kept, v_raw, v, sems_v, sem_k
):
    half, hidden = v_raw.shape
    steps = hidden // cols
    for i in range(steps):
        fetch(v_hbm, v_raw, sems_v, i, cols).start()
    compact(slot_ref, dy_ref, kept)
    save = pltpu.make_async_copy(kept, kept_hbm, sem_k)
    save.start()

    def step(i, carry):
        at = columns(i, cols)
        fetch(v_hbm, v_raw, sems_v, i, cols).wait()
        dequant(v_raw.at[at], sv_ref, v, 0, i * (cols // 128))
        send_ref[at] = dot(kept[...], v[...]).astype(BF)
        return carry

    lax.fori_loop(0, steps, step, 0)
    save.wait()


def backward_kernel(
    chunk, sg_ref, su_ref, ab_ref, ab_in, dh_ref, dh_in, slot_ref, wg_hbm, wu_hbm,
    d_hbm, dx_hbm, d_all, wide, both, wg_raw, wu_raw, wcat, dx, sems_g, sems_u, sems_x, sem_d, sem_m,
):
    half, hidden = wg_raw.shape
    parts = half // chunk
    block = 64

    def load(source, target, sems, i):
        at = pl.ds(pl.multiple_of(i * chunk, chunk), chunk)
        return pltpu.make_async_copy(source.at[at], target.at[at], sems.at[i])

    for i in range(parts):
        load(wg_hbm, wg_raw, sems_g, i).start()
        load(wu_hbm, wu_raw, sems_u, i).start()

    def activate(i, carry):
        at = pl.ds(pl.multiple_of(i * block, block), block)
        d_hidden = dh_ref[at].astype(F32) + dh_in[at].astype(F32)
        act_a = ab_ref[0, at].astype(F32) + ab_in[0, at].astype(F32)
        act_b = ab_ref[1, at].astype(F32) + ab_in[1, at].astype(F32)
        sigma = jax.nn.sigmoid(act_a)
        silu_a = act_a * sigma
        hid = (silu_a * act_b).astype(BF)
        d_a = d_hidden * act_b * sigma * (1.0 + act_a * (1.0 - sigma))
        d_all[0, at] = d_a.astype(BF)
        d_all[1, at] = (d_hidden * silu_a).astype(BF)
        d_all[2, at] = hid
        grad = jnp.sum(hid.astype(F32) * d_hidden, axis=1, keepdims=True)
        high = grad.astype(BF).astype(F32)
        lane = lax.broadcasted_iota(jnp.int32, (block, META), 1)
        pair = jnp.where(lane == 0, high, jnp.where(lane == 1, grad - high, 0.0))
        both[at] = pair.astype(BF)
        return carry

    lax.fori_loop(0, dh_ref.shape[0] // block, activate, 0)
    save = pltpu.make_async_copy(d_all, d_hbm, sem_d)
    save.start()
    wide[:, :hidden] = dot(slot_ref[...], d_all[0], ROWS).astype(BF)
    wide[:, hidden:] = dot(slot_ref[...], d_all[1], ROWS).astype(BF)
    dx[:, half:] = dot(slot_ref[...], both[...], ROWS).astype(BF)
    tail = pltpu.make_async_copy(dx.at[:, half:], dx_hbm.at[:, half:], sem_m)
    tail.start()

    def step(i, carry):
        at = pl.ds(pl.multiple_of(i * chunk, chunk), chunk)
        load(wg_hbm, wg_raw, sems_g, i).wait()
        load(wu_hbm, wu_raw, sems_u, i).wait()
        dequant(wg_raw.at[at], sg_ref, wcat.at[:, :hidden], i * (chunk // 128), 0)
        dequant(wu_raw.at[at], su_ref, wcat.at[:, hidden:], i * (chunk // 128), 0)
        dx[columns(i, chunk)] = dot(wide[...], wcat[...], LAST).astype(BF)
        fetch(dx, dx_hbm, sems_x, i, chunk).start()
        return carry

    lax.fori_loop(0, parts, step, 0)
    for i in range(parts):
        fetch(dx, dx_hbm, sems_x, i, chunk).wait()
    tail.wait()
    save.wait()


def combine_kernel(n_local, top, ret_ref, pick_ref, meta_ref, *outs):
    width = ret_ref.shape[1] - META
    pick = pick_ref[...]
    meta = meta_ref[...].astype(F32)
    total = dot(pick, ret_ref[:, :width], ROWS).astype(BF)
    rows = ret_ref.shape[0]
    owner = owner_of_row(rows, n_local, rows // n_local)
    grads = ret_ref[:, width:].astype(F32)
    high = jnp.where(owner, grads[:, 0:1], 0.0).astype(BF)
    low = jnp.where(owner, grads[:, 1:2], 0.0).astype(BF)
    by_expert = dot(pick, high, ROWS) + dot(pick, low, ROWS)
    base = (1 + lax.div(lax.axis_index("group"), 2) * n_local).astype(F32)
    lane = lax.broadcasted_iota(jnp.int32, meta.shape, 1)
    tail = jnp.zeros(meta.shape, F32)
    for k in range(top):
        hit = matches(meta, k, base, n_local) & (meta[:, SLOT + k : SLOT + k + 1] < CAP)
        value = jnp.sum(jnp.where(hit, by_expert, 0.0), axis=1, keepdims=True)
        tail = jnp.where(lane == k, value / meta[:, GATE + k : GATE + k + 1], tail)
    tail = tail.astype(BF)
    block = outs[0].shape[0]
    for m, out in enumerate(outs):
        out[:, :width] = total[m * block : (m + 1) * block]
        out[:, width:] = tail[m * block : (m + 1) * block]


def finish_kernel(b0, b1, b2, b3, tokens_ref, gates_ref):
    half = tokens_ref.shape[1] // 2
    first = lax.rem(lax.axis_index("group"), 2) == 0
    own = b0[...].astype(F32) + b2[...].astype(F32)
    other = b1[:, :half].astype(F32) + b3[:, :half].astype(F32)
    mine = own[:, :half]
    tokens_ref[:, :half] = jnp.where(first, mine, other).astype(BF)
    tokens_ref[:, half:] = jnp.where(first, other, mine).astype(BF)
    lane = lax.broadcasted_iota(jnp.int32, (gates_ref.shape[0], META), 1)
    row = lax.broadcasted_iota(jnp.int32, (gates_ref.shape[0], META), 0)
    turn = jnp.where(lane == row, 1.0, 0.0).astype(BF)
    gates_ref[...] = dot(turn, own[:, half:].astype(BF), LAST).astype(BF)


def shape(*dims, dtype=BF):
    return jax.ShapeDtypeStruct(dims, dtype)


def shards(
    x_q,
    x_scale,
    cotangent,
    gates,
    experts,
    replicas,
    slots,
    w_gate_q,
    w_up_q,
    w_down_q,
    gate_scales,
    up_scales,
    down_scales,
):
    n_group = lax.axis_size("group")
    n_local = lax.axis_size("local")
    tok, width = x_q.shape
    top = experts.shape[1]
    half = width // 2
    hidden = w_gate_q.shape[2]
    column = n_group * tok
    rows = n_local * n_group * 4
    kept = 2 * CAP
    wide = half + META

    def across(block, apart):
        return lax.ppermute(block, "group", [(i, i ^ apart) for i in range(n_group)])

    def spread(block):
        return lax.all_to_all(block, "local", split_axis=0, concat_axis=0, tiled=True)

    same_x, other_x, same_dy, other_dy = call(
        prepare_kernel,
        (shape(tok, wide), shape(tok, wide), shape(tok, half), shape(tok, half)),
        (x_q, x_scale, cotangent, experts.T, replicas.T, slots.T, gates.T),
        limit=63,
        moved=tok * width * 8,
        grid=(1,),
        in_specs=[whole(tok, width), whole(*x_scale.shape), whole(tok, width)]
        + [whole(top, tok)] * 4,
        out_specs=[whole(tok, wide)] * 2 + [whole(tok, half)] * 2,
    )
    near_x = [same_x, across(other_x, 1), across(same_x, 2), across(other_x, 3)]
    near_dy = [same_dy, across(other_dy, 1), across(same_dy, 2), across(other_dy, 3)]
    packed_x, pick, gated, column_meta = call(
        functools.partial(pack_x_kernel, n_local, top, rows // n_local),
        (shape(rows, wide), shape(rows, column), shape(rows, column), shape(column, META)),
        tuple(near_x),
        limit=LIMIT,
        flops=2 * rows * column * wide,
        moved=2 * rows * wide,
        in_specs=[VMEM] * 4,
        out_specs=[HBM] + [VMEM] * 3,
        scratch_shapes=[pltpu.VMEM((column, wide), BF), pltpu.VMEM((rows, wide), BF), SEMS((4,))],
    )
    packed_dy = call(
        pack_dy_kernel,
        shape(rows, half),
        (gated, *near_dy),
        limit=LIMIT,
        flops=2 * rows * column * half,
        moved=2 * rows * half,
        in_specs=[VMEM] * 5,
        out_specs=HBM,
        scratch_shapes=[pltpu.VMEM((column, half), BF), pltpu.VMEM((rows, half), BF), SEMS((4,))],
    )
    got_x = spread(packed_x)
    got_x, packed_dy = lax.optimization_barrier((got_x, packed_dy))
    got_dy = spread(packed_dy)

    weights = [w[:, 0, :] for w in (w_gate_q, w_up_q, w_down_q)]
    scales = [s[:, 0, :].T for s in (gate_scales, up_scales, down_scales)]
    cols = 256
    steps = hidden // cols
    raw = pltpu.VMEM((half, hidden), BF)
    rows_x, send_ab, slot_of = call(
        functools.partial(forward_kernel, n_local, top, cols),
        (shape(kept, half), shape(2, kept, hidden), shape(kept, rows)),
        (scales[0], scales[1], got_x, weights[0], weights[1]),
        limit=LIMIT_FORWARD,
        flops=4 * kept * half * hidden,
        moved=4 * half * hidden + 4 * rows * half,
        in_specs=[SMEM, SMEM, VMEM, HBM, HBM],
        out_specs=[HBM, VMEM, VMEM],
        scratch_shapes=[pltpu.VMEM((kept, half), BF), raw, raw]
        + [pltpu.VMEM((half, cols), BF)] * 2
        + [SEMS((steps,)), SEMS((steps,)), SEMS],
    )
    their_ab = across(send_ab, 1)
    rows_dy, send_dh = call(
        functools.partial(down_kernel, cols),
        (shape(kept, half), shape(kept, hidden)),
        (scales[2], slot_of, got_dy, weights[2]),
        limit=LIMIT_DOWN,
        flops=2 * kept * half * hidden,
        moved=2 * half * hidden + 4 * rows * half,
        in_specs=[SMEM, VMEM, VMEM, HBM],
        out_specs=[HBM, VMEM],
        scratch_shapes=[
            pltpu.VMEM((kept, half), BF), raw, pltpu.VMEM((half, cols), BF), SEMS((steps,)), SEMS,
        ],
    )
    their_dh = across(send_dh, 1)
    chunk = 512
    parts = half // chunk
    d_all, dx = call(
        functools.partial(backward_kernel, chunk),
        (shape(3, kept, hidden), shape(rows, wide)),
        (
            scales[0], scales[1], send_ab, their_ab, send_dh, their_dh, slot_of,
            weights[0], weights[1],
        ),
        limit=LIMIT_BACKWARD,
        flops=4 * rows * half * hidden,
        moved=4 * half * hidden + 2 * rows * half,
        in_specs=[SMEM, SMEM] + [VMEM] * 5 + [HBM, HBM],
        out_specs=[HBM, HBM],
        scratch_shapes=[
            pltpu.VMEM((3, kept, hidden), BF),
            pltpu.VMEM((rows, 2 * hidden), BF),
            pltpu.VMEM((kept, META), BF),
            raw,
            raw,
            pltpu.VMEM((chunk, 2 * hidden), BF),
            pltpu.VMEM((rows, wide), BF),
            SEMS((parts,)),
            SEMS((parts,)),
            SEMS((parts,)),
            SEMS,
            SEMS,
        ],
    )
    returned = spread(dx)
    grads = [
        dot(left, right, ROWS).astype(BF)
        for left, right in ((rows_x, d_all[0]), (rows_x, d_all[1]), (rows_dy, d_all[2]))
    ]
    blocks = call(
        functools.partial(combine_kernel, n_local, top),
        tuple(shape(tok, wide) for _ in range(n_group)),
        (returned, pick, column_meta),
        flops=2 * rows * column * half,
        limit=24,
        moved=2 * rows * half,
        in_specs=[VMEM] * 3,
        out_specs=[VMEM] * n_group,
    )
    back = [blocks[0]] + [across(blocks[m], m) for m in range(1, n_group)]
    grad_tokens, grad_gates = call(
        finish_kernel,
        (shape(tok, width), shape(top, tok)),
        tuple(back),
        limit=24,
        moved=tok * width * 6,
        grid=(1,),
        in_specs=[whole(tok, wide)] * 4,
        out_specs=[whole(tok, width), whole(top, tok)],
    )
    return (
        grad_tokens,
        grad_gates.T,
        grads[0][:, None, :],
        grads[1][:, None, :],
        grads[2][:, None, :],
    )


def solution(mesh):
    by_token = P(("group", "local"), None)
    by_expert = P("group", "local", None)
    return jax.shard_map(
        shards,
        mesh=mesh,
        in_specs=(by_token,) * 7 + (by_expert,) * 6,
        out_specs=(by_token,) * 2 + (by_expert,) * 3,
        check_vma=False,
    )
```

```python
import functools

import jax
import jax.numpy as jnp
from jax import lax
from jax.experimental import pallas as pl
from jax.experimental.pallas import tpu as pltpu
from jax.sharding import PartitionSpec as P

CAP = 192
META = 128
CODE, SLOT, GATE = 0, 8, 16
BF = jnp.bfloat16
F32 = jnp.float32
MIB = 1024 * 1024
LIMIT = 24
LIMIT_FACTOR = 50
LIMIT_FORWARD = 50
LIMIT_DOWN = 50
LIMIT_BACKWARD = 51

ROWS = (((0,), (0,)), ((), ()))
LAST = (((1,), (1,)), ((), ()))


def dot(left, right, dims=(((1,), (0,)), ((), ()))):
    return lax.dot_general(left, right, dims, preferred_element_type=F32)


def call(kernel, outs, args, limit, flops=0, moved=0, **kw):
    return pl.pallas_call(
        kernel,
        out_shape=outs,
        compiler_params=pltpu.CompilerParams(vmem_limit_bytes=limit * MIB),
        cost_estimate=pl.CostEstimate(flops=flops, bytes_accessed=moved, transcendentals=0),
        **kw,
    )(*args)


SMEM = pl.BlockSpec(memory_space=pltpu.SMEM)
VMEM = pl.BlockSpec(memory_space=pltpu.VMEM)
HBM = pl.BlockSpec(memory_space=pltpu.HBM)
SEMS = pltpu.SemaphoreType.DMA


def whole(*dims):
    return pl.BlockSpec(dims, lambda i: (0,) * len(dims))


def placed(source, offset):
    lane = lax.broadcasted_iota(jnp.int32, (source.shape[0], META), 1)
    row = lax.broadcasted_iota(jnp.int32, (source.shape[0], META), 0)
    return dot(source.astype(BF), jnp.where(lane == row + offset, 1.0, 0.0).astype(BF), ROWS)


def prepare_kernel(
    xq_ref, xs_ref, dy_ref, e_ref, r_ref, s_ref, g_ref, same_x, other_x, same_dy, other_dy
):
    half = xq_ref.shape[1] // 2
    blocks = half // 128
    first = lax.rem(lax.axis_index("group"), 2) == 0
    code = (1 + e_ref[...] + 64 * r_ref[...]).astype(F32)
    meta = placed(code, CODE) + placed(s_ref[...].astype(F32), SLOT) + placed(g_ref[...], GATE)
    same_x[:, half:] = meta.astype(BF)
    other_x[:, half:] = meta.astype(BF)
    for c in range(blocks):
        low, high = c * 128, half + c * 128
        x_low = (xq_ref[:, low : low + 128].astype(F32) * xs_ref[:, c : c + 1]).astype(BF)
        x_high = (
            xq_ref[:, high : high + 128].astype(F32) * xs_ref[:, blocks + c : blocks + c + 1]
        ).astype(BF)
        same_x[:, low : low + 128] = jnp.where(first, x_low, x_high)
        other_x[:, low : low + 128] = jnp.where(first, x_high, x_low)
    dy_low, dy_high = dy_ref[:, :half], dy_ref[:, half:]
    same_dy[...] = jnp.where(first, dy_low, dy_high)
    other_dy[...] = jnp.where(first, dy_high, dy_low)


def matches(meta, k, base, count):
    lane = lax.broadcasted_iota(jnp.int32, (meta.shape[0], count), 1).astype(F32)
    code = meta[:, CODE + k : CODE + k + 1] - base
    return (code == lane) | (code - 64.0 == lane)


def owner_of_row(rows, count, per, start=0):
    row = lax.broadcasted_iota(jnp.int32, (rows, count), 0) + start
    lane = lax.broadcasted_iota(jnp.int32, (rows, count), 1)
    return lax.div(row, per) == lane


def pack_x_kernel(
    n_local, top, per, b0, b1, b2, b3, out_hbm, pick_ref, gated_ref, meta_out, tokens, out, sems
):
    half = b0.shape[1] - META
    count = tokens.shape[0]
    block = b0.shape[0]
    for m, b in enumerate((b0, b1, b2, b3)):
        tokens[m * block : (m + 1) * block] = b[...]
    meta_out[...] = tokens[:, half:]
    lane = lax.broadcasted_iota(jnp.int32, (4 * top, META), 1)
    row = lax.broadcasted_iota(jnp.int32, (4 * top, META), 0)
    turn = jnp.where(lane == row, 1.0, 0.0).astype(BF)
    meta = dot(turn, tokens[:, half:], LAST)
    base = (1 + lax.div(lax.axis_index("group"), 2) * n_local).astype(F32)
    expert = lax.broadcasted_iota(jnp.int32, (n_local, count), 0).astype(F32) + base
    named = jnp.zeros((n_local, count), F32)
    gate = jnp.zeros((n_local, count), F32)
    for k in range(top):
        code = meta[CODE + k : CODE + k + 1]
        kept = meta[SLOT + k : SLOT + k + 1] < CAP
        hit = ((code == expert) | (code - 64.0 == expert)) & kept
        named = jnp.where(hit, 1.0, named)
        gate = jnp.where(hit, meta[GATE + k : GATE + k + 1], gate)
    row = lax.broadcasted_iota(jnp.int32, (count, count), 0)
    col = lax.broadcasted_iota(jnp.int32, (count, count), 1)
    before = jnp.where(row < col, 1.0, 0.0).astype(BF)
    rank = jnp.where(named > 0.0, dot(named.astype(BF), before), -1.0)
    position = lax.broadcasted_iota(jnp.int32, (per, count), 0).astype(F32)
    for j in range(n_local):
        at = slice(j * per, (j + 1) * per)
        hit = rank[j : j + 1] == position
        pick_ref[at] = jnp.where(hit, 1.0, 0.0).astype(BF)
        gated_ref[at] = jnp.where(hit, gate[j : j + 1], 0.0).astype(BF)
    multiply_out(pick_ref, tokens, out, out_hbm, sems)


def multiply_out(left, right, out, out_hbm, sems):
    parts = sems.shape[0]
    size = out.shape[0] // parts

    def copy(i):
        at = pl.ds(pl.multiple_of(i * size, size), size)
        return pltpu.make_async_copy(out.at[at], out_hbm.at[at], sems.at[i])

    def step(i, carry):
        at = pl.ds(pl.multiple_of(i * size, size), size)
        out[at] = dot(left[at], right[...]).astype(BF)
        copy(i).start()
        return carry

    lax.fori_loop(0, parts, step, 0)
    for i in range(parts):
        copy(i).wait()


def pack_dy_kernel(gated_ref, b0, b1, b2, b3, out_hbm, tokens, out, sems):
    block = b0.shape[0]
    for m, b in enumerate((b0, b1, b2, b3)):
        tokens[m * block : (m + 1) * block] = b[...]
    multiply_out(gated_ref, tokens, out, out_hbm, sems)


def dequant(quant_ref, scales_ref, out_ref, row, col):
    rows, cols = quant_ref.shape
    for c in range(cols // 128):
        for r in range(rows // 128):
            at = (slice(r * 128, (r + 1) * 128), slice(c * 128, (c + 1) * 128))
            factor = jnp.full((1, 16, 128), scales_ref[col + c, row + r], F32).astype(BF)
            out_ref[at] = (quant_ref[at].reshape(8, 16, 128) * factor).reshape(128, 128)


def columns(i, size):
    return (slice(None), pl.ds(pl.multiple_of(i * size, size), size))


def fetch(source, target, sems, i, size):
    at = columns(i, size)
    return pltpu.make_async_copy(source.at[at], target.at[at], sems.at[i])


def compact(slot_ref, rows_ref, kept, size=512):
    def step(i, carry):
        at = columns(i, size)
        kept[at] = dot(slot_ref[...], rows_ref[at]).astype(BF)
        return carry

    lax.fori_loop(0, kept.shape[1] // size, step, 0)


def forward_kernel(
    n_local, top, cols, sg_ref, su_ref, x_ref, wg_hbm, wu_hbm,
    kept_hbm, send_ref, slot_ref, kept, wg_raw, wu_raw, wg, wu, sems_g, sems_u, sem_k,
):
    half, hidden = wg_raw.shape
    steps = hidden // cols
    for i in range(steps):
        fetch(wg_hbm, wg_raw, sems_g, i, cols).start()
        fetch(wu_hbm, wu_raw, sems_u, i, cols).start()
    lane = lax.broadcasted_iota(jnp.int32, (2 * top, META), 1)
    row = lax.broadcasted_iota(jnp.int32, (2 * top, META), 0)
    turn = jnp.where(lane == row, 1.0, 0.0).astype(BF)
    meta = dot(turn, x_ref[:, half:], LAST)
    own = (
        1 + lax.div(lax.axis_index("group"), 2) * n_local + lax.axis_index("local")
    ).astype(F32)
    target = jnp.full((1, meta.shape[1]), -1.0, F32)
    for k in range(top):
        code = meta[CODE + k : CODE + k + 1]
        slot = meta[SLOT + k : SLOT + k + 1]
        target = jnp.where(code == own, slot, target)
        target = jnp.where(code == own + 64.0, slot + CAP, target)
    row = lax.broadcasted_iota(jnp.int32, slot_ref.shape, 0).astype(F32)
    slot_ref[...] = jnp.where(row == target, 1.0, 0.0).astype(BF)
    compact(slot_ref, x_ref, kept)
    save = pltpu.make_async_copy(kept, kept_hbm, sem_k)
    save.start()

    def step(i, carry):
        at = columns(i, cols)
        fetch(wg_hbm, wg_raw, sems_g, i, cols).wait()
        fetch(wu_hbm, wu_raw, sems_u, i, cols).wait()
        dequant(wg_raw.at[at], sg_ref, wg, 0, i * (cols // 128))
        dequant(wu_raw.at[at], su_ref, wu, 0, i * (cols // 128))
        send_ref[(0, *at)] = dot(kept[...], wg[...]).astype(BF)
        send_ref[(1, *at)] = dot(kept[...], wu[...]).astype(BF)
        return carry

    lax.fori_loop(0, steps, step, 0)
    save.wait()


def down_kernel(
    cols, sv_ref, slot_ref, dy_ref, v_hbm, kept_hbm, send_ref, kept, v_raw, v, sems_v, sem_k
):
    half, hidden = v_raw.shape
    steps = hidden // cols
    for i in range(steps):
        fetch(v_hbm, v_raw, sems_v, i, cols).start()
    compact(slot_ref, dy_ref, kept)
    save = pltpu.make_async_copy(kept, kept_hbm, sem_k)
    save.start()

    def step(i, carry):
        at = columns(i, cols)
        fetch(v_hbm, v_raw, sems_v, i, cols).wait()
        dequant(v_raw.at[at], sv_ref, v, 0, i * (cols // 128))
        send_ref[at] = dot(kept[...], v[...]).astype(BF)
        return carry

    lax.fori_loop(0, steps, step, 0)
    save.wait()


def factor_kernel(
    chunk, sg_ref, su_ref, ab_ref, ab_in, wg_hbm, wu_hbm,
    factor_ref, hid_ref, both_w, wg_raw, wu_raw, sems_g, sems_u,
):
    half, hidden = wg_raw.shape
    parts = half // chunk
    block = 64

    def load(source, target, sems, i):
        at = pl.ds(pl.multiple_of(i * chunk, chunk), chunk)
        return pltpu.make_async_copy(source.at[at], target.at[at], sems.at[i])

    for i in range(parts):
        load(wg_hbm, wg_raw, sems_g, i).start()
        load(wu_hbm, wu_raw, sems_u, i).start()

    def activate(i, carry):
        at = pl.ds(pl.multiple_of(i * block, block), block)
        act_a = ab_ref[0, at].astype(F32) + ab_in[0, at].astype(F32)
        act_b = ab_ref[1, at].astype(F32) + ab_in[1, at].astype(F32)
        sigma = jax.nn.sigmoid(act_a)
        silu_a = act_a * sigma
        hid_ref[at] = (silu_a * act_b).astype(BF)
        factor_ref[0, at] = act_b * sigma * (1.0 + act_a * (1.0 - sigma))
        factor_ref[1, at] = silu_a
        return carry

    lax.fori_loop(0, hid_ref.shape[0] // block, activate, 0)

    def step(i, carry):
        at = pl.ds(pl.multiple_of(i * chunk, chunk), chunk)
        load(wg_hbm, wg_raw, sems_g, i).wait()
        load(wu_hbm, wu_raw, sems_u, i).wait()
        dequant(wg_raw.at[at], sg_ref, both_w.at[at, :hidden], i * (chunk // 128), 0)
        dequant(wu_raw.at[at], su_ref, both_w.at[at, hidden:], i * (chunk // 128), 0)
        return carry

    lax.fori_loop(0, parts, step, 0)


def backward_kernel(
    chunk, factor_ref, hid_ref, dh_ref, dh_in, slot_ref, w_hbm,
    d_hbm, dx_hbm, d_ab, wide, pairs, both_w, dx, sems_w, sems_x, sem_d, sem_m,
):
    kept, hidden = hid_ref.shape
    half = both_w.shape[0]
    parts = half // chunk
    block = 64

    def load(i):
        at = pl.ds(pl.multiple_of(i * chunk, chunk), chunk)
        return pltpu.make_async_copy(w_hbm.at[at], both_w.at[at], sems_w.at[i])

    for i in range(parts):
        load(i).start()

    def activate(i, carry):
        at = pl.ds(pl.multiple_of(i * block, block), block)
        d_hidden = dh_ref[at].astype(F32) + dh_in[at].astype(F32)
        d_ab[0, at] = (d_hidden * factor_ref[0, at]).astype(BF)
        d_ab[1, at] = (d_hidden * factor_ref[1, at]).astype(BF)
        grad = jnp.sum(hid_ref[at].astype(F32) * d_hidden, axis=1, keepdims=True)
        high = grad.astype(BF).astype(F32)
        lane = lax.broadcasted_iota(jnp.int32, (block, META), 1)
        pair = jnp.where(lane == 0, high, jnp.where(lane == 1, grad - high, 0.0))
        pairs[at] = pair.astype(BF)
        return carry

    lax.fori_loop(0, kept // block, activate, 0)
    save = pltpu.make_async_copy(d_ab, d_hbm, sem_d)
    save.start()

    def widen(i, carry):
        wide[columns(i, hidden)] = dot(slot_ref[...], d_ab[i], ROWS).astype(BF)
        return carry

    lax.fori_loop(0, 2, widen, 0)
    dx[:, half:] = dot(slot_ref[...], pairs[...], ROWS).astype(BF)
    tail = pltpu.make_async_copy(dx.at[:, half:], dx_hbm.at[:, half:], sem_m)
    tail.start()

    def step(i, carry):
        at = pl.ds(pl.multiple_of(i * chunk, chunk), chunk)
        load(i).wait()
        dx[columns(i, chunk)] = dot(wide[...], both_w[at], LAST).astype(BF)
        fetch(dx, dx_hbm, sems_x, i, chunk).start()
        return carry

    lax.fori_loop(0, parts, step, 0)
    for i in range(parts):
        fetch(dx, dx_hbm, sems_x, i, chunk).wait()
    tail.wait()
    save.wait()


def combine_kernel(n_local, top, ret_ref, pick_ref, meta_ref, *outs):
    width = ret_ref.shape[1] - META
    pick = pick_ref[...]
    meta = meta_ref[...].astype(F32)
    total = dot(pick, ret_ref[:, :width], ROWS).astype(BF)
    rows = ret_ref.shape[0]
    owner = owner_of_row(rows, n_local, rows // n_local)
    grads = ret_ref[:, width:].astype(F32)
    high = jnp.where(owner, grads[:, 0:1], 0.0).astype(BF)
    low = jnp.where(owner, grads[:, 1:2], 0.0).astype(BF)
    by_expert = dot(pick, high, ROWS) + dot(pick, low, ROWS)
    base = (1 + lax.div(lax.axis_index("group"), 2) * n_local).astype(F32)
    lane = lax.broadcasted_iota(jnp.int32, meta.shape, 1)
    tail = jnp.zeros(meta.shape, F32)
    for k in range(top):
        hit = matches(meta, k, base, n_local) & (meta[:, SLOT + k : SLOT + k + 1] < CAP)
        value = jnp.sum(jnp.where(hit, by_expert, 0.0), axis=1, keepdims=True)
        tail = jnp.where(lane == k, value / meta[:, GATE + k : GATE + k + 1], tail)
    tail = tail.astype(BF)
    block = outs[0].shape[0]
    for m, out in enumerate(outs):
        out[:, :width] = total[m * block : (m + 1) * block]
        out[:, width:] = tail[m * block : (m + 1) * block]


def finish_kernel(b0, b1, b2, b3, tokens_ref, gates_ref):
    half = tokens_ref.shape[1] // 2
    first = lax.rem(lax.axis_index("group"), 2) == 0
    own = b0[...].astype(F32) + b2[...].astype(F32)
    other = b1[:, :half].astype(F32) + b3[:, :half].astype(F32)
    mine = own[:, :half]
    tokens_ref[:, :half] = jnp.where(first, mine, other).astype(BF)
    tokens_ref[:, half:] = jnp.where(first, other, mine).astype(BF)
    lane = lax.broadcasted_iota(jnp.int32, (gates_ref.shape[0], META), 1)
    row = lax.broadcasted_iota(jnp.int32, (gates_ref.shape[0], META), 0)
    turn = jnp.where(lane == row, 1.0, 0.0).astype(BF)
    gates_ref[...] = dot(turn, own[:, half:].astype(BF), LAST).astype(BF)


def shape(*dims, dtype=BF):
    return jax.ShapeDtypeStruct(dims, dtype)


def shards(
    x_q,
    x_scale,
    cotangent,
    gates,
    experts,
    replicas,
    slots,
    w_gate_q,
    w_up_q,
    w_down_q,
    gate_scales,
    up_scales,
    down_scales,
):
    n_group = lax.axis_size("group")
    n_local = lax.axis_size("local")
    tok, width = x_q.shape
    top = experts.shape[1]
    half = width // 2
    hidden = w_gate_q.shape[2]
    column = n_group * tok
    rows = n_local * n_group * 4
    kept = 2 * CAP
    wide = half + META

    def across(block, apart):
        return lax.ppermute(block, "group", [(i, i ^ apart) for i in range(n_group)])

    def spread(block):
        return lax.all_to_all(block, "local", split_axis=0, concat_axis=0, tiled=True)

    same_x, other_x, same_dy, other_dy = call(
        prepare_kernel,
        (shape(tok, wide), shape(tok, wide), shape(tok, half), shape(tok, half)),
        (x_q, x_scale, cotangent, experts.T, replicas.T, slots.T, gates.T),
        limit=63,
        moved=tok * width * 8,
        grid=(1,),
        in_specs=[whole(tok, width), whole(*x_scale.shape), whole(tok, width)]
        + [whole(top, tok)] * 4,
        out_specs=[whole(tok, wide)] * 2 + [whole(tok, half)] * 2,
    )
    near_x = [same_x, across(other_x, 1), across(same_x, 2), across(other_x, 3)]
    near_dy = [same_dy, across(other_dy, 1), across(same_dy, 2), across(other_dy, 3)]
    packed_x, pick, gated, column_meta = call(
        functools.partial(pack_x_kernel, n_local, top, rows // n_local),
        (shape(rows, wide), shape(rows, column), shape(rows, column), shape(column, META)),
        tuple(near_x),
        limit=LIMIT,
        flops=2 * rows * column * wide,
        moved=2 * rows * wide,
        in_specs=[VMEM] * 4,
        out_specs=[HBM] + [VMEM] * 3,
        scratch_shapes=[pltpu.VMEM((column, wide), BF), pltpu.VMEM((rows, wide), BF), SEMS((4,))],
    )
    packed_dy = call(
        pack_dy_kernel,
        shape(rows, half),
        (gated, *near_dy),
        limit=LIMIT,
        flops=2 * rows * column * half,
        moved=2 * rows * half,
        in_specs=[VMEM] * 5,
        out_specs=HBM,
        scratch_shapes=[pltpu.VMEM((column, half), BF), pltpu.VMEM((rows, half), BF), SEMS((4,))],
    )
    got_x = spread(packed_x)
    got_x, packed_dy = lax.optimization_barrier((got_x, packed_dy))
    got_dy = spread(packed_dy)

    weights = [w[:, 0, :] for w in (w_gate_q, w_up_q, w_down_q)]
    scales = [s[:, 0, :].T for s in (gate_scales, up_scales, down_scales)]
    cols = 256
    steps = hidden // cols
    raw = pltpu.VMEM((half, hidden), BF)
    rows_x, send_ab, slot_of = call(
        functools.partial(forward_kernel, n_local, top, cols),
        (shape(kept, half), shape(2, kept, hidden), shape(kept, rows)),
        (scales[0], scales[1], got_x, weights[0], weights[1]),
        limit=LIMIT_FORWARD,
        flops=4 * kept * half * hidden,
        moved=4 * half * hidden + 4 * rows * half,
        in_specs=[SMEM, SMEM, VMEM, HBM, HBM],
        out_specs=[HBM, VMEM, VMEM],
        scratch_shapes=[pltpu.VMEM((kept, half), BF), raw, raw]
        + [pltpu.VMEM((half, cols), BF)] * 2
        + [SEMS((steps,)), SEMS((steps,)), SEMS],
    )
    their_ab = across(send_ab, 1)
    rows_dy, send_dh = call(
        functools.partial(down_kernel, cols),
        (shape(kept, half), shape(kept, hidden)),
        (scales[2], slot_of, got_dy, weights[2]),
        limit=LIMIT_DOWN,
        flops=2 * kept * half * hidden,
        moved=2 * half * hidden + 4 * rows * half,
        in_specs=[SMEM, VMEM, VMEM, HBM],
        out_specs=[HBM, VMEM],
        scratch_shapes=[
            pltpu.VMEM((kept, half), BF), raw, pltpu.VMEM((half, cols), BF), SEMS((steps,)), SEMS,
        ],
    )
    their_dh = across(send_dh, 1)
    chunk = 512
    parts = half // chunk
    factor, hid, both_w = call(
        functools.partial(factor_kernel, chunk),
        (shape(2, kept, hidden, dtype=F32), shape(kept, hidden), shape(half, 2 * hidden)),
        (scales[0], scales[1], send_ab, their_ab, weights[0], weights[1]),
        limit=LIMIT_FACTOR,
        flops=16 * kept * hidden,
        moved=8 * half * hidden,
        in_specs=[SMEM, SMEM, VMEM, VMEM, HBM, HBM],
        out_specs=[VMEM] * 3,
        scratch_shapes=[raw, raw, SEMS((parts,)), SEMS((parts,))],
    )
    d_ab, dx = call(
        functools.partial(backward_kernel, chunk),
        (shape(2, kept, hidden), shape(rows, wide)),
        (factor, hid, send_dh, their_dh, slot_of, both_w),
        limit=LIMIT_BACKWARD,
        flops=4 * rows * half * hidden,
        moved=4 * half * hidden + 2 * rows * half,
        in_specs=[VMEM] * 5 + [HBM],
        out_specs=[HBM, HBM],
        scratch_shapes=[
            pltpu.VMEM((2, kept, hidden), BF),
            pltpu.VMEM((rows, 2 * hidden), BF),
            pltpu.VMEM((kept, META), BF),
            pltpu.VMEM((half, 2 * hidden), BF),
            pltpu.VMEM((rows, wide), BF),
            SEMS((parts,)),
            SEMS((parts,)),
            SEMS,
            SEMS,
        ],
    )
    returned = spread(dx)
    grads = [
        dot(left, right, ROWS).astype(BF)
        for left, right in ((rows_x, d_ab[0]), (rows_x, d_ab[1]), (rows_dy, hid))
    ]
    returned, *grads = lax.optimization_barrier((returned, *grads))
    blocks = call(
        functools.partial(combine_kernel, n_local, top),
        tuple(shape(tok, wide) for _ in range(n_group)),
        (returned, pick, column_meta),
        flops=2 * rows * column * half,
        limit=24,
        moved=2 * rows * half,
        in_specs=[VMEM] * 3,
        out_specs=[VMEM] * n_group,
    )
    back = [blocks[0]] + [across(blocks[m], m) for m in range(1, n_group)]
    grad_tokens, grad_gates = call(
        finish_kernel,
        (shape(tok, width), shape(top, tok)),
        tuple(back),
        limit=24,
        moved=tok * width * 6,
        grid=(1,),
        in_specs=[whole(tok, wide)] * 4,
        out_specs=[whole(tok, width), whole(top, tok)],
    )
    return (
        grad_tokens,
        grad_gates.T,
        grads[0][:, None, :],
        grads[1][:, None, :],
        grads[2][:, None, :],
    )


def solution(mesh):
    by_token = P(("group", "local"), None)
    by_expert = P("group", "local", None)
    return jax.shard_map(
        shards,
        mesh=mesh,
        in_specs=(by_token,) * 7 + (by_expert,) * 6,
        out_specs=(by_token,) * 2 + (by_expert,) * 3,
        check_vma=False,
    )
```

```python
import functools

import jax
import jax.numpy as jnp
from jax import lax
from jax.experimental import pallas as pl
from jax.experimental.pallas import tpu as pltpu
from jax.sharding import PartitionSpec as P

CAP = 192
META = 128
CODE, SLOT, GATE = 0, 8, 16
BF = jnp.bfloat16
F32 = jnp.float32
MIB = 1024 * 1024
LIMIT = 24
LIMIT_FACTOR = 52
LIMIT_FORWARD = 52
LIMIT_DOWN = 52
LIMIT_BACKWARD = 51

ROWS = (((0,), (0,)), ((), ()))
LAST = (((1,), (1,)), ((), ()))


def dot(left, right, dims=(((1,), (0,)), ((), ()))):
    return lax.dot_general(left, right, dims, preferred_element_type=F32)


def call(kernel, outs, args, limit, flops=0, moved=0, **kw):
    return pl.pallas_call(
        kernel,
        out_shape=outs,
        compiler_params=pltpu.CompilerParams(vmem_limit_bytes=limit * MIB),
        cost_estimate=pl.CostEstimate(flops=flops, bytes_accessed=moved, transcendentals=0),
        **kw,
    )(*args)


SMEM = pl.BlockSpec(memory_space=pltpu.SMEM)
VMEM = pl.BlockSpec(memory_space=pltpu.VMEM)
HBM = pl.BlockSpec(memory_space=pltpu.HBM)
SEMS = pltpu.SemaphoreType.DMA


def whole(*dims):
    return pl.BlockSpec(dims, lambda i: (0,) * len(dims))


def placed(source, offset):
    lane = lax.broadcasted_iota(jnp.int32, (source.shape[0], META), 1)
    row = lax.broadcasted_iota(jnp.int32, (source.shape[0], META), 0)
    return dot(source.astype(BF), jnp.where(lane == row + offset, 1.0, 0.0).astype(BF), ROWS)


def prepare_kernel(
    xq_ref, xs_ref, dy_ref, e_ref, r_ref, s_ref, g_ref, same_x, other_x, same_dy, other_dy
):
    half = xq_ref.shape[1] // 2
    blocks = half // 128
    first = lax.rem(lax.axis_index("group"), 2) == 0
    code = (1 + e_ref[...] + 64 * r_ref[...]).astype(F32)
    meta = placed(code, CODE) + placed(s_ref[...].astype(F32), SLOT) + placed(g_ref[...], GATE)
    same_x[:, half:] = meta.astype(BF)
    other_x[:, half:] = meta.astype(BF)
    for c in range(blocks):
        low, high = c * 128, half + c * 128
        x_low = (xq_ref[:, low : low + 128].astype(F32) * xs_ref[:, c : c + 1]).astype(BF)
        x_high = (
            xq_ref[:, high : high + 128].astype(F32) * xs_ref[:, blocks + c : blocks + c + 1]
        ).astype(BF)
        same_x[:, low : low + 128] = jnp.where(first, x_low, x_high)
        other_x[:, low : low + 128] = jnp.where(first, x_high, x_low)
    dy_low, dy_high = dy_ref[:, :half], dy_ref[:, half:]
    same_dy[...] = jnp.where(first, dy_low, dy_high)
    other_dy[...] = jnp.where(first, dy_high, dy_low)


def matches(meta, k, base, count):
    lane = lax.broadcasted_iota(jnp.int32, (meta.shape[0], count), 1).astype(F32)
    code = meta[:, CODE + k : CODE + k + 1] - base
    return (code == lane) | (code - 64.0 == lane)


def owner_of_row(rows, count, per, start=0):
    row = lax.broadcasted_iota(jnp.int32, (rows, count), 0) + start
    lane = lax.broadcasted_iota(jnp.int32, (rows, count), 1)
    return lax.div(row, per) == lane


def pack_x_kernel(
    n_local, top, per, b0, b1, b2, b3, out_hbm, pick_ref, gated_ref, meta_out, tokens, out, sems
):
    half = b0.shape[1] - META
    count = tokens.shape[0]
    block = b0.shape[0]
    for m, b in enumerate((b0, b1, b2, b3)):
        tokens[m * block : (m + 1) * block] = b[...]
    meta_out[...] = tokens[:, half:]
    lane = lax.broadcasted_iota(jnp.int32, (4 * top, META), 1)
    row = lax.broadcasted_iota(jnp.int32, (4 * top, META), 0)
    turn = jnp.where(lane == row, 1.0, 0.0).astype(BF)
    meta = dot(turn, tokens[:, half:], LAST)
    base = (1 + lax.div(lax.axis_index("group"), 2) * n_local).astype(F32)
    expert = lax.broadcasted_iota(jnp.int32, (n_local, count), 0).astype(F32) + base
    named = jnp.zeros((n_local, count), F32)
    gate = jnp.zeros((n_local, count), F32)
    for k in range(top):
        code = meta[CODE + k : CODE + k + 1]
        kept = meta[SLOT + k : SLOT + k + 1] < CAP
        hit = ((code == expert) | (code - 64.0 == expert)) & kept
        named = jnp.where(hit, 1.0, named)
        gate = jnp.where(hit, meta[GATE + k : GATE + k + 1], gate)
    row = lax.broadcasted_iota(jnp.int32, (count, count), 0)
    col = lax.broadcasted_iota(jnp.int32, (count, count), 1)
    before = jnp.where(row < col, 1.0, 0.0).astype(BF)
    rank = jnp.where(named > 0.0, dot(named.astype(BF), before), -1.0)
    position = lax.broadcasted_iota(jnp.int32, (per, count), 0).astype(F32)
    for j in range(n_local):
        at = slice(j * per, (j + 1) * per)
        hit = rank[j : j + 1] == position
        pick_ref[at] = jnp.where(hit, 1.0, 0.0).astype(BF)
        gated_ref[at] = jnp.where(hit, gate[j : j + 1], 0.0).astype(BF)
    multiply_out(pick_ref, tokens, out, out_hbm, sems)


def multiply_out(left, right, out, out_hbm, sems):
    parts = sems.shape[0]
    size = out.shape[0] // parts

    def copy(i):
        at = pl.ds(pl.multiple_of(i * size, size), size)
        return pltpu.make_async_copy(out.at[at], out_hbm.at[at], sems.at[i])

    def step(i, carry):
        at = pl.ds(pl.multiple_of(i * size, size), size)
        out[at] = dot(left[at], right[...]).astype(BF)
        copy(i).start()
        return carry

    lax.fori_loop(0, parts, step, 0)
    for i in range(parts):
        copy(i).wait()


def pack_dy_kernel(gated_ref, b0, b1, b2, b3, out_hbm, tokens, out, sems):
    block = b0.shape[0]
    for m, b in enumerate((b0, b1, b2, b3)):
        tokens[m * block : (m + 1) * block] = b[...]
    multiply_out(gated_ref, tokens, out, out_hbm, sems)


def dequant(quant_ref, scales_ref, out_ref, row, col):
    rows, cols = quant_ref.shape
    for c in range(cols // 128):
        for r in range(rows // 128):
            at = (slice(r * 128, (r + 1) * 128), slice(c * 128, (c + 1) * 128))
            factor = jnp.full((1, 16, 128), scales_ref[col + c, row + r], F32).astype(BF)
            out_ref[at] = (quant_ref[at].reshape(8, 16, 128) * factor).reshape(128, 128)


def columns(i, size):
    return (slice(None), pl.ds(pl.multiple_of(i * size, size), size))


def fetch(source, target, sems, i, size):
    at = columns(i, size)
    return pltpu.make_async_copy(source.at[at], target.at[at], sems.at[i])


def start_all(source, target, sems):
    for i in range(sems.shape[0]):
        fetch(source, target, sems, i, target.shape[1] // sems.shape[0]).start()


def compact(slot_ref, rows_hbm, rows_ref, sems, kept):
    size = kept.shape[1] // sems.shape[0]

    def step(i, carry):
        at = columns(i, size)
        fetch(rows_hbm, rows_ref, sems, i, size).wait()
        kept[at] = dot(slot_ref[...], rows_ref[at]).astype(BF)
        return carry

    lax.fori_loop(0, kept.shape[1] // size, step, 0)


def forward_kernel(
    n_local, top, cols, sg_ref, su_ref, x_hbm, wg_hbm, wu_hbm,
    kept_hbm, send_ref, slot_ref, x_ref, meta_ref, kept, wg_raw, wu_raw, wg, wu,
    sems_x, sems_g, sems_u, sem_m, sem_k,
):
    half, hidden = wg_raw.shape
    steps = hidden // cols
    tail = pltpu.make_async_copy(x_hbm.at[:, half:], meta_ref, sem_m)
    tail.start()
    start_all(x_hbm, x_ref, sems_x)
    for i in range(steps):
        fetch(wg_hbm, wg_raw, sems_g, i, cols).start()
        fetch(wu_hbm, wu_raw, sems_u, i, cols).start()
    lane = lax.broadcasted_iota(jnp.int32, (2 * top, META), 1)
    row = lax.broadcasted_iota(jnp.int32, (2 * top, META), 0)
    turn = jnp.where(lane == row, 1.0, 0.0).astype(BF)
    tail.wait()
    meta = dot(turn, meta_ref[...], LAST)
    own = (
        1 + lax.div(lax.axis_index("group"), 2) * n_local + lax.axis_index("local")
    ).astype(F32)
    target = jnp.full((1, meta.shape[1]), -1.0, F32)
    for k in range(top):
        code = meta[CODE + k : CODE + k + 1]
        slot = meta[SLOT + k : SLOT + k + 1]
        target = jnp.where(code == own, slot, target)
        target = jnp.where(code == own + 64.0, slot + CAP, target)
    row = lax.broadcasted_iota(jnp.int32, slot_ref.shape, 0).astype(F32)
    slot_ref[...] = jnp.where(row == target, 1.0, 0.0).astype(BF)
    compact(slot_ref, x_hbm, x_ref, sems_x, kept)
    save = pltpu.make_async_copy(kept, kept_hbm, sem_k)
    save.start()

    def step(i, carry):
        at = columns(i, cols)
        fetch(wg_hbm, wg_raw, sems_g, i, cols).wait()
        fetch(wu_hbm, wu_raw, sems_u, i, cols).wait()
        dequant(wg_raw.at[at], sg_ref, wg, 0, i * (cols // 128))
        dequant(wu_raw.at[at], su_ref, wu, 0, i * (cols // 128))
        send_ref[(0, *at)] = dot(kept[...], wg[...]).astype(BF)
        send_ref[(1, *at)] = dot(kept[...], wu[...]).astype(BF)
        return carry

    lax.fori_loop(0, steps, step, 0)
    save.wait()


def down_kernel(
    cols, sv_ref, slot_ref, dy_hbm, v_hbm, kept_hbm, send_ref,
    dy_ref, kept, v_raw, v, sems_y, sems_v, sem_k,
):
    half, hidden = v_raw.shape
    steps = hidden // cols
    start_all(dy_hbm, dy_ref, sems_y)
    for i in range(steps):
        fetch(v_hbm, v_raw, sems_v, i, cols).start()
    compact(slot_ref, dy_hbm, dy_ref, sems_y, kept)
    save = pltpu.make_async_copy(kept, kept_hbm, sem_k)
    save.start()

    def step(i, carry):
        at = columns(i, cols)
        fetch(v_hbm, v_raw, sems_v, i, cols).wait()
        dequant(v_raw.at[at], sv_ref, v, 0, i * (cols // 128))
        send_ref[at] = dot(kept[...], v[...]).astype(BF)
        return carry

    lax.fori_loop(0, steps, step, 0)
    save.wait()


def factor_kernel(
    chunk, sg_ref, su_ref, ab_ref, ab_in, wg_hbm, wu_hbm,
    factor_ref, hid_ref, both_w, wg_raw, wu_raw, sems_g, sems_u,
):
    half, hidden = wg_raw.shape
    parts = half // chunk
    block = 64

    def load(source, target, sems, i):
        at = pl.ds(pl.multiple_of(i * chunk, chunk), chunk)
        return pltpu.make_async_copy(source.at[at], target.at[at], sems.at[i])

    for i in range(parts):
        load(wg_hbm, wg_raw, sems_g, i).start()
        load(wu_hbm, wu_raw, sems_u, i).start()

    def activate(i, carry):
        at = pl.ds(pl.multiple_of(i * block, block), block)
        act_a = ab_ref[0, at].astype(F32) + ab_in[0, at].astype(F32)
        act_b = ab_ref[1, at].astype(F32) + ab_in[1, at].astype(F32)
        sigma = jax.nn.sigmoid(act_a)
        silu_a = act_a * sigma
        hid_ref[at] = (silu_a * act_b).astype(BF)
        factor_ref[0, at] = act_b * sigma * (1.0 + act_a * (1.0 - sigma))
        factor_ref[1, at] = silu_a
        return carry

    lax.fori_loop(0, hid_ref.shape[0] // block, activate, 0)

    def step(i, carry):
        at = pl.ds(pl.multiple_of(i * chunk, chunk), chunk)
        load(wg_hbm, wg_raw, sems_g, i).wait()
        load(wu_hbm, wu_raw, sems_u, i).wait()
        dequant(wg_raw.at[at], sg_ref, both_w.at[at, :hidden], i * (chunk // 128), 0)
        dequant(wu_raw.at[at], su_ref, both_w.at[at, hidden:], i * (chunk // 128), 0)
        return carry

    lax.fori_loop(0, parts, step, 0)


def backward_kernel(
    chunk, factor_hbm, hid_ref, dh_ref, dh_in, slot_ref, w_hbm,
    d_hbm, dx_hbm, factor_ref, d_ab, wide, pairs, both_w, dx, sems_f, sems_w, sems_x, sem_d, sem_m,
):
    kept, hidden = hid_ref.shape
    half = both_w.shape[0]
    parts = half // chunk
    block = kept // sems_f.shape[0]

    def factors(i):
        at = (slice(None), pl.ds(pl.multiple_of(i * block, block), block))
        return pltpu.make_async_copy(factor_hbm.at[at], factor_ref.at[at], sems_f.at[i])

    for i in range(kept // block):
        factors(i).start()

    def load(i):
        at = pl.ds(pl.multiple_of(i * chunk, chunk), chunk)
        return pltpu.make_async_copy(w_hbm.at[at], both_w.at[at], sems_w.at[i])

    for i in range(parts):
        load(i).start()

    def activate(i, carry):
        at = pl.ds(pl.multiple_of(i * block, block), block)
        d_hidden = dh_ref[at].astype(F32) + dh_in[at].astype(F32)
        factors(i).wait()
        d_ab[0, at] = (d_hidden * factor_ref[0, at]).astype(BF)
        d_ab[1, at] = (d_hidden * factor_ref[1, at]).astype(BF)
        grad = jnp.sum(hid_ref[at].astype(F32) * d_hidden, axis=1, keepdims=True)
        high = grad.astype(BF).astype(F32)
        lane = lax.broadcasted_iota(jnp.int32, (block, META), 1)
        pair = jnp.where(lane == 0, high, jnp.where(lane == 1, grad - high, 0.0))
        pairs[at] = pair.astype(BF)
        return carry

    lax.fori_loop(0, kept // block, activate, 0)
    save = pltpu.make_async_copy(d_ab, d_hbm, sem_d)
    save.start()

    def widen(i, carry):
        wide[columns(i, hidden)] = dot(slot_ref[...], d_ab[i], ROWS).astype(BF)
        return carry

    lax.fori_loop(0, 2, widen, 0)
    dx[:, half:] = dot(slot_ref[...], pairs[...], ROWS).astype(BF)
    tail = pltpu.make_async_copy(dx.at[:, half:], dx_hbm.at[:, half:], sem_m)
    tail.start()

    def step(i, carry):
        at = pl.ds(pl.multiple_of(i * chunk, chunk), chunk)
        load(i).wait()
        dx[columns(i, chunk)] = dot(wide[...], both_w[at], LAST).astype(BF)
        fetch(dx, dx_hbm, sems_x, i, chunk).start()
        return carry

    lax.fori_loop(0, parts, step, 0)
    for i in range(parts):
        fetch(dx, dx_hbm, sems_x, i, chunk).wait()
    tail.wait()
    save.wait()


def combine_kernel(n_local, top, ret_ref, pick_ref, meta_ref, *outs):
    width = ret_ref.shape[1] - META
    pick = pick_ref[...]
    meta = meta_ref[...].astype(F32)
    total = dot(pick, ret_ref[:, :width], ROWS).astype(BF)
    rows = ret_ref.shape[0]
    owner = owner_of_row(rows, n_local, rows // n_local)
    grads = ret_ref[:, width:].astype(F32)
    high = jnp.where(owner, grads[:, 0:1], 0.0).astype(BF)
    low = jnp.where(owner, grads[:, 1:2], 0.0).astype(BF)
    by_expert = dot(pick, high, ROWS) + dot(pick, low, ROWS)
    base = (1 + lax.div(lax.axis_index("group"), 2) * n_local).astype(F32)
    lane = lax.broadcasted_iota(jnp.int32, meta.shape, 1)
    tail = jnp.zeros(meta.shape, F32)
    for k in range(top):
        hit = matches(meta, k, base, n_local) & (meta[:, SLOT + k : SLOT + k + 1] < CAP)
        value = jnp.sum(jnp.where(hit, by_expert, 0.0), axis=1, keepdims=True)
        tail = jnp.where(lane == k, value / meta[:, GATE + k : GATE + k + 1], tail)
    tail = tail.astype(BF)
    block = outs[0].shape[0]
    for m, out in enumerate(outs):
        out[:, :width] = total[m * block : (m + 1) * block]
        out[:, width:] = tail[m * block : (m + 1) * block]


def finish_kernel(b0, b1, b2, b3, tokens_ref, gates_ref):
    half = tokens_ref.shape[1] // 2
    first = lax.rem(lax.axis_index("group"), 2) == 0
    own = b0[...].astype(F32) + b2[...].astype(F32)
    other = b1[:, :half].astype(F32) + b3[:, :half].astype(F32)
    mine = own[:, :half]
    tokens_ref[:, :half] = jnp.where(first, mine, other).astype(BF)
    tokens_ref[:, half:] = jnp.where(first, other, mine).astype(BF)
    lane = lax.broadcasted_iota(jnp.int32, (gates_ref.shape[0], META), 1)
    row = lax.broadcasted_iota(jnp.int32, (gates_ref.shape[0], META), 0)
    turn = jnp.where(lane == row, 1.0, 0.0).astype(BF)
    gates_ref[...] = dot(turn, own[:, half:].astype(BF), LAST).astype(BF)


def shape(*dims, dtype=BF):
    return jax.ShapeDtypeStruct(dims, dtype)


def shards(
    x_q,
    x_scale,
    cotangent,
    gates,
    experts,
    replicas,
    slots,
    w_gate_q,
    w_up_q,
    w_down_q,
    gate_scales,
    up_scales,
    down_scales,
):
    n_group = lax.axis_size("group")
    n_local = lax.axis_size("local")
    tok, width = x_q.shape
    top = experts.shape[1]
    half = width // 2
    hidden = w_gate_q.shape[2]
    column = n_group * tok
    rows = n_local * n_group * 4
    kept = 2 * CAP
    wide = half + META

    def across(block, apart):
        return lax.ppermute(block, "group", [(i, i ^ apart) for i in range(n_group)])

    def spread(block):
        return lax.all_to_all(block, "local", split_axis=0, concat_axis=0, tiled=True)

    same_x, other_x, same_dy, other_dy = call(
        prepare_kernel,
        (shape(tok, wide), shape(tok, wide), shape(tok, half), shape(tok, half)),
        (x_q, x_scale, cotangent, experts.T, replicas.T, slots.T, gates.T),
        limit=63,
        moved=tok * width * 8,
        grid=(1,),
        in_specs=[whole(tok, width), whole(*x_scale.shape), whole(tok, width)]
        + [whole(top, tok)] * 4,
        out_specs=[whole(tok, wide)] * 2 + [whole(tok, half)] * 2,
    )
    near_x = [same_x, across(other_x, 1), across(same_x, 2), across(other_x, 3)]
    near_dy = [same_dy, across(other_dy, 1), across(same_dy, 2), across(other_dy, 3)]
    packed_x, pick, gated, column_meta = call(
        functools.partial(pack_x_kernel, n_local, top, rows // n_local),
        (shape(rows, wide), shape(rows, column), shape(rows, column), shape(column, META)),
        tuple(near_x),
        limit=LIMIT,
        flops=2 * rows * column * wide,
        moved=2 * rows * wide,
        in_specs=[VMEM] * 4,
        out_specs=[HBM] + [VMEM] * 3,
        scratch_shapes=[pltpu.VMEM((column, wide), BF), pltpu.VMEM((rows, wide), BF), SEMS((4,))],
    )
    packed_dy = call(
        pack_dy_kernel,
        shape(rows, half),
        (gated, *near_dy),
        limit=LIMIT,
        flops=2 * rows * column * half,
        moved=2 * rows * half,
        in_specs=[VMEM] * 5,
        out_specs=HBM,
        scratch_shapes=[pltpu.VMEM((column, half), BF), pltpu.VMEM((rows, half), BF), SEMS((4,))],
    )
    got_x = spread(packed_x)
    got_x, packed_dy = lax.optimization_barrier((got_x, packed_dy))
    got_dy = spread(packed_dy)

    weights = [w[:, 0, :] for w in (w_gate_q, w_up_q, w_down_q)]
    scales = [s[:, 0, :].T for s in (gate_scales, up_scales, down_scales)]
    cols = 256
    steps = hidden // cols
    raw = pltpu.VMEM((half, hidden), BF)
    rows_x, send_ab, slot_of = call(
        functools.partial(forward_kernel, n_local, top, cols),
        (shape(kept, half), shape(2, kept, hidden), shape(kept, rows)),
        (scales[0], scales[1], got_x, weights[0], weights[1]),
        limit=LIMIT_FORWARD,
        flops=4 * kept * half * hidden,
        moved=4 * half * hidden + 4 * rows * half,
        in_specs=[SMEM, SMEM, HBM, HBM, HBM],
        out_specs=[HBM, VMEM, VMEM],
        scratch_shapes=[pltpu.VMEM((rows, half), BF), pltpu.VMEM((rows, META), BF)]
        + [pltpu.VMEM((kept, half), BF), raw, raw]
        + [pltpu.VMEM((half, cols), BF)] * 2
        + [SEMS((4,)), SEMS((steps,)), SEMS((steps,)), SEMS, SEMS],
    )
    their_ab = across(send_ab, 1)
    rows_dy, send_dh = call(
        functools.partial(down_kernel, cols),
        (shape(kept, half), shape(kept, hidden)),
        (scales[2], slot_of, got_dy, weights[2]),
        limit=LIMIT_DOWN,
        flops=2 * kept * half * hidden,
        moved=2 * half * hidden + 4 * rows * half,
        in_specs=[SMEM, VMEM, HBM, HBM],
        out_specs=[HBM, VMEM],
        scratch_shapes=[
            pltpu.VMEM((rows, half), BF), pltpu.VMEM((kept, half), BF), raw,
            pltpu.VMEM((half, cols), BF), SEMS((4,)), SEMS((steps,)), SEMS,
        ],
    )
    their_dh = across(send_dh, 1)
    chunk = 512
    parts = half // chunk
    factor, hid, both_w = call(
        functools.partial(factor_kernel, chunk),
        (shape(2, kept, hidden, dtype=F32), shape(kept, hidden), shape(half, 2 * hidden)),
        (scales[0], scales[1], send_ab, their_ab, weights[0], weights[1]),
        limit=LIMIT_FACTOR,
        flops=16 * kept * hidden,
        moved=8 * half * hidden,
        in_specs=[SMEM, SMEM, VMEM, VMEM, HBM, HBM],
        out_specs=[VMEM] * 3,
        scratch_shapes=[raw, raw, SEMS((parts,)), SEMS((parts,))],
    )
    d_ab, dx = call(
        functools.partial(backward_kernel, chunk),
        (shape(2, kept, hidden), shape(rows, wide)),
        (factor, hid, send_dh, their_dh, slot_of, both_w),
        limit=LIMIT_BACKWARD,
        flops=4 * rows * half * hidden,
        moved=4 * half * hidden + 2 * rows * half,
        in_specs=[HBM] + [VMEM] * 4 + [HBM],
        out_specs=[HBM, HBM],
        scratch_shapes=[
            pltpu.VMEM((2, kept, hidden), F32),
            pltpu.VMEM((2, kept, hidden), BF),
            pltpu.VMEM((rows, 2 * hidden), BF),
            pltpu.VMEM((kept, META), BF),
            pltpu.VMEM((half, 2 * hidden), BF),
            pltpu.VMEM((rows, wide), BF),
            SEMS((4,)),
            SEMS((parts,)),
            SEMS((parts,)),
            SEMS,
            SEMS,
        ],
    )
    returned = spread(dx)
    grads = [
        dot(left, right, ROWS).astype(BF)
        for left, right in ((rows_x, d_ab[0]), (rows_x, d_ab[1]), (rows_dy, hid))
    ]
    returned, *grads = lax.optimization_barrier((returned, *grads))
    blocks = call(
        functools.partial(combine_kernel, n_local, top),
        tuple(shape(tok, wide) for _ in range(n_group)),
        (returned, pick, column_meta),
        flops=2 * rows * column * half,
        limit=24,
        moved=2 * rows * half,
        in_specs=[VMEM] * 3,
        out_specs=[VMEM] * n_group,
    )
    back = [blocks[0]] + [across(blocks[m], m) for m in range(1, n_group)]
    grad_tokens, grad_gates = call(
        finish_kernel,
        (shape(tok, width), shape(top, tok)),
        tuple(back),
        limit=24,
        moved=tok * width * 6,
        grid=(1,),
        in_specs=[whole(tok, wide)] * 4,
        out_specs=[whole(tok, width), whole(top, tok)],
    )
    return (
        grad_tokens,
        grad_gates.T,
        grads[0][:, None, :],
        grads[1][:, None, :],
        grads[2][:, None, :],
    )


def solution(mesh):
    by_token = P(("group", "local"), None)
    by_expert = P("group", "local", None)
    return jax.shard_map(
        shards,
        mesh=mesh,
        in_specs=(by_token,) * 7 + (by_expert,) * 6,
        out_specs=(by_token,) * 2 + (by_expert,) * 3,
        check_vma=False,
    )
```

```python
import functools

import jax
import jax.numpy as jnp
from jax import lax
from jax.experimental import pallas as pl
from jax.experimental.pallas import tpu as pltpu
from jax.sharding import PartitionSpec as P

CAP = 192
META = 128
CODE, SLOT, GATE = 0, 8, 16
BF = jnp.bfloat16
F32 = jnp.float32
MIB = 1024 * 1024
LIMIT = 24
LIMIT_FACTOR = 52
LIMIT_FORWARD = 52
LIMIT_DOWN = 52
LIMIT_BACKWARD = 51

ROWS = (((0,), (0,)), ((), ()))
LAST = (((1,), (1,)), ((), ()))


def dot(left, right, dims=(((1,), (0,)), ((), ()))):
    return lax.dot_general(left, right, dims, preferred_element_type=F32)


def call(kernel, outs, args, limit, flops=0, moved=0, **kw):
    return pl.pallas_call(
        kernel,
        out_shape=outs,
        compiler_params=pltpu.CompilerParams(vmem_limit_bytes=limit * MIB),
        cost_estimate=pl.CostEstimate(flops=flops, bytes_accessed=moved, transcendentals=0),
        **kw,
    )(*args)


SMEM = pl.BlockSpec(memory_space=pltpu.SMEM)
VMEM = pl.BlockSpec(memory_space=pltpu.VMEM)
HBM = pl.BlockSpec(memory_space=pltpu.HBM)
SEMS = pltpu.SemaphoreType.DMA


def whole(*dims):
    return pl.BlockSpec(dims, lambda i: (0,) * len(dims))


def placed(source, offset):
    lane = lax.broadcasted_iota(jnp.int32, (source.shape[0], META), 1)
    row = lax.broadcasted_iota(jnp.int32, (source.shape[0], META), 0)
    return dot(source.astype(BF), jnp.where(lane == row + offset, 1.0, 0.0).astype(BF), ROWS)


def prepare_kernel(
    xq_ref, xs_ref, dy_ref, e_ref, r_ref, s_ref, g_ref, same_x, other_x, same_dy, other_dy
):
    half = xq_ref.shape[1] // 2
    blocks = half // 128
    first = lax.rem(lax.axis_index("group"), 2) == 0
    code = (1 + e_ref[...] + 64 * r_ref[...]).astype(F32)
    meta = placed(code, CODE) + placed(s_ref[...].astype(F32), SLOT) + placed(g_ref[...], GATE)
    same_x[:, half:] = meta.astype(BF)
    other_x[:, half:] = meta.astype(BF)
    for c in range(blocks):
        low, high = c * 128, half + c * 128
        x_low = (xq_ref[:, low : low + 128].astype(F32) * xs_ref[:, c : c + 1]).astype(BF)
        x_high = (
            xq_ref[:, high : high + 128].astype(F32) * xs_ref[:, blocks + c : blocks + c + 1]
        ).astype(BF)
        same_x[:, low : low + 128] = jnp.where(first, x_low, x_high)
        other_x[:, low : low + 128] = jnp.where(first, x_high, x_low)
    dy_low, dy_high = dy_ref[:, :half], dy_ref[:, half:]
    same_dy[...] = jnp.where(first, dy_low, dy_high)
    other_dy[...] = jnp.where(first, dy_high, dy_low)


def matches(meta, k, base, count):
    lane = lax.broadcasted_iota(jnp.int32, (meta.shape[0], count), 1).astype(F32)
    code = meta[:, CODE + k : CODE + k + 1] - base
    return (code == lane) | (code - 64.0 == lane)


def owner_of_row(rows, count, per, start=0):
    row = lax.broadcasted_iota(jnp.int32, (rows, count), 0) + start
    lane = lax.broadcasted_iota(jnp.int32, (rows, count), 1)
    return lax.div(row, per) == lane


def pack_x_kernel(
    n_local, top, per, b0, b1, b2, b3, out_hbm, pick_ref, gated_ref, meta_out, tokens, out, sems
):
    half = b0.shape[1] - META
    count = tokens.shape[0]
    block = b0.shape[0]
    for m, b in enumerate((b0, b1, b2, b3)):
        tokens[m * block : (m + 1) * block] = b[...]
    meta_out[...] = tokens[:, half:]
    lane = lax.broadcasted_iota(jnp.int32, (4 * top, META), 1)
    row = lax.broadcasted_iota(jnp.int32, (4 * top, META), 0)
    turn = jnp.where(lane == row, 1.0, 0.0).astype(BF)
    meta = dot(turn, tokens[:, half:], LAST)
    base = (1 + lax.div(lax.axis_index("group"), 2) * n_local).astype(F32)
    expert = lax.broadcasted_iota(jnp.int32, (n_local, count), 0).astype(F32) + base
    named = jnp.zeros((n_local, count), F32)
    gate = jnp.zeros((n_local, count), F32)
    for k in range(top):
        code = meta[CODE + k : CODE + k + 1]
        kept = meta[SLOT + k : SLOT + k + 1] < CAP
        hit = ((code == expert) | (code - 64.0 == expert)) & kept
        named = jnp.where(hit, 1.0, named)
        gate = jnp.where(hit, meta[GATE + k : GATE + k + 1], gate)
    row = lax.broadcasted_iota(jnp.int32, (count, count), 0)
    col = lax.broadcasted_iota(jnp.int32, (count, count), 1)
    before = jnp.where(row < col, 1.0, 0.0).astype(BF)
    rank = jnp.where(named > 0.0, dot(named.astype(BF), before), -1.0)
    position = lax.broadcasted_iota(jnp.int32, (per, count), 0).astype(F32)
    for j in range(n_local):
        at = slice(j * per, (j + 1) * per)
        hit = rank[j : j + 1] == position
        pick_ref[at] = jnp.where(hit, 1.0, 0.0).astype(BF)
        gated_ref[at] = jnp.where(hit, gate[j : j + 1], 0.0).astype(BF)
    multiply_out(pick_ref, tokens, out, out_hbm, sems)


def multiply_out(left, right, out, out_hbm, sems):
    parts = sems.shape[0]
    size = out.shape[0] // parts

    def copy(i):
        at = pl.ds(pl.multiple_of(i * size, size), size)
        return pltpu.make_async_copy(out.at[at], out_hbm.at[at], sems.at[i])

    def step(i, carry):
        at = pl.ds(pl.multiple_of(i * size, size), size)
        out[at] = dot(left[at], right[...]).astype(BF)
        copy(i).start()
        return carry

    lax.fori_loop(0, parts, step, 0)
    for i in range(parts):
        copy(i).wait()


def pack_dy_kernel(gated_ref, b0, b1, b2, b3, out_hbm, tokens, out, sems):
    block = b0.shape[0]
    for m, b in enumerate((b0, b1, b2, b3)):
        tokens[m * block : (m + 1) * block] = b[...]
    multiply_out(gated_ref, tokens, out, out_hbm, sems)


def dequant(quant_ref, scales_ref, out_ref, row, col):
    rows, cols = quant_ref.shape
    for c in range(cols // 128):
        for r in range(rows // 128):
            at = (slice(r * 128, (r + 1) * 128), slice(c * 128, (c + 1) * 128))
            factor = jnp.full((1, 16, 128), scales_ref[col + c, row + r], F32).astype(BF)
            out_ref[at] = (quant_ref[at].reshape(8, 16, 128) * factor).reshape(128, 128)


def columns(i, size):
    return (slice(None), pl.ds(pl.multiple_of(i * size, size), size))


def fetch(source, target, sems, i, size):
    at = columns(i, size)
    return pltpu.make_async_copy(source.at[at], target.at[at], sems.at[i])


def start_all(source, target, sems):
    for i in range(sems.shape[0]):
        fetch(source, target, sems, i, target.shape[1] // sems.shape[0]).start()


def compact(slot_ref, rows_hbm, rows_ref, sems, kept):
    size = kept.shape[1] // sems.shape[0]

    def step(i, carry):
        at = columns(i, size)
        fetch(rows_hbm, rows_ref, sems, i, size).wait()
        kept[at] = dot(slot_ref[...], rows_ref[at]).astype(BF)
        return carry

    lax.fori_loop(0, kept.shape[1] // size, step, 0)


def forward_kernel(
    n_local, top, cols, sg_ref, x_hbm, wg_hbm,
    kept_hbm, send_ref, slot_ref, x_ref, meta_ref, kept, wg_raw, wg,
    sems_x, sems_g, sem_m, sem_k,
):
    half, hidden = wg_raw.shape
    steps = hidden // cols
    tail = pltpu.make_async_copy(x_hbm.at[:, half:], meta_ref, sem_m)
    tail.start()
    start_all(x_hbm, x_ref, sems_x)
    for i in range(steps):
        fetch(wg_hbm, wg_raw, sems_g, i, cols).start()
    lane = lax.broadcasted_iota(jnp.int32, (2 * top, META), 1)
    row = lax.broadcasted_iota(jnp.int32, (2 * top, META), 0)
    turn = jnp.where(lane == row, 1.0, 0.0).astype(BF)
    tail.wait()
    meta = dot(turn, meta_ref[...], LAST)
    own = (
        1 + lax.div(lax.axis_index("group"), 2) * n_local + lax.axis_index("local")
    ).astype(F32)
    target = jnp.full((1, meta.shape[1]), -1.0, F32)
    for k in range(top):
        code = meta[CODE + k : CODE + k + 1]
        slot = meta[SLOT + k : SLOT + k + 1]
        target = jnp.where(code == own, slot, target)
        target = jnp.where(code == own + 64.0, slot + CAP, target)
    row = lax.broadcasted_iota(jnp.int32, slot_ref.shape, 0).astype(F32)
    slot_ref[...] = jnp.where(row == target, 1.0, 0.0).astype(BF)
    compact(slot_ref, x_hbm, x_ref, sems_x, kept)
    save = pltpu.make_async_copy(kept, kept_hbm, sem_k)
    save.start()

    project(kept, wg_hbm, wg_raw, wg, sg_ref, sems_g, send_ref)
    save.wait()


def project(kept, w_hbm, w_raw, w, scales_ref, sems, send_ref):
    cols = w.shape[1]

    def step(i, carry):
        at = columns(i, cols)
        fetch(w_hbm, w_raw, sems, i, cols).wait()
        dequant(w_raw.at[at], scales_ref, w, 0, i * (cols // 128))
        send_ref[at] = dot(kept[...], w[...]).astype(BF)
        return carry

    lax.fori_loop(0, sems.shape[0], step, 0)


def up_kernel(s_ref, kept_ref, w_hbm, send_ref, w_raw, w, sems):
    start_all(w_hbm, w_raw, sems)
    project(kept_ref, w_hbm, w_raw, w, s_ref, sems, send_ref)


def down_kernel(
    cols, sv_ref, slot_ref, dy_hbm, v_hbm, kept_hbm, send_ref,
    dy_ref, kept, v_raw, v, sems_y, sems_v, sem_k,
):
    half, hidden = v_raw.shape
    steps = hidden // cols
    start_all(dy_hbm, dy_ref, sems_y)
    for i in range(steps):
        fetch(v_hbm, v_raw, sems_v, i, cols).start()
    compact(slot_ref, dy_hbm, dy_ref, sems_y, kept)
    save = pltpu.make_async_copy(kept, kept_hbm, sem_k)
    save.start()

    project(kept, v_hbm, v_raw, v, sv_ref, sems_v, send_ref)
    save.wait()


def factor_kernel(
    chunk, sg_ref, su_ref, a_ref, b_ref, a_in, b_in, wg_hbm, wu_hbm,
    factor_ref, hid_ref, both_w, wg_raw, wu_raw, sems_g, sems_u,
):
    half, hidden = wg_raw.shape
    parts = half // chunk
    block = 64

    def load(source, target, sems, i):
        at = pl.ds(pl.multiple_of(i * chunk, chunk), chunk)
        return pltpu.make_async_copy(source.at[at], target.at[at], sems.at[i])

    for i in range(parts):
        load(wg_hbm, wg_raw, sems_g, i).start()
        load(wu_hbm, wu_raw, sems_u, i).start()

    def activate(i, carry):
        at = pl.ds(pl.multiple_of(i * block, block), block)
        act_a = a_ref[at].astype(F32) + a_in[at].astype(F32)
        act_b = b_ref[at].astype(F32) + b_in[at].astype(F32)
        sigma = jax.nn.sigmoid(act_a)
        silu_a = act_a * sigma
        hid_ref[at] = (silu_a * act_b).astype(BF)
        factor_ref[0, at] = act_b * sigma * (1.0 + act_a * (1.0 - sigma))
        factor_ref[1, at] = silu_a
        return carry

    lax.fori_loop(0, hid_ref.shape[0] // block, activate, 0)

    def step(i, carry):
        at = pl.ds(pl.multiple_of(i * chunk, chunk), chunk)
        load(wg_hbm, wg_raw, sems_g, i).wait()
        load(wu_hbm, wu_raw, sems_u, i).wait()
        dequant(wg_raw.at[at], sg_ref, both_w.at[at, :hidden], i * (chunk // 128), 0)
        dequant(wu_raw.at[at], su_ref, both_w.at[at, hidden:], i * (chunk // 128), 0)
        return carry

    lax.fori_loop(0, parts, step, 0)


def backward_kernel(
    chunk, factor_hbm, hid_ref, dh_ref, dh_in, slot_ref, w_hbm,
    d_hbm, dx_hbm, factor_ref, d_ab, wide, pairs, both_w, dx, sems_f, sems_w, sems_x, sem_d, sem_m,
):
    kept, hidden = hid_ref.shape
    half = both_w.shape[0]
    parts = half // chunk
    block = kept // sems_f.shape[0]

    def factors(i):
        at = (slice(None), pl.ds(pl.multiple_of(i * block, block), block))
        return pltpu.make_async_copy(factor_hbm.at[at], factor_ref.at[at], sems_f.at[i])

    for i in range(kept // block):
        factors(i).start()

    def load(i):
        at = pl.ds(pl.multiple_of(i * chunk, chunk), chunk)
        return pltpu.make_async_copy(w_hbm.at[at], both_w.at[at], sems_w.at[i])

    for i in range(parts):
        load(i).start()

    def activate(i, carry):
        at = pl.ds(pl.multiple_of(i * block, block), block)
        d_hidden = dh_ref[at].astype(F32) + dh_in[at].astype(F32)
        factors(i).wait()
        d_ab[0, at] = (d_hidden * factor_ref[0, at]).astype(BF)
        d_ab[1, at] = (d_hidden * factor_ref[1, at]).astype(BF)
        grad = jnp.sum(hid_ref[at].astype(F32) * d_hidden, axis=1, keepdims=True)
        high = grad.astype(BF).astype(F32)
        lane = lax.broadcasted_iota(jnp.int32, (block, META), 1)
        pair = jnp.where(lane == 0, high, jnp.where(lane == 1, grad - high, 0.0))
        pairs[at] = pair.astype(BF)
        return carry

    lax.fori_loop(0, kept // block, activate, 0)
    save = pltpu.make_async_copy(d_ab, d_hbm, sem_d)
    save.start()

    def widen(i, carry):
        wide[columns(i, hidden)] = dot(slot_ref[...], d_ab[i], ROWS).astype(BF)
        return carry

    lax.fori_loop(0, 2, widen, 0)
    dx[:, half:] = dot(slot_ref[...], pairs[...], ROWS).astype(BF)
    tail = pltpu.make_async_copy(dx.at[:, half:], dx_hbm.at[:, half:], sem_m)
    tail.start()

    def step(i, carry):
        at = pl.ds(pl.multiple_of(i * chunk, chunk), chunk)
        load(i).wait()
        dx[columns(i, chunk)] = dot(wide[...], both_w[at], LAST).astype(BF)
        fetch(dx, dx_hbm, sems_x, i, chunk).start()
        return carry

    lax.fori_loop(0, parts, step, 0)
    for i in range(parts):
        fetch(dx, dx_hbm, sems_x, i, chunk).wait()
    tail.wait()
    save.wait()


def combine_kernel(n_local, top, ret_ref, pick_ref, meta_ref, *outs):
    width = ret_ref.shape[1] - META
    pick = pick_ref[...]
    meta = meta_ref[...].astype(F32)
    total = dot(pick, ret_ref[:, :width], ROWS).astype(BF)
    rows = ret_ref.shape[0]
    owner = owner_of_row(rows, n_local, rows // n_local)
    grads = ret_ref[:, width:].astype(F32)
    high = jnp.where(owner, grads[:, 0:1], 0.0).astype(BF)
    low = jnp.where(owner, grads[:, 1:2], 0.0).astype(BF)
    by_expert = dot(pick, high, ROWS) + dot(pick, low, ROWS)
    base = (1 + lax.div(lax.axis_index("group"), 2) * n_local).astype(F32)
    lane = lax.broadcasted_iota(jnp.int32, meta.shape, 1)
    tail = jnp.zeros(meta.shape, F32)
    for k in range(top):
        hit = matches(meta, k, base, n_local) & (meta[:, SLOT + k : SLOT + k + 1] < CAP)
        value = jnp.sum(jnp.where(hit, by_expert, 0.0), axis=1, keepdims=True)
        tail = jnp.where(lane == k, value / meta[:, GATE + k : GATE + k + 1], tail)
    tail = tail.astype(BF)
    block = outs[0].shape[0]
    for m, out in enumerate(outs):
        out[:, :width] = total[m * block : (m + 1) * block]
        out[:, width:] = tail[m * block : (m + 1) * block]


def finish_kernel(b0, b1, b2, b3, tokens_ref, gates_ref):
    half = tokens_ref.shape[1] // 2
    first = lax.rem(lax.axis_index("group"), 2) == 0
    own = b0[...].astype(F32) + b2[...].astype(F32)
    other = b1[:, :half].astype(F32) + b3[:, :half].astype(F32)
    mine = own[:, :half]
    tokens_ref[:, :half] = jnp.where(first, mine, other).astype(BF)
    tokens_ref[:, half:] = jnp.where(first, other, mine).astype(BF)
    lane = lax.broadcasted_iota(jnp.int32, (gates_ref.shape[0], META), 1)
    row = lax.broadcasted_iota(jnp.int32, (gates_ref.shape[0], META), 0)
    turn = jnp.where(lane == row, 1.0, 0.0).astype(BF)
    gates_ref[...] = dot(turn, own[:, half:].astype(BF), LAST).astype(BF)


def shape(*dims, dtype=BF):
    return jax.ShapeDtypeStruct(dims, dtype)


def shards(
    x_q,
    x_scale,
    cotangent,
    gates,
    experts,
    replicas,
    slots,
    w_gate_q,
    w_up_q,
    w_down_q,
    gate_scales,
    up_scales,
    down_scales,
):
    n_group = lax.axis_size("group")
    n_local = lax.axis_size("local")
    tok, width = x_q.shape
    top = experts.shape[1]
    half = width // 2
    hidden = w_gate_q.shape[2]
    column = n_group * tok
    rows = n_local * n_group * 4
    kept = 2 * CAP
    wide = half + META

    def across(block, apart):
        return lax.ppermute(block, "group", [(i, i ^ apart) for i in range(n_group)])

    def spread(block):
        return lax.all_to_all(block, "local", split_axis=0, concat_axis=0, tiled=True)

    same_x, other_x, same_dy, other_dy = call(
        prepare_kernel,
        (shape(tok, wide), shape(tok, wide), shape(tok, half), shape(tok, half)),
        (x_q, x_scale, cotangent, experts.T, replicas.T, slots.T, gates.T),
        limit=63,
        moved=tok * width * 8,
        grid=(1,),
        in_specs=[whole(tok, width), whole(*x_scale.shape), whole(tok, width)]
        + [whole(top, tok)] * 4,
        out_specs=[whole(tok, wide)] * 2 + [whole(tok, half)] * 2,
    )
    near_x = [same_x, across(other_x, 1), across(same_x, 2), across(other_x, 3)]
    near_dy = [same_dy, across(other_dy, 1), across(same_dy, 2), across(other_dy, 3)]
    packed_x, pick, gated, column_meta = call(
        functools.partial(pack_x_kernel, n_local, top, rows // n_local),
        (shape(rows, wide), shape(rows, column), shape(rows, column), shape(column, META)),
        tuple(near_x),
        limit=LIMIT,
        flops=2 * rows * column * wide,
        moved=2 * rows * wide,
        in_specs=[VMEM] * 4,
        out_specs=[HBM] + [VMEM] * 3,
        scratch_shapes=[pltpu.VMEM((column, wide), BF), pltpu.VMEM((rows, wide), BF), SEMS((4,))],
    )
    packed_dy = call(
        pack_dy_kernel,
        shape(rows, half),
        (gated, *near_dy),
        limit=LIMIT,
        flops=2 * rows * column * half,
        moved=2 * rows * half,
        in_specs=[VMEM] * 5,
        out_specs=HBM,
        scratch_shapes=[pltpu.VMEM((column, half), BF), pltpu.VMEM((rows, half), BF), SEMS((4,))],
    )
    got_x = spread(packed_x)
    got_x, packed_dy = lax.optimization_barrier((got_x, packed_dy))
    got_dy = spread(packed_dy)

    weights = [w[:, 0, :] for w in (w_gate_q, w_up_q, w_down_q)]
    scales = [s[:, 0, :].T for s in (gate_scales, up_scales, down_scales)]
    cols = 256
    steps = hidden // cols
    raw = pltpu.VMEM((half, hidden), BF)
    rows_x, send_a, slot_of = call(
        functools.partial(forward_kernel, n_local, top, cols),
        (shape(kept, half), shape(kept, hidden), shape(kept, rows)),
        (scales[0], got_x, weights[0]),
        limit=LIMIT_FORWARD,
        flops=2 * kept * half * hidden,
        moved=2 * half * hidden + 4 * rows * half,
        in_specs=[SMEM, HBM, HBM],
        out_specs=[HBM, VMEM, VMEM],
        scratch_shapes=[pltpu.VMEM((rows, half), BF), pltpu.VMEM((rows, META), BF)]
        + [pltpu.VMEM((kept, half), BF), raw, pltpu.VMEM((half, cols), BF)]
        + [SEMS((4,)), SEMS((steps,)), SEMS, SEMS],
    )
    their_a = across(send_a, 1)
    send_b = call(
        up_kernel,
        shape(kept, hidden),
        (scales[1], rows_x, weights[1]),
        limit=LIMIT_FORWARD,
        flops=2 * kept * half * hidden,
        moved=2 * half * hidden + 2 * kept * half,
        in_specs=[SMEM, VMEM, HBM],
        out_specs=VMEM,
        scratch_shapes=[raw, pltpu.VMEM((half, cols), BF), SEMS((steps,))],
    )
    their_a, send_b = lax.optimization_barrier((their_a, send_b))
    their_b = across(send_b, 1)
    rows_dy, send_dh = call(
        functools.partial(down_kernel, cols),
        (shape(kept, half), shape(kept, hidden)),
        (scales[2], slot_of, got_dy, weights[2]),
        limit=LIMIT_DOWN,
        flops=2 * kept * half * hidden,
        moved=2 * half * hidden + 4 * rows * half,
        in_specs=[SMEM, VMEM, HBM, HBM],
        out_specs=[HBM, VMEM],
        scratch_shapes=[
            pltpu.VMEM((rows, half), BF), pltpu.VMEM((kept, half), BF), raw,
            pltpu.VMEM((half, cols), BF), SEMS((4,)), SEMS((steps,)), SEMS,
        ],
    )
    their_dh = across(send_dh, 1)
    chunk = 512
    parts = half // chunk
    factor, hid, both_w = call(
        functools.partial(factor_kernel, chunk),
        (shape(2, kept, hidden, dtype=F32), shape(kept, hidden), shape(half, 2 * hidden)),
        (scales[0], scales[1], send_a, send_b, their_a, their_b, weights[0], weights[1]),
        limit=LIMIT_FACTOR,
        flops=16 * kept * hidden,
        moved=8 * half * hidden,
        in_specs=[SMEM, SMEM] + [VMEM] * 4 + [HBM, HBM],
        out_specs=[VMEM] * 3,
        scratch_shapes=[raw, raw, SEMS((parts,)), SEMS((parts,))],
    )
    d_ab, dx = call(
        functools.partial(backward_kernel, chunk),
        (shape(2, kept, hidden), shape(rows, wide)),
        (factor, hid, send_dh, their_dh, slot_of, both_w),
        limit=LIMIT_BACKWARD,
        flops=4 * rows * half * hidden,
        moved=4 * half * hidden + 2 * rows * half,
        in_specs=[HBM] + [VMEM] * 4 + [HBM],
        out_specs=[HBM, HBM],
        scratch_shapes=[
            pltpu.VMEM((2, kept, hidden), F32),
            pltpu.VMEM((2, kept, hidden), BF),
            pltpu.VMEM((rows, 2 * hidden), BF),
            pltpu.VMEM((kept, META), BF),
            pltpu.VMEM((half, 2 * hidden), BF),
            pltpu.VMEM((rows, wide), BF),
            SEMS((4,)),
            SEMS((parts,)),
            SEMS((parts,)),
            SEMS,
            SEMS,
        ],
    )
    returned = spread(dx)
    grads = [
        dot(left, right, ROWS).astype(BF)
        for left, right in ((rows_x, d_ab[0]), (rows_x, d_ab[1]), (rows_dy, hid))
    ]
    returned, *grads = lax.optimization_barrier((returned, *grads))
    blocks = call(
        functools.partial(combine_kernel, n_local, top),
        tuple(shape(tok, wide) for _ in range(n_group)),
        (returned, pick, column_meta),
        flops=2 * rows * column * half,
        limit=24,
        moved=2 * rows * half,
        in_specs=[VMEM] * 3,
        out_specs=[VMEM] * n_group,
    )
    back = [blocks[0]] + [across(blocks[m], m) for m in range(1, n_group)]
    grad_tokens, grad_gates = call(
        finish_kernel,
        (shape(tok, width), shape(top, tok)),
        tuple(back),
        limit=24,
        moved=tok * width * 6,
        grid=(1,),
        in_specs=[whole(tok, wide)] * 4,
        out_specs=[whole(tok, width), whole(top, tok)],
    )
    return (
        grad_tokens,
        grad_gates.T,
        grads[0][:, None, :],
        grads[1][:, None, :],
        grads[2][:, None, :],
    )


def solution(mesh):
    by_token = P(("group", "local"), None)
    by_expert = P("group", "local", None)
    return jax.shard_map(
        shards,
        mesh=mesh,
        in_specs=(by_token,) * 7 + (by_expert,) * 6,
        out_specs=(by_token,) * 2 + (by_expert,) * 3,
        check_vma=False,
    )
```

```python
import functools

import jax
import jax.numpy as jnp
from jax import lax
from jax.experimental import pallas as pl
from jax.experimental.pallas import tpu as pltpu
from jax.sharding import PartitionSpec as P

CAP = 192
META = 128
CODE, SLOT, GATE = 0, 8, 16
BF = jnp.bfloat16
F32 = jnp.float32
MIB = 1024 * 1024
LIMIT = 24
LIMIT_FACTOR = 52
LIMIT_FORWARD = 52
LIMIT_DOWN = 52
LIMIT_BACKWARD = 51

ROWS = (((0,), (0,)), ((), ()))
LAST = (((1,), (1,)), ((), ()))


def dot(left, right, dims=(((1,), (0,)), ((), ()))):
    return lax.dot_general(left, right, dims, preferred_element_type=F32)


def call(kernel, outs, args, limit, flops=0, moved=0, **kw):
    return pl.pallas_call(
        kernel,
        out_shape=outs,
        compiler_params=pltpu.CompilerParams(vmem_limit_bytes=limit * MIB),
        cost_estimate=pl.CostEstimate(flops=flops, bytes_accessed=moved, transcendentals=0),
        **kw,
    )(*args)


SMEM = pl.BlockSpec(memory_space=pltpu.SMEM)
VMEM = pl.BlockSpec(memory_space=pltpu.VMEM)
HBM = pl.BlockSpec(memory_space=pltpu.HBM)
SEMS = pltpu.SemaphoreType.DMA


def whole(*dims):
    return pl.BlockSpec(dims, lambda i: (0,) * len(dims))


def placed(source, offset):
    lane = lax.broadcasted_iota(jnp.int32, (source.shape[0], META), 1)
    row = lax.broadcasted_iota(jnp.int32, (source.shape[0], META), 0)
    return dot(source.astype(BF), jnp.where(lane == row + offset, 1.0, 0.0).astype(BF), ROWS)


def prepare_kernel(
    xq_ref, xs_ref, dy_ref, e_ref, r_ref, s_ref, g_ref, same_x, other_x, same_dy, other_dy
):
    half = xq_ref.shape[1] // 2
    blocks = half // 128
    first = lax.rem(lax.axis_index("group"), 2) == 0
    code = (1 + e_ref[...] + 64 * r_ref[...]).astype(F32)
    meta = placed(code, CODE) + placed(s_ref[...].astype(F32), SLOT) + placed(g_ref[...], GATE)
    same_x[:, half:] = meta.astype(BF)
    other_x[:, half:] = meta.astype(BF)
    for c in range(blocks):
        low, high = c * 128, half + c * 128
        x_low = (xq_ref[:, low : low + 128].astype(F32) * xs_ref[:, c : c + 1]).astype(BF)
        x_high = (
            xq_ref[:, high : high + 128].astype(F32) * xs_ref[:, blocks + c : blocks + c + 1]
        ).astype(BF)
        same_x[:, low : low + 128] = jnp.where(first, x_low, x_high)
        other_x[:, low : low + 128] = jnp.where(first, x_high, x_low)
    dy_low, dy_high = dy_ref[:, :half], dy_ref[:, half:]
    same_dy[...] = jnp.where(first, dy_low, dy_high)
    other_dy[...] = jnp.where(first, dy_high, dy_low)


def matches(meta, k, base, count):
    lane = lax.broadcasted_iota(jnp.int32, (meta.shape[0], count), 1).astype(F32)
    code = meta[:, CODE + k : CODE + k + 1] - base
    return (code == lane) | (code - 64.0 == lane)


def owner_of_row(rows, count, per, start=0):
    row = lax.broadcasted_iota(jnp.int32, (rows, count), 0) + start
    lane = lax.broadcasted_iota(jnp.int32, (rows, count), 1)
    return lax.div(row, per) == lane


def pack_x_kernel(
    n_local, top, per, b0, b1, b2, b3, out_hbm, pick_ref, gated_ref, meta_out, tokens, out, sems
):
    half = b0.shape[1] - META
    count = tokens.shape[0]
    block = b0.shape[0]
    for m, b in enumerate((b0, b1, b2, b3)):
        tokens[m * block : (m + 1) * block] = b[...]
    meta_out[...] = tokens[:, half:]
    lane = lax.broadcasted_iota(jnp.int32, (4 * top, META), 1)
    row = lax.broadcasted_iota(jnp.int32, (4 * top, META), 0)
    turn = jnp.where(lane == row, 1.0, 0.0).astype(BF)
    meta = dot(turn, tokens[:, half:], LAST)
    base = (1 + lax.div(lax.axis_index("group"), 2) * n_local).astype(F32)
    expert = lax.broadcasted_iota(jnp.int32, (n_local, count), 0).astype(F32) + base
    named = jnp.zeros((n_local, count), F32)
    gate = jnp.zeros((n_local, count), F32)
    for k in range(top):
        code = meta[CODE + k : CODE + k + 1]
        kept = meta[SLOT + k : SLOT + k + 1] < CAP
        hit = ((code == expert) | (code - 64.0 == expert)) & kept
        named = jnp.where(hit, 1.0, named)
        gate = jnp.where(hit, meta[GATE + k : GATE + k + 1], gate)
    row = lax.broadcasted_iota(jnp.int32, (count, count), 0)
    col = lax.broadcasted_iota(jnp.int32, (count, count), 1)
    before = jnp.where(row < col, 1.0, 0.0).astype(BF)
    rank = jnp.where(named > 0.0, dot(named.astype(BF), before), -1.0)
    position = lax.broadcasted_iota(jnp.int32, (per, count), 0).astype(F32)
    for j in range(n_local):
        at = slice(j * per, (j + 1) * per)
        hit = rank[j : j + 1] == position
        pick_ref[at] = jnp.where(hit, 1.0, 0.0).astype(BF)
        gated_ref[at] = jnp.where(hit, gate[j : j + 1], 0.0).astype(BF)
    multiply_out(pick_ref, tokens, out, out_hbm, sems)


def multiply_out(left, right, out, out_hbm, sems):
    parts = sems.shape[0]
    size = out.shape[0] // parts

    def copy(i):
        at = pl.ds(pl.multiple_of(i * size, size), size)
        return pltpu.make_async_copy(out.at[at], out_hbm.at[at], sems.at[i])

    def step(i, carry):
        at = pl.ds(pl.multiple_of(i * size, size), size)
        out[at] = dot(left[at], right[...]).astype(BF)
        copy(i).start()
        return carry

    lax.fori_loop(0, parts, step, 0)
    for i in range(parts):
        copy(i).wait()


def pack_dy_kernel(gated_ref, b0, b1, b2, b3, out_hbm, tokens, out, sems):
    block = b0.shape[0]
    for m, b in enumerate((b0, b1, b2, b3)):
        tokens[m * block : (m + 1) * block] = b[...]
    multiply_out(gated_ref, tokens, out, out_hbm, sems)


def dequant(quant_ref, scales_ref, out_ref, row, col):
    rows, cols = quant_ref.shape
    for c in range(cols // 128):
        for r in range(rows // 128):
            at = (slice(r * 128, (r + 1) * 128), slice(c * 128, (c + 1) * 128))
            factor = jnp.full((1, 16, 128), scales_ref[col + c, row + r], F32).astype(BF)
            out_ref[at] = (quant_ref[at].reshape(8, 16, 128) * factor).reshape(128, 128)


def columns(i, size):
    return (slice(None), pl.ds(pl.multiple_of(i * size, size), size))


def fetch(source, target, sems, i, size):
    at = columns(i, size)
    return pltpu.make_async_copy(source.at[at], target.at[at], sems.at[i])


def start_all(source, target, sems):
    for i in range(sems.shape[0]):
        fetch(source, target, sems, i, target.shape[1] // sems.shape[0]).start()


def compact(slot_ref, rows_hbm, rows_ref, sems, kept):
    size = kept.shape[1] // sems.shape[0]

    def step(i, carry):
        at = columns(i, size)
        fetch(rows_hbm, rows_ref, sems, i, size).wait()
        kept[at] = dot(slot_ref[...], rows_ref[at]).astype(BF)
        return carry

    lax.fori_loop(0, kept.shape[1] // size, step, 0)


def forward_kernel(
    n_local, top, cols, sg_ref, x_hbm, wg_hbm,
    send_ref, slot_ref, x_ref, meta_ref, kept, wg_raw, wg, sems_x, sems_g, sem_m,
):
    half, hidden = wg_raw.shape
    steps = hidden // cols
    tail = pltpu.make_async_copy(x_hbm.at[:, half:], meta_ref, sem_m)
    tail.start()
    start_all(x_hbm, x_ref, sems_x)
    for i in range(steps):
        fetch(wg_hbm, wg_raw, sems_g, i, cols).start()
    lane = lax.broadcasted_iota(jnp.int32, (2 * top, META), 1)
    row = lax.broadcasted_iota(jnp.int32, (2 * top, META), 0)
    turn = jnp.where(lane == row, 1.0, 0.0).astype(BF)
    tail.wait()
    meta = dot(turn, meta_ref[...], LAST)
    own = (
        1 + lax.div(lax.axis_index("group"), 2) * n_local + lax.axis_index("local")
    ).astype(F32)
    target = jnp.full((1, meta.shape[1]), -1.0, F32)
    for k in range(top):
        code = meta[CODE + k : CODE + k + 1]
        slot = meta[SLOT + k : SLOT + k + 1]
        target = jnp.where(code == own, slot, target)
        target = jnp.where(code == own + 64.0, slot + CAP, target)
    row = lax.broadcasted_iota(jnp.int32, slot_ref.shape, 0).astype(F32)
    slot_ref[...] = jnp.where(row == target, 1.0, 0.0).astype(BF)
    compact(slot_ref, x_hbm, x_ref, sems_x, kept)
    project(kept, wg_hbm, wg_raw, wg, sg_ref, sems_g, send_ref)


def project(kept, w_hbm, w_raw, w, scales_ref, sems, send_ref):
    cols = w.shape[1]

    def step(i, carry):
        at = columns(i, cols)
        fetch(w_hbm, w_raw, sems, i, cols).wait()
        dequant(w_raw.at[at], scales_ref, w, 0, i * (cols // 128))
        send_ref[at] = dot(kept[...], w[...]).astype(BF)
        return carry

    lax.fori_loop(0, sems.shape[0], step, 0)


def project_kernel(
    cols, sv_ref, slot_ref, dy_hbm, v_hbm, kept_hbm, send_ref,
    dy_ref, kept, v_raw, v, sems_y, sems_v, sem_k,
):
    half, hidden = v_raw.shape
    steps = hidden // cols
    start_all(dy_hbm, dy_ref, sems_y)
    for i in range(steps):
        fetch(v_hbm, v_raw, sems_v, i, cols).start()
    compact(slot_ref, dy_hbm, dy_ref, sems_y, kept)
    save = pltpu.make_async_copy(kept, kept_hbm, sem_k)
    save.start()

    project(kept, v_hbm, v_raw, v, sv_ref, sems_v, send_ref)
    save.wait()


def factor_kernel(
    chunk, sg_ref, su_ref, a_ref, b_ref, a_in, b_in, wg_hbm, wu_hbm,
    factor_ref, hid_ref, both_w, wg_raw, wu_raw, sems_g, sems_u,
):
    half, hidden = wg_raw.shape
    parts = half // chunk
    block = 64

    def load(source, target, sems, i):
        at = pl.ds(pl.multiple_of(i * chunk, chunk), chunk)
        return pltpu.make_async_copy(source.at[at], target.at[at], sems.at[i])

    for i in range(parts):
        load(wg_hbm, wg_raw, sems_g, i).start()
        load(wu_hbm, wu_raw, sems_u, i).start()

    def activate(i, carry):
        at = pl.ds(pl.multiple_of(i * block, block), block)
        act_a = a_ref[at].astype(F32) + a_in[at].astype(F32)
        act_b = b_ref[at].astype(F32) + b_in[at].astype(F32)
        sigma = jax.nn.sigmoid(act_a)
        silu_a = act_a * sigma
        hid_ref[at] = (silu_a * act_b).astype(BF)
        factor_ref[0, at] = (act_b * sigma * (1.0 + act_a * (1.0 - sigma))).astype(BF)
        factor_ref[1, at] = silu_a.astype(BF)
        return carry

    lax.fori_loop(0, hid_ref.shape[0] // block, activate, 0)

    def step(i, carry):
        at = pl.ds(pl.multiple_of(i * chunk, chunk), chunk)
        load(wg_hbm, wg_raw, sems_g, i).wait()
        load(wu_hbm, wu_raw, sems_u, i).wait()
        dequant(wg_raw.at[at], sg_ref, both_w.at[at, :hidden], i * (chunk // 128), 0)
        dequant(wu_raw.at[at], su_ref, both_w.at[at, hidden:], i * (chunk // 128), 0)
        return carry

    lax.fori_loop(0, parts, step, 0)


def backward_kernel(
    chunk, factor_hbm, hid_ref, dh_ref, dh_in, slot_ref, w_hbm,
    d_hbm, dx_hbm, factor_ref, d_ab, wide, pairs, both_w, dx, sems_f, sems_w, sems_x, sem_d, sem_m,
):
    kept, hidden = hid_ref.shape
    half = both_w.shape[0]
    parts = half // chunk
    block = kept // sems_f.shape[0]

    def factors(i):
        at = (slice(None), pl.ds(pl.multiple_of(i * block, block), block))
        return pltpu.make_async_copy(factor_hbm.at[at], factor_ref.at[at], sems_f.at[i])

    for i in range(kept // block):
        factors(i).start()

    def load(i):
        at = pl.ds(pl.multiple_of(i * chunk, chunk), chunk)
        return pltpu.make_async_copy(w_hbm.at[at], both_w.at[at], sems_w.at[i])

    for i in range(parts):
        load(i).start()

    def activate(i, carry):
        at = pl.ds(pl.multiple_of(i * block, block), block)
        d_hidden = dh_ref[at].astype(F32) + dh_in[at].astype(F32)
        factors(i).wait()
        d_ab[0, at] = (d_hidden * factor_ref[0, at].astype(F32)).astype(BF)
        d_ab[1, at] = (d_hidden * factor_ref[1, at].astype(F32)).astype(BF)
        grad = jnp.sum(hid_ref[at].astype(F32) * d_hidden, axis=1, keepdims=True)
        high = grad.astype(BF).astype(F32)
        lane = lax.broadcasted_iota(jnp.int32, (block, META), 1)
        pair = jnp.where(lane == 0, high, jnp.where(lane == 1, grad - high, 0.0))
        pairs[at] = pair.astype(BF)
        return carry

    lax.fori_loop(0, kept // block, activate, 0)
    save = pltpu.make_async_copy(d_ab, d_hbm, sem_d)
    save.start()

    def widen(i, carry):
        wide[columns(i, hidden)] = dot(slot_ref[...], d_ab[i], ROWS).astype(BF)
        return carry

    lax.fori_loop(0, 2, widen, 0)
    dx[:, half:] = dot(slot_ref[...], pairs[...], ROWS).astype(BF)
    tail = pltpu.make_async_copy(dx.at[:, half:], dx_hbm.at[:, half:], sem_m)
    tail.start()

    def step(i, carry):
        at = pl.ds(pl.multiple_of(i * chunk, chunk), chunk)
        load(i).wait()
        dx[columns(i, chunk)] = dot(wide[...], both_w[at], LAST).astype(BF)
        fetch(dx, dx_hbm, sems_x, i, chunk).start()
        return carry

    lax.fori_loop(0, parts, step, 0)
    for i in range(parts):
        fetch(dx, dx_hbm, sems_x, i, chunk).wait()
    tail.wait()
    save.wait()


def combine_kernel(n_local, top, ret_ref, pick_ref, meta_ref, *outs):
    width = ret_ref.shape[1] - META
    pick = pick_ref[...]
    meta = meta_ref[...].astype(F32)
    total = dot(pick, ret_ref[:, :width], ROWS).astype(BF)
    rows = ret_ref.shape[0]
    owner = owner_of_row(rows, n_local, rows // n_local)
    grads = ret_ref[:, width:].astype(F32)
    high = jnp.where(owner, grads[:, 0:1], 0.0).astype(BF)
    low = jnp.where(owner, grads[:, 1:2], 0.0).astype(BF)
    by_expert = dot(pick, high, ROWS) + dot(pick, low, ROWS)
    base = (1 + lax.div(lax.axis_index("group"), 2) * n_local).astype(F32)
    lane = lax.broadcasted_iota(jnp.int32, meta.shape, 1)
    tail = jnp.zeros(meta.shape, F32)
    for k in range(top):
        hit = matches(meta, k, base, n_local) & (meta[:, SLOT + k : SLOT + k + 1] < CAP)
        value = jnp.sum(jnp.where(hit, by_expert, 0.0), axis=1, keepdims=True)
        tail = jnp.where(lane == k, value / meta[:, GATE + k : GATE + k + 1], tail)
    tail = tail.astype(BF)
    block = outs[0].shape[0]
    for m, out in enumerate(outs):
        out[:, :width] = total[m * block : (m + 1) * block]
        out[:, width:] = tail[m * block : (m + 1) * block]


def finish_kernel(b0, b1, b2, b3, tokens_ref, gates_ref):
    half = tokens_ref.shape[1] // 2
    first = lax.rem(lax.axis_index("group"), 2) == 0
    own = b0[...].astype(F32) + b2[...].astype(F32)
    other = b1[:, :half].astype(F32) + b3[:, :half].astype(F32)
    mine = own[:, :half]
    tokens_ref[:, :half] = jnp.where(first, mine, other).astype(BF)
    tokens_ref[:, half:] = jnp.where(first, other, mine).astype(BF)
    lane = lax.broadcasted_iota(jnp.int32, (gates_ref.shape[0], META), 1)
    row = lax.broadcasted_iota(jnp.int32, (gates_ref.shape[0], META), 0)
    turn = jnp.where(lane == row, 1.0, 0.0).astype(BF)
    gates_ref[...] = dot(turn, own[:, half:].astype(BF), LAST).astype(BF)


def shape(*dims, dtype=BF):
    return jax.ShapeDtypeStruct(dims, dtype)


def shards(
    x_q,
    x_scale,
    cotangent,
    gates,
    experts,
    replicas,
    slots,
    w_gate_q,
    w_up_q,
    w_down_q,
    gate_scales,
    up_scales,
    down_scales,
):
    n_group = lax.axis_size("group")
    n_local = lax.axis_size("local")
    tok, width = x_q.shape
    top = experts.shape[1]
    half = width // 2
    hidden = w_gate_q.shape[2]
    column = n_group * tok
    rows = n_local * n_group * 4
    kept = 2 * CAP
    wide = half + META

    def across(block, apart):
        return lax.ppermute(block, "group", [(i, i ^ apart) for i in range(n_group)])

    def spread(block):
        return lax.all_to_all(block, "local", split_axis=0, concat_axis=0, tiled=True)

    same_x, other_x, same_dy, other_dy = call(
        prepare_kernel,
        (shape(tok, wide), shape(tok, wide), shape(tok, half), shape(tok, half)),
        (x_q, x_scale, cotangent, experts.T, replicas.T, slots.T, gates.T),
        limit=63,
        moved=tok * width * 8,
        grid=(1,),
        in_specs=[whole(tok, width), whole(*x_scale.shape), whole(tok, width)]
        + [whole(top, tok)] * 4,
        out_specs=[whole(tok, wide)] * 2 + [whole(tok, half)] * 2,
    )
    near_x = [same_x, across(other_x, 1), across(same_x, 2), across(other_x, 3)]
    near_dy = [same_dy, across(other_dy, 1), across(same_dy, 2), across(other_dy, 3)]
    packed_x, pick, gated, column_meta = call(
        functools.partial(pack_x_kernel, n_local, top, rows // n_local),
        (shape(rows, wide), shape(rows, column), shape(rows, column), shape(column, META)),
        tuple(near_x),
        limit=LIMIT,
        flops=2 * rows * column * wide,
        moved=2 * rows * wide,
        in_specs=[VMEM] * 4,
        out_specs=[HBM] + [VMEM] * 3,
        scratch_shapes=[pltpu.VMEM((column, wide), BF), pltpu.VMEM((rows, wide), BF), SEMS((4,))],
    )
    packed_dy = call(
        pack_dy_kernel,
        shape(rows, half),
        (gated, *near_dy),
        limit=LIMIT,
        flops=2 * rows * column * half,
        moved=2 * rows * half,
        in_specs=[VMEM] * 5,
        out_specs=HBM,
        scratch_shapes=[pltpu.VMEM((column, half), BF), pltpu.VMEM((rows, half), BF), SEMS((4,))],
    )
    got_x = spread(packed_x)
    got_x, packed_dy = lax.optimization_barrier((got_x, packed_dy))
    got_dy = spread(packed_dy)

    weights = [w[:, 0, :] for w in (w_gate_q, w_up_q, w_down_q)]
    scales = [s[:, 0, :].T for s in (gate_scales, up_scales, down_scales)]
    cols = 256
    steps = hidden // cols
    raw = pltpu.VMEM((half, hidden), BF)
    send_a, slot_of = call(
        functools.partial(forward_kernel, n_local, top, cols),
        (shape(kept, hidden), shape(kept, rows)),
        (scales[0], got_x, weights[0]),
        limit=LIMIT_FORWARD,
        flops=2 * kept * half * hidden,
        moved=2 * half * hidden + 4 * rows * half,
        in_specs=[SMEM, HBM, HBM],
        out_specs=[VMEM, VMEM],
        scratch_shapes=[pltpu.VMEM((rows, half), BF), pltpu.VMEM((rows, META), BF)]
        + [pltpu.VMEM((kept, half), BF), raw, pltpu.VMEM((half, cols), BF)]
        + [SEMS((4,)), SEMS((steps,)), SEMS],
    )
    their_a = across(send_a, 1)
    rows_x, send_b = call(
        functools.partial(project_kernel, cols),
        (shape(kept, half), shape(kept, hidden)),
        (scales[1], slot_of, got_x, weights[1]),
        limit=LIMIT_DOWN,
        flops=2 * kept * half * hidden,
        moved=2 * half * hidden + 4 * rows * half,
        in_specs=[SMEM, VMEM, HBM, HBM],
        out_specs=[HBM, VMEM],
        scratch_shapes=[
            pltpu.VMEM((rows, half), BF), pltpu.VMEM((kept, half), BF), raw,
            pltpu.VMEM((half, cols), BF), SEMS((4,)), SEMS((steps,)), SEMS,
        ],
    )
    their_a, send_b = lax.optimization_barrier((their_a, send_b))
    their_b = across(send_b, 1)
    rows_dy, send_dh = call(
        functools.partial(project_kernel, cols),
        (shape(kept, half), shape(kept, hidden)),
        (scales[2], slot_of, got_dy, weights[2]),
        limit=LIMIT_DOWN,
        flops=2 * kept * half * hidden,
        moved=2 * half * hidden + 4 * rows * half,
        in_specs=[SMEM, VMEM, HBM, HBM],
        out_specs=[HBM, VMEM],
        scratch_shapes=[
            pltpu.VMEM((rows, half), BF), pltpu.VMEM((kept, half), BF), raw,
            pltpu.VMEM((half, cols), BF), SEMS((4,)), SEMS((steps,)), SEMS,
        ],
    )
    their_dh = across(send_dh, 1)
    chunk = 512
    parts = half // chunk
    factor, hid, both_w = call(
        functools.partial(factor_kernel, chunk),
        (shape(2, kept, hidden), shape(kept, hidden), shape(half, 2 * hidden)),
        (scales[0], scales[1], send_a, send_b, their_a, their_b, weights[0], weights[1]),
        limit=LIMIT_FACTOR,
        flops=16 * kept * hidden,
        moved=8 * half * hidden,
        in_specs=[SMEM, SMEM] + [VMEM] * 4 + [HBM, HBM],
        out_specs=[VMEM] * 3,
        scratch_shapes=[raw, raw, SEMS((parts,)), SEMS((parts,))],
    )
    d_ab, dx = call(
        functools.partial(backward_kernel, chunk),
        (shape(2, kept, hidden), shape(rows, wide)),
        (factor, hid, send_dh, their_dh, slot_of, both_w),
        limit=LIMIT_BACKWARD,
        flops=4 * rows * half * hidden,
        moved=4 * half * hidden + 2 * rows * half,
        in_specs=[HBM] + [VMEM] * 4 + [HBM],
        out_specs=[HBM, HBM],
        scratch_shapes=[
            pltpu.VMEM((2, kept, hidden), BF),
            pltpu.VMEM((2, kept, hidden), BF),
            pltpu.VMEM((rows, 2 * hidden), BF),
            pltpu.VMEM((kept, META), BF),
            pltpu.VMEM((half, 2 * hidden), BF),
            pltpu.VMEM((rows, wide), BF),
            SEMS((4,)),
            SEMS((parts,)),
            SEMS((parts,)),
            SEMS,
            SEMS,
        ],
    )
    returned = spread(dx)
    grads = [
        dot(left, right, ROWS).astype(BF)
        for left, right in ((rows_x, d_ab[0]), (rows_x, d_ab[1]), (rows_dy, hid))
    ]
    returned, *grads = lax.optimization_barrier((returned, *grads))
    blocks = call(
        functools.partial(combine_kernel, n_local, top),
        tuple(shape(tok, wide) for _ in range(n_group)),
        (returned, pick, column_meta),
        flops=2 * rows * column * half,
        limit=24,
        moved=2 * rows * half,
        in_specs=[VMEM] * 3,
        out_specs=[VMEM] * n_group,
    )
    back = [blocks[0]] + [across(blocks[m], m) for m in range(1, n_group)]
    grad_tokens, grad_gates = call(
        finish_kernel,
        (shape(tok, width), shape(top, tok)),
        tuple(back),
        limit=24,
        moved=tok * width * 6,
        grid=(1,),
        in_specs=[whole(tok, wide)] * 4,
        out_specs=[whole(tok, width), whole(top, tok)],
    )
    return (
        grad_tokens,
        grad_gates.T,
        grads[0][:, None, :],
        grads[1][:, None, :],
        grads[2][:, None, :],
    )


def solution(mesh):
    by_token = P(("group", "local"), None)
    by_expert = P("group", "local", None)
    return jax.shard_map(
        shards,
        mesh=mesh,
        in_specs=(by_token,) * 7 + (by_expert,) * 6,
        out_specs=(by_token,) * 2 + (by_expert,) * 3,
        check_vma=False,
    )
```

```python
import functools

import jax
import jax.numpy as jnp
from jax import lax
from jax.experimental import pallas as pl
from jax.experimental.pallas import tpu as pltpu
from jax.sharding import PartitionSpec as P

CAP = 192
META = 128
CODE, SLOT, GATE = 0, 8, 16
BF = jnp.bfloat16
F32 = jnp.float32
MIB = 1024 * 1024
LIMIT = 24
LIMIT_FACTOR = 52
LIMIT_FORWARD = 52
LIMIT_DOWN = 52
LIMIT_BACKWARD = 51

ROWS = (((0,), (0,)), ((), ()))
LAST = (((1,), (1,)), ((), ()))


def dot(left, right, dims=(((1,), (0,)), ((), ()))):
    return lax.dot_general(left, right, dims, preferred_element_type=F32)


def call(kernel, outs, args, limit, flops=0, moved=0, **kw):
    return pl.pallas_call(
        kernel,
        out_shape=outs,
        compiler_params=pltpu.CompilerParams(vmem_limit_bytes=limit * MIB),
        cost_estimate=pl.CostEstimate(flops=flops, bytes_accessed=moved, transcendentals=0),
        **kw,
    )(*args)


SMEM = pl.BlockSpec(memory_space=pltpu.SMEM)
VMEM = pl.BlockSpec(memory_space=pltpu.VMEM)
HBM = pl.BlockSpec(memory_space=pltpu.HBM)
SEMS = pltpu.SemaphoreType.DMA


def whole(*dims):
    return pl.BlockSpec(dims, lambda i: (0,) * len(dims))


def placed(source, offset):
    lane = lax.broadcasted_iota(jnp.int32, (source.shape[0], META), 1)
    row = lax.broadcasted_iota(jnp.int32, (source.shape[0], META), 0)
    return dot(source.astype(BF), jnp.where(lane == row + offset, 1.0, 0.0).astype(BF), ROWS)


def prepare_kernel(
    xq_ref, xs_ref, dy_ref, e_ref, r_ref, s_ref, g_ref, same_x, other_x, same_dy, other_dy
):
    half = xq_ref.shape[1] // 2
    blocks = half // 128
    first = lax.rem(lax.axis_index("group"), 2) == 0
    code = (1 + e_ref[...] + 64 * r_ref[...]).astype(F32)
    meta = placed(code, CODE) + placed(s_ref[...].astype(F32), SLOT) + placed(g_ref[...], GATE)
    same_x[:, half:] = meta.astype(BF)
    other_x[:, half:] = meta.astype(BF)
    for c in range(blocks):
        low, high = c * 128, half + c * 128
        x_low = (xq_ref[:, low : low + 128].astype(F32) * xs_ref[:, c : c + 1]).astype(BF)
        x_high = (
            xq_ref[:, high : high + 128].astype(F32) * xs_ref[:, blocks + c : blocks + c + 1]
        ).astype(BF)
        same_x[:, low : low + 128] = jnp.where(first, x_low, x_high)
        other_x[:, low : low + 128] = jnp.where(first, x_high, x_low)
    dy_low, dy_high = dy_ref[:, :half], dy_ref[:, half:]
    same_dy[...] = jnp.where(first, dy_low, dy_high)
    other_dy[...] = jnp.where(first, dy_high, dy_low)


def matches(meta, k, base, count):
    lane = lax.broadcasted_iota(jnp.int32, (meta.shape[0], count), 1).astype(F32)
    code = meta[:, CODE + k : CODE + k + 1] - base
    return (code == lane) | (code - 64.0 == lane)


def owner_of_row(rows, count, per, start=0):
    row = lax.broadcasted_iota(jnp.int32, (rows, count), 0) + start
    lane = lax.broadcasted_iota(jnp.int32, (rows, count), 1)
    return lax.div(row, per) == lane


def pack_x_kernel(
    n_local, top, per, b0, b1, b2, b3, out_hbm, pick_ref, gated_ref, meta_out, tokens, out, sems
):
    half = b0.shape[1] - META
    count = tokens.shape[0]
    block = b0.shape[0]
    for m, b in enumerate((b0, b1, b2, b3)):
        tokens[m * block : (m + 1) * block] = b[...]
    meta_out[...] = tokens[:, half:]
    lane = lax.broadcasted_iota(jnp.int32, (4 * top, META), 1)
    row = lax.broadcasted_iota(jnp.int32, (4 * top, META), 0)
    turn = jnp.where(lane == row, 1.0, 0.0).astype(BF)
    meta = dot(turn, tokens[:, half:], LAST)
    base = (1 + lax.div(lax.axis_index("group"), 2) * n_local).astype(F32)
    expert = lax.broadcasted_iota(jnp.int32, (n_local, count), 0).astype(F32) + base
    named = jnp.zeros((n_local, count), F32)
    gate = jnp.zeros((n_local, count), F32)
    for k in range(top):
        code = meta[CODE + k : CODE + k + 1]
        kept = meta[SLOT + k : SLOT + k + 1] < CAP
        hit = ((code == expert) | (code - 64.0 == expert)) & kept
        named = jnp.where(hit, 1.0, named)
        gate = jnp.where(hit, meta[GATE + k : GATE + k + 1], gate)
    row = lax.broadcasted_iota(jnp.int32, (count, count), 0)
    col = lax.broadcasted_iota(jnp.int32, (count, count), 1)
    before = jnp.where(row < col, 1.0, 0.0).astype(BF)
    rank = jnp.where(named > 0.0, dot(named.astype(BF), before), -1.0)
    position = lax.broadcasted_iota(jnp.int32, (per, count), 0).astype(F32)
    for j in range(n_local):
        at = slice(j * per, (j + 1) * per)
        hit = rank[j : j + 1] == position
        pick_ref[at] = jnp.where(hit, 1.0, 0.0).astype(BF)
        gated_ref[at] = jnp.where(hit, gate[j : j + 1], 0.0).astype(BF)
    multiply_out(pick_ref, tokens, out, out_hbm, sems)


def multiply_out(left, right, out, out_hbm, sems):
    parts = sems.shape[0]
    size = out.shape[0] // parts

    def copy(i):
        at = pl.ds(pl.multiple_of(i * size, size), size)
        return pltpu.make_async_copy(out.at[at], out_hbm.at[at], sems.at[i])

    def step(i, carry):
        at = pl.ds(pl.multiple_of(i * size, size), size)
        out[at] = dot(left[at], right[...]).astype(BF)
        copy(i).start()
        return carry

    lax.fori_loop(0, parts, step, 0)
    for i in range(parts):
        copy(i).wait()


def pack_dy_kernel(gated_ref, b0, b1, b2, b3, out_hbm, tokens, out, sems):
    block = b0.shape[0]
    for m, b in enumerate((b0, b1, b2, b3)):
        tokens[m * block : (m + 1) * block] = b[...]
    multiply_out(gated_ref, tokens, out, out_hbm, sems)


def dequant(quant_ref, scales_ref, out_ref, row, col):
    rows, cols = quant_ref.shape
    for c in range(cols // 128):
        for r in range(rows // 128):
            at = (slice(r * 128, (r + 1) * 128), slice(c * 128, (c + 1) * 128))
            factor = jnp.full((1, 16, 128), scales_ref[col + c, row + r], F32).astype(BF)
            out_ref[at] = (quant_ref[at].reshape(8, 16, 128) * factor).reshape(128, 128)


def columns(i, size):
    return (slice(None), pl.ds(pl.multiple_of(i * size, size), size))


def fetch(source, target, sems, i, size):
    at = columns(i, size)
    return pltpu.make_async_copy(source.at[at], target.at[at], sems.at[i])


def start_all(source, target, sems):
    for i in range(sems.shape[0]):
        fetch(source, target, sems, i, target.shape[1] // sems.shape[0]).start()


def compact(slot_ref, rows_hbm, rows_ref, sems, kept):
    size = kept.shape[1] // sems.shape[0]

    def step(i, carry):
        at = columns(i, size)
        fetch(rows_hbm, rows_ref, sems, i, size).wait()
        kept[at] = dot(slot_ref[...], rows_ref[at]).astype(BF)
        return carry

    lax.fori_loop(0, kept.shape[1] // size, step, 0)


def forward_kernel(
    n_local, top, cols, sg_ref, x_hbm, wg_hbm,
    send_ref, slot_ref, x_ref, meta_ref, kept, wg_raw, wg, sems_x, sems_g, sem_m,
):
    half, hidden = wg_raw.shape
    steps = hidden // cols
    tail = pltpu.make_async_copy(x_hbm.at[:, half:], meta_ref, sem_m)
    tail.start()
    start_all(x_hbm, x_ref, sems_x)
    for i in range(steps):
        fetch(wg_hbm, wg_raw, sems_g, i, cols).start()
    lane = lax.broadcasted_iota(jnp.int32, (2 * top, META), 1)
    row = lax.broadcasted_iota(jnp.int32, (2 * top, META), 0)
    turn = jnp.where(lane == row, 1.0, 0.0).astype(BF)
    tail.wait()
    meta = dot(turn, meta_ref[...], LAST)
    own = (
        1 + lax.div(lax.axis_index("group"), 2) * n_local + lax.axis_index("local")
    ).astype(F32)
    target = jnp.full((1, meta.shape[1]), -1.0, F32)
    for k in range(top):
        code = meta[CODE + k : CODE + k + 1]
        slot = meta[SLOT + k : SLOT + k + 1]
        target = jnp.where(code == own, slot, target)
        target = jnp.where(code == own + 64.0, slot + CAP, target)
    row = lax.broadcasted_iota(jnp.int32, slot_ref.shape, 0).astype(F32)
    slot_ref[...] = jnp.where(row == target, 1.0, 0.0).astype(BF)
    compact(slot_ref, x_hbm, x_ref, sems_x, kept)
    project(kept, wg_hbm, wg_raw, wg, sg_ref, sems_g, send_ref)


def project(kept, w_hbm, w_raw, w, scales_ref, sems, send_ref):
    cols = w.shape[1]

    def step(i, carry):
        at = columns(i, cols)
        fetch(w_hbm, w_raw, sems, i, cols).wait()
        dequant(w_raw.at[at], scales_ref, w, 0, i * (cols // 128))
        send_ref[at] = dot(kept[...], w[...]).astype(BF)
        return carry

    lax.fori_loop(0, sems.shape[0], step, 0)


def project_kernel(
    cols, sv_ref, slot_ref, dy_hbm, v_hbm, kept_hbm, send_ref,
    dy_ref, kept, v_raw, v, sems_y, sems_v, sem_k,
):
    half, hidden = v_raw.shape
    steps = hidden // cols
    start_all(dy_hbm, dy_ref, sems_y)
    for i in range(steps):
        fetch(v_hbm, v_raw, sems_v, i, cols).start()
    compact(slot_ref, dy_hbm, dy_ref, sems_y, kept)
    save = pltpu.make_async_copy(kept, kept_hbm, sem_k)
    save.start()

    project(kept, v_hbm, v_raw, v, sv_ref, sems_v, send_ref)
    save.wait()


def factor_kernel(
    chunk, sg_ref, su_ref, a_ref, b_ref, a_in, b_in, wg_hbm, wu_hbm,
    factor_ref, hid_ref, both_w, wg_raw, wu_raw, sems_g, sems_u,
):
    half, hidden = wg_raw.shape
    parts = half // chunk
    block = 64

    def load(source, target, sems, i):
        at = pl.ds(pl.multiple_of(i * chunk, chunk), chunk)
        return pltpu.make_async_copy(source.at[at], target.at[at], sems.at[i])

    for i in range(parts):
        load(wg_hbm, wg_raw, sems_g, i).start()
        load(wu_hbm, wu_raw, sems_u, i).start()

    def activate(i, carry):
        at = pl.ds(pl.multiple_of(i * block, block), block)
        act_a = a_ref[at].astype(F32) + a_in[at].astype(F32)
        act_b = b_ref[at].astype(F32) + b_in[at].astype(F32)
        sigma = jax.nn.sigmoid(act_a)
        silu_a = act_a * sigma
        hid_ref[at] = (silu_a * act_b).astype(BF)
        factor_ref[0, at] = (act_b * sigma * (1.0 + act_a * (1.0 - sigma))).astype(BF)
        factor_ref[1, at] = silu_a.astype(BF)
        return carry

    lax.fori_loop(0, hid_ref.shape[0] // block, activate, 0)

    def step(i, carry):
        at = pl.ds(pl.multiple_of(i * chunk, chunk), chunk)
        load(wg_hbm, wg_raw, sems_g, i).wait()
        load(wu_hbm, wu_raw, sems_u, i).wait()
        dequant(wg_raw.at[at], sg_ref, both_w.at[at, :hidden], i * (chunk // 128), 0)
        dequant(wu_raw.at[at], su_ref, both_w.at[at, hidden:], i * (chunk // 128), 0)
        return carry

    lax.fori_loop(0, parts, step, 0)


def backward_kernel(
    chunk, factor_ref, hid_ref, dh_ref, dh_in, slot_ref, w_hbm,
    d_hbm, dx_hbm, d_ab, wide, pairs, both_w, dx, sems_w, sems_x, sem_d, sem_m,
):
    kept, hidden = hid_ref.shape
    half = both_w.shape[0]
    parts = half // chunk
    block = 64

    def load(i):
        at = pl.ds(pl.multiple_of(i * chunk, chunk), chunk)
        return pltpu.make_async_copy(w_hbm.at[at], both_w.at[at], sems_w.at[i])

    for i in range(parts):
        load(i).start()

    def activate(i, carry):
        at = pl.ds(pl.multiple_of(i * block, block), block)
        d_hidden = dh_ref[at].astype(F32) + dh_in[at].astype(F32)
        d_ab[0, at] = (d_hidden * factor_ref[0, at].astype(F32)).astype(BF)
        d_ab[1, at] = (d_hidden * factor_ref[1, at].astype(F32)).astype(BF)
        grad = jnp.sum(hid_ref[at].astype(F32) * d_hidden, axis=1, keepdims=True)
        high = grad.astype(BF).astype(F32)
        lane = lax.broadcasted_iota(jnp.int32, (block, META), 1)
        pair = jnp.where(lane == 0, high, jnp.where(lane == 1, grad - high, 0.0))
        pairs[at] = pair.astype(BF)
        return carry

    lax.fori_loop(0, kept // block, activate, 0)
    save = pltpu.make_async_copy(d_ab, d_hbm, sem_d)
    save.start()

    def widen(i, carry):
        wide[columns(i, hidden)] = dot(slot_ref[...], d_ab[i], ROWS).astype(BF)
        return carry

    lax.fori_loop(0, 2, widen, 0)
    dx[:, half:] = dot(slot_ref[...], pairs[...], ROWS).astype(BF)
    tail = pltpu.make_async_copy(dx.at[:, half:], dx_hbm.at[:, half:], sem_m)
    tail.start()

    def step(i, carry):
        at = pl.ds(pl.multiple_of(i * chunk, chunk), chunk)
        load(i).wait()
        dx[columns(i, chunk)] = dot(wide[...], both_w[at], LAST).astype(BF)
        fetch(dx, dx_hbm, sems_x, i, chunk).start()
        return carry

    lax.fori_loop(0, parts, step, 0)
    for i in range(parts):
        fetch(dx, dx_hbm, sems_x, i, chunk).wait()
    tail.wait()
    save.wait()


def combine_kernel(n_local, top, ret_ref, pick_ref, meta_ref, *outs):
    width = ret_ref.shape[1] - META
    pick = pick_ref[...]
    meta = meta_ref[...].astype(F32)
    total = dot(pick, ret_ref[:, :width], ROWS).astype(BF)
    rows = ret_ref.shape[0]
    owner = owner_of_row(rows, n_local, rows // n_local)
    grads = ret_ref[:, width:].astype(F32)
    high = jnp.where(owner, grads[:, 0:1], 0.0).astype(BF)
    low = jnp.where(owner, grads[:, 1:2], 0.0).astype(BF)
    by_expert = dot(pick, high, ROWS) + dot(pick, low, ROWS)
    base = (1 + lax.div(lax.axis_index("group"), 2) * n_local).astype(F32)
    lane = lax.broadcasted_iota(jnp.int32, meta.shape, 1)
    tail = jnp.zeros(meta.shape, F32)
    for k in range(top):
        hit = matches(meta, k, base, n_local) & (meta[:, SLOT + k : SLOT + k + 1] < CAP)
        value = jnp.sum(jnp.where(hit, by_expert, 0.0), axis=1, keepdims=True)
        tail = jnp.where(lane == k, value / meta[:, GATE + k : GATE + k + 1], tail)
    tail = tail.astype(BF)
    block = outs[0].shape[0]
    for m, out in enumerate(outs):
        out[:, :width] = total[m * block : (m + 1) * block]
        out[:, width:] = tail[m * block : (m + 1) * block]


def finish_kernel(b0, b1, b2, b3, tokens_ref, gates_ref):
    half = tokens_ref.shape[1] // 2
    first = lax.rem(lax.axis_index("group"), 2) == 0
    own = b0[...].astype(F32) + b2[...].astype(F32)
    other = b1[:, :half].astype(F32) + b3[:, :half].astype(F32)
    mine = own[:, :half]
    tokens_ref[:, :half] = jnp.where(first, mine, other).astype(BF)
    tokens_ref[:, half:] = jnp.where(first, other, mine).astype(BF)
    lane = lax.broadcasted_iota(jnp.int32, (gates_ref.shape[0], META), 1)
    row = lax.broadcasted_iota(jnp.int32, (gates_ref.shape[0], META), 0)
    turn = jnp.where(lane == row, 1.0, 0.0).astype(BF)
    gates_ref[...] = dot(turn, own[:, half:].astype(BF), LAST).astype(BF)


def shape(*dims, dtype=BF):
    return jax.ShapeDtypeStruct(dims, dtype)


def shards(
    x_q,
    x_scale,
    cotangent,
    gates,
    experts,
    replicas,
    slots,
    w_gate_q,
    w_up_q,
    w_down_q,
    gate_scales,
    up_scales,
    down_scales,
):
    n_group = lax.axis_size("group")
    n_local = lax.axis_size("local")
    tok, width = x_q.shape
    top = experts.shape[1]
    half = width // 2
    hidden = w_gate_q.shape[2]
    column = n_group * tok
    rows = n_local * n_group * 4
    kept = 2 * CAP
    wide = half + META

    def across(block, apart):
        return lax.ppermute(block, "group", [(i, i ^ apart) for i in range(n_group)])

    def spread(block):
        return lax.all_to_all(block, "local", split_axis=0, concat_axis=0, tiled=True)

    same_x, other_x, same_dy, other_dy = call(
        prepare_kernel,
        (shape(tok, wide), shape(tok, wide), shape(tok, half), shape(tok, half)),
        (x_q, x_scale, cotangent, experts.T, replicas.T, slots.T, gates.T),
        limit=63,
        moved=tok * width * 8,
        grid=(1,),
        in_specs=[whole(tok, width), whole(*x_scale.shape), whole(tok, width)]
        + [whole(top, tok)] * 4,
        out_specs=[whole(tok, wide)] * 2 + [whole(tok, half)] * 2,
    )
    near_x = [same_x, across(other_x, 1), across(same_x, 2), across(other_x, 3)]
    near_dy = [same_dy, across(other_dy, 1), across(same_dy, 2), across(other_dy, 3)]
    packed_x, pick, gated, column_meta = call(
        functools.partial(pack_x_kernel, n_local, top, rows // n_local),
        (shape(rows, wide), shape(rows, column), shape(rows, column), shape(column, META)),
        tuple(near_x),
        limit=LIMIT,
        flops=2 * rows * column * wide,
        moved=2 * rows * wide,
        in_specs=[VMEM] * 4,
        out_specs=[HBM] + [VMEM] * 3,
        scratch_shapes=[pltpu.VMEM((column, wide), BF), pltpu.VMEM((rows, wide), BF), SEMS((4,))],
    )
    packed_dy = call(
        pack_dy_kernel,
        shape(rows, half),
        (gated, *near_dy),
        limit=LIMIT,
        flops=2 * rows * column * half,
        moved=2 * rows * half,
        in_specs=[VMEM] * 5,
        out_specs=HBM,
        scratch_shapes=[pltpu.VMEM((column, half), BF), pltpu.VMEM((rows, half), BF), SEMS((4,))],
    )
    got_x = spread(packed_x)
    got_x, packed_dy = lax.optimization_barrier((got_x, packed_dy))
    got_dy = spread(packed_dy)

    weights = [w[:, 0, :] for w in (w_gate_q, w_up_q, w_down_q)]
    scales = [s[:, 0, :].T for s in (gate_scales, up_scales, down_scales)]
    cols = 256
    steps = hidden // cols
    raw = pltpu.VMEM((half, hidden), BF)
    send_a, slot_of = call(
        functools.partial(forward_kernel, n_local, top, cols),
        (shape(kept, hidden), shape(kept, rows)),
        (scales[0], got_x, weights[0]),
        limit=LIMIT_FORWARD,
        flops=2 * kept * half * hidden,
        moved=2 * half * hidden + 4 * rows * half,
        in_specs=[SMEM, HBM, HBM],
        out_specs=[VMEM, VMEM],
        scratch_shapes=[pltpu.VMEM((rows, half), BF), pltpu.VMEM((rows, META), BF)]
        + [pltpu.VMEM((kept, half), BF), raw, pltpu.VMEM((half, cols), BF)]
        + [SEMS((4,)), SEMS((steps,)), SEMS],
    )
    their_a = across(send_a, 1)
    rows_x, send_b = call(
        functools.partial(project_kernel, cols),
        (shape(kept, half), shape(kept, hidden)),
        (scales[1], slot_of, got_x, weights[1]),
        limit=LIMIT_DOWN,
        flops=2 * kept * half * hidden,
        moved=2 * half * hidden + 4 * rows * half,
        in_specs=[SMEM, VMEM, HBM, HBM],
        out_specs=[HBM, VMEM],
        scratch_shapes=[
            pltpu.VMEM((rows, half), BF), pltpu.VMEM((kept, half), BF), raw,
            pltpu.VMEM((half, cols), BF), SEMS((4,)), SEMS((steps,)), SEMS,
        ],
    )
    their_a, send_b = lax.optimization_barrier((their_a, send_b))
    their_b = across(send_b, 1)
    rows_dy, send_dh = call(
        functools.partial(project_kernel, cols),
        (shape(kept, half), shape(kept, hidden)),
        (scales[2], slot_of, got_dy, weights[2]),
        limit=LIMIT_DOWN,
        flops=2 * kept * half * hidden,
        moved=2 * half * hidden + 4 * rows * half,
        in_specs=[SMEM, VMEM, HBM, HBM],
        out_specs=[HBM, VMEM],
        scratch_shapes=[
            pltpu.VMEM((rows, half), BF), pltpu.VMEM((kept, half), BF), raw,
            pltpu.VMEM((half, cols), BF), SEMS((4,)), SEMS((steps,)), SEMS,
        ],
    )
    their_dh = across(send_dh, 1)
    chunk = 512
    parts = half // chunk
    factor, hid, both_w = call(
        functools.partial(factor_kernel, chunk),
        (shape(2, kept, hidden), shape(kept, hidden), shape(half, 2 * hidden)),
        (scales[0], scales[1], send_a, send_b, their_a, their_b, weights[0], weights[1]),
        limit=LIMIT_FACTOR,
        flops=16 * kept * hidden,
        moved=8 * half * hidden,
        in_specs=[SMEM, SMEM] + [VMEM] * 4 + [HBM, HBM],
        out_specs=[VMEM] * 3,
        scratch_shapes=[raw, raw, SEMS((parts,)), SEMS((parts,))],
    )
    d_ab, dx = call(
        functools.partial(backward_kernel, chunk),
        (shape(2, kept, hidden), shape(rows, wide)),
        (factor, hid, send_dh, their_dh, slot_of, both_w),
        limit=LIMIT_BACKWARD,
        flops=4 * rows * half * hidden,
        moved=4 * half * hidden + 2 * rows * half,
        in_specs=[VMEM] * 5 + [HBM],
        out_specs=[HBM, HBM],
        scratch_shapes=[
            pltpu.VMEM((2, kept, hidden), BF),
            pltpu.VMEM((rows, 2 * hidden), BF),
            pltpu.VMEM((kept, META), BF),
            pltpu.VMEM((half, 2 * hidden), BF),
            pltpu.VMEM((rows, wide), BF),
            SEMS((parts,)),
            SEMS((parts,)),
            SEMS,
            SEMS,
        ],
    )
    returned = spread(dx)
    grads = [
        dot(left, right, ROWS).astype(BF)
        for left, right in ((rows_x, d_ab[0]), (rows_x, d_ab[1]), (rows_dy, hid))
    ]
    returned, *grads = lax.optimization_barrier((returned, *grads))
    blocks = call(
        functools.partial(combine_kernel, n_local, top),
        tuple(shape(tok, wide) for _ in range(n_group)),
        (returned, pick, column_meta),
        flops=2 * rows * column * half,
        limit=24,
        moved=2 * rows * half,
        in_specs=[VMEM] * 3,
        out_specs=[VMEM] * n_group,
    )
    back = [blocks[0]] + [across(blocks[m], m) for m in range(1, n_group)]
    grad_tokens, grad_gates = call(
        finish_kernel,
        (shape(tok, width), shape(top, tok)),
        tuple(back),
        limit=24,
        moved=tok * width * 6,
        grid=(1,),
        in_specs=[whole(tok, wide)] * 4,
        out_specs=[whole(tok, width), whole(top, tok)],
    )
    return (
        grad_tokens,
        grad_gates.T,
        grads[0][:, None, :],
        grads[1][:, None, :],
        grads[2][:, None, :],
    )


def solution(mesh):
    by_token = P(("group", "local"), None)
    by_expert = P("group", "local", None)
    return jax.shard_map(
        shards,
        mesh=mesh,
        in_specs=(by_token,) * 7 + (by_expert,) * 6,
        out_specs=(by_token,) * 2 + (by_expert,) * 3,
        check_vma=False,
    )
```

```python
import functools

import jax
import jax.numpy as jnp
from jax import lax
from jax.experimental import pallas as pl
from jax.experimental.pallas import tpu as pltpu
from jax.sharding import PartitionSpec as P

CAP = 192
META = 128
CODE, SLOT, GATE = 0, 8, 16
BF = jnp.bfloat16
F32 = jnp.float32
MIB = 1024 * 1024
LIMIT = 24
LIMIT_FACTOR = 52
LIMIT_FORWARD = 52
LIMIT_DOWN = 52
LIMIT_BACKWARD = 51

ROWS = (((0,), (0,)), ((), ()))
LAST = (((1,), (1,)), ((), ()))


def dot(left, right, dims=(((1,), (0,)), ((), ()))):
    return lax.dot_general(left, right, dims, preferred_element_type=F32)


def call(kernel, outs, args, limit, flops=0, moved=0, **kw):
    return pl.pallas_call(
        kernel,
        out_shape=outs,
        compiler_params=pltpu.CompilerParams(vmem_limit_bytes=limit * MIB),
        cost_estimate=pl.CostEstimate(flops=flops, bytes_accessed=moved, transcendentals=0),
        **kw,
    )(*args)


SMEM = pl.BlockSpec(memory_space=pltpu.SMEM)
VMEM = pl.BlockSpec(memory_space=pltpu.VMEM)
HBM = pl.BlockSpec(memory_space=pltpu.HBM)
SEMS = pltpu.SemaphoreType.DMA


def whole(*dims):
    return pl.BlockSpec(dims, lambda i: (0,) * len(dims))


def placed(source, offset):
    lane = lax.broadcasted_iota(jnp.int32, (source.shape[0], META), 1)
    row = lax.broadcasted_iota(jnp.int32, (source.shape[0], META), 0)
    return dot(source.astype(BF), jnp.where(lane == row + offset, 1.0, 0.0).astype(BF), ROWS)


def prepare_kernel(
    xq_ref, xs_ref, dy_ref, e_ref, r_ref, s_ref, g_ref, same_x, other_x, same_dy, other_dy
):
    half = xq_ref.shape[1] // 2
    blocks = half // 128
    first = lax.rem(lax.axis_index("group"), 2) == 0
    code = (1 + e_ref[...] + 64 * r_ref[...]).astype(F32)
    meta = placed(code, CODE) + placed(s_ref[...].astype(F32), SLOT) + placed(g_ref[...], GATE)
    same_x[:, half:] = meta.astype(BF)
    other_x[:, half:] = meta.astype(BF)
    for c in range(blocks):
        low, high = c * 128, half + c * 128
        x_low = (xq_ref[:, low : low + 128].astype(F32) * xs_ref[:, c : c + 1]).astype(BF)
        x_high = (
            xq_ref[:, high : high + 128].astype(F32) * xs_ref[:, blocks + c : blocks + c + 1]
        ).astype(BF)
        same_x[:, low : low + 128] = jnp.where(first, x_low, x_high)
        other_x[:, low : low + 128] = jnp.where(first, x_high, x_low)
    dy_low, dy_high = dy_ref[:, :half], dy_ref[:, half:]
    same_dy[...] = jnp.where(first, dy_low, dy_high)
    other_dy[...] = jnp.where(first, dy_high, dy_low)


def matches(meta, k, base, count):
    lane = lax.broadcasted_iota(jnp.int32, (meta.shape[0], count), 1).astype(F32)
    code = meta[:, CODE + k : CODE + k + 1] - base
    return (code == lane) | (code - 64.0 == lane)


def owner_of_row(rows, count, per, start=0):
    row = lax.broadcasted_iota(jnp.int32, (rows, count), 0) + start
    lane = lax.broadcasted_iota(jnp.int32, (rows, count), 1)
    return lax.div(row, per) == lane


def pack_x_kernel(
    n_local, top, per, b0, b1, b2, b3, out_hbm, pick_ref, gated_ref, meta_out, tokens, out, sems
):
    half = b0.shape[1] - META
    count = tokens.shape[0]
    block = b0.shape[0]
    for m, b in enumerate((b0, b1, b2, b3)):
        tokens[m * block : (m + 1) * block] = b[...]
    meta_out[...] = tokens[:, half:]
    lane = lax.broadcasted_iota(jnp.int32, (4 * top, META), 1)
    row = lax.broadcasted_iota(jnp.int32, (4 * top, META), 0)
    turn = jnp.where(lane == row, 1.0, 0.0).astype(BF)
    meta = dot(turn, tokens[:, half:], LAST)
    base = (1 + lax.div(lax.axis_index("group"), 2) * n_local).astype(F32)
    expert = lax.broadcasted_iota(jnp.int32, (n_local, count), 0).astype(F32) + base
    named = jnp.zeros((n_local, count), F32)
    gate = jnp.zeros((n_local, count), F32)
    for k in range(top):
        code = meta[CODE + k : CODE + k + 1]
        kept = meta[SLOT + k : SLOT + k + 1] < CAP
        hit = ((code == expert) | (code - 64.0 == expert)) & kept
        named = jnp.where(hit, 1.0, named)
        gate = jnp.where(hit, meta[GATE + k : GATE + k + 1], gate)
    row = lax.broadcasted_iota(jnp.int32, (count, count), 0)
    col = lax.broadcasted_iota(jnp.int32, (count, count), 1)
    before = jnp.where(row < col, 1.0, 0.0).astype(BF)
    rank = jnp.where(named > 0.0, dot(named.astype(BF), before), -1.0)
    position = lax.broadcasted_iota(jnp.int32, (per, count), 0).astype(F32)
    for j in range(n_local):
        at = slice(j * per, (j + 1) * per)
        hit = rank[j : j + 1] == position
        pick_ref[at] = jnp.where(hit, 1.0, 0.0).astype(BF)
        gated_ref[at] = jnp.where(hit, gate[j : j + 1], 0.0).astype(BF)
    multiply_out(pick_ref, tokens, out, out_hbm, sems)


def multiply_out(left, right, out, out_hbm, sems):
    parts = sems.shape[0]
    size = out.shape[0] // parts

    def copy(i):
        at = pl.ds(pl.multiple_of(i * size, size), size)
        return pltpu.make_async_copy(out.at[at], out_hbm.at[at], sems.at[i])

    def step(i, carry):
        at = pl.ds(pl.multiple_of(i * size, size), size)
        out[at] = dot(left[at], right[...]).astype(BF)
        copy(i).start()
        return carry

    lax.fori_loop(0, parts, step, 0)
    for i in range(parts):
        copy(i).wait()


def pack_dy_kernel(gated_ref, b0, b1, b2, b3, out_hbm, tokens, out, sems):
    block = b0.shape[0]
    for m, b in enumerate((b0, b1, b2, b3)):
        tokens[m * block : (m + 1) * block] = b[...]
    multiply_out(gated_ref, tokens, out, out_hbm, sems)


def dequant(quant_ref, scales_ref, out_ref, row, col):
    rows, cols = quant_ref.shape
    for c in range(cols // 128):
        for r in range(rows // 128):
            at = (slice(r * 128, (r + 1) * 128), slice(c * 128, (c + 1) * 128))
            factor = jnp.full((1, 16, 128), scales_ref[col + c, row + r], F32).astype(BF)
            out_ref[at] = (quant_ref[at].reshape(8, 16, 128) * factor).reshape(128, 128)


def columns(i, size):
    return (slice(None), pl.ds(pl.multiple_of(i * size, size), size))


def fetch(source, target, sems, i, size):
    at = columns(i, size)
    return pltpu.make_async_copy(source.at[at], target.at[at], sems.at[i])


def start_all(source, target, sems):
    for i in range(sems.shape[0]):
        fetch(source, target, sems, i, target.shape[1] // sems.shape[0]).start()


def compact(slot_ref, rows_hbm, rows_ref, sems, kept):
    size = kept.shape[1] // sems.shape[0]

    def step(i, carry):
        at = columns(i, size)
        fetch(rows_hbm, rows_ref, sems, i, size).wait()
        kept[at] = dot(slot_ref[...], rows_ref[at]).astype(BF)
        return carry

    lax.fori_loop(0, kept.shape[1] // size, step, 0)


def forward_kernel(
    n_local, top, cols, sg_ref, x_hbm, wg_hbm,
    send_ref, slot_ref, x_ref, meta_ref, kept, wg_raw, wg, sems_x, sems_g, sem_m,
):
    half, hidden = wg_raw.shape
    steps = hidden // cols
    tail = pltpu.make_async_copy(x_hbm.at[:, half:], meta_ref, sem_m)
    tail.start()
    start_all(x_hbm, x_ref, sems_x)
    for i in range(steps):
        fetch(wg_hbm, wg_raw, sems_g, i, cols).start()
    lane = lax.broadcasted_iota(jnp.int32, (2 * top, META), 1)
    row = lax.broadcasted_iota(jnp.int32, (2 * top, META), 0)
    turn = jnp.where(lane == row, 1.0, 0.0).astype(BF)
    tail.wait()
    meta = dot(turn, meta_ref[...], LAST)
    own = (
        1 + lax.div(lax.axis_index("group"), 2) * n_local + lax.axis_index("local")
    ).astype(F32)
    target = jnp.full((1, meta.shape[1]), -1.0, F32)
    for k in range(top):
        code = meta[CODE + k : CODE + k + 1]
        slot = meta[SLOT + k : SLOT + k + 1]
        target = jnp.where(code == own, slot, target)
        target = jnp.where(code == own + 64.0, slot + CAP, target)
    row = lax.broadcasted_iota(jnp.int32, slot_ref.shape, 0).astype(F32)
    slot_ref[...] = jnp.where(row == target, 1.0, 0.0).astype(BF)
    compact(slot_ref, x_hbm, x_ref, sems_x, kept)
    project(kept, wg_hbm, wg_raw, wg, sg_ref, sems_g, send_ref)


def project(kept, w_hbm, w_raw, w, scales_ref, sems, send_ref):
    cols = w.shape[1]

    def step(i, carry):
        at = columns(i, cols)
        fetch(w_hbm, w_raw, sems, i, cols).wait()
        dequant(w_raw.at[at], scales_ref, w, 0, i * (cols // 128))
        send_ref[at] = dot(kept[...], w[...]).astype(BF)
        return carry

    lax.fori_loop(0, sems.shape[0], step, 0)


def project_kernel(
    cols, sv_ref, slot_ref, dy_hbm, v_hbm, kept_hbm, send_ref,
    dy_ref, kept, v_raw, v, sems_y, sems_v, sem_k,
):
    half, hidden = v_raw.shape
    steps = hidden // cols
    start_all(dy_hbm, dy_ref, sems_y)
    for i in range(steps):
        fetch(v_hbm, v_raw, sems_v, i, cols).start()
    compact(slot_ref, dy_hbm, dy_ref, sems_y, kept)
    save = pltpu.make_async_copy(kept, kept_hbm, sem_k)
    save.start()

    project(kept, v_hbm, v_raw, v, sv_ref, sems_v, send_ref)
    save.wait()


def factor_kernel(
    chunk, sg_ref, su_ref, a_ref, b_ref, a_in, b_in, wg_hbm, wu_hbm,
    factor_ref, hid_ref, both_w, wg_raw, wu_raw, sems_g, sems_u,
):
    half, hidden = wg_raw.shape
    parts = half // chunk
    block = 64

    def load(source, target, sems, i):
        at = pl.ds(pl.multiple_of(i * chunk, chunk), chunk)
        return pltpu.make_async_copy(source.at[at], target.at[at], sems.at[i])

    for i in range(parts):
        load(wg_hbm, wg_raw, sems_g, i).start()
        load(wu_hbm, wu_raw, sems_u, i).start()

    def activate(i, carry):
        at = pl.ds(pl.multiple_of(i * block, block), block)
        act_a = a_ref[at].astype(F32) + a_in[at].astype(F32)
        act_b = b_ref[at].astype(F32) + b_in[at].astype(F32)
        sigma = jax.nn.sigmoid(act_a)
        silu_a = act_a * sigma
        hid_ref[at] = (silu_a * act_b).astype(BF)
        factor_ref[0, at] = (act_b * sigma * (1.0 + act_a * (1.0 - sigma))).astype(BF)
        factor_ref[1, at] = silu_a.astype(BF)
        return carry

    lax.fori_loop(0, hid_ref.shape[0] // block, activate, 0)

    def step(i, carry):
        at = pl.ds(pl.multiple_of(i * chunk, chunk), chunk)
        load(wg_hbm, wg_raw, sems_g, i).wait()
        load(wu_hbm, wu_raw, sems_u, i).wait()
        dequant(wg_raw.at[at], sg_ref, both_w.at[at, :hidden], i * (chunk // 128), 0)
        dequant(wu_raw.at[at], su_ref, both_w.at[at, hidden:], i * (chunk // 128), 0)
        return carry

    lax.fori_loop(0, parts, step, 0)


def backward_kernel(
    chunk, factor_ref, hid_ref, dh_ref, dh_in, slot_ref, w_hbm,
    d_hbm, dx_hbm, d_ab, wide, pairs, both_w, dx, sems_w, sems_x, sem_d, sem_m,
):
    kept, hidden = hid_ref.shape
    half = both_w.shape[0]
    parts = half // chunk
    block = 64

    def load(i):
        at = pl.ds(pl.multiple_of(i * chunk, chunk), chunk)
        return pltpu.make_async_copy(w_hbm.at[at], both_w.at[at], sems_w.at[i])

    for i in range(parts):
        load(i).start()

    def activate(i, carry):
        at = pl.ds(pl.multiple_of(i * block, block), block)
        d_hidden = dh_ref[at].astype(F32) + dh_in[at].astype(F32)
        d_ab[0, at] = (d_hidden * factor_ref[0, at].astype(F32)).astype(BF)
        d_ab[1, at] = (d_hidden * factor_ref[1, at].astype(F32)).astype(BF)
        grad = jnp.sum(hid_ref[at].astype(F32) * d_hidden, axis=1, keepdims=True)
        high = grad.astype(BF).astype(F32)
        lane = lax.broadcasted_iota(jnp.int32, (block, META), 1)
        pair = jnp.where(lane == 0, high, jnp.where(lane == 1, grad - high, 0.0))
        pairs[at] = pair.astype(BF)
        return carry

    lax.fori_loop(0, kept // block, activate, 0)
    save = pltpu.make_async_copy(d_ab, d_hbm, sem_d)
    save.start()

    def widen(i, carry):
        wide[columns(i, hidden)] = dot(slot_ref[...], d_ab[i], ROWS).astype(BF)
        return carry

    lax.fori_loop(0, 2, widen, 0)
    dx[:, half:] = dot(slot_ref[...], pairs[...], ROWS).astype(BF)
    tail = pltpu.make_async_copy(dx.at[:, half:], dx_hbm.at[:, half:], sem_m)
    tail.start()

    def step(i, carry):
        at = pl.ds(pl.multiple_of(i * chunk, chunk), chunk)
        load(i).wait()
        dx[columns(i, chunk)] = dot(wide[...], both_w[at], LAST).astype(BF)
        fetch(dx, dx_hbm, sems_x, i, chunk).start()
        return carry

    lax.fori_loop(0, parts, step, 0)
    for i in range(parts):
        fetch(dx, dx_hbm, sems_x, i, chunk).wait()
    tail.wait()
    save.wait()


def combine_kernel(n_local, top, ret_ref, pick_ref, meta_ref, *outs):
    width = ret_ref.shape[1] - META
    pick = pick_ref[...]
    meta = meta_ref[...].astype(F32)
    total = dot(pick, ret_ref[:, :width], ROWS).astype(BF)
    rows = ret_ref.shape[0]
    owner = owner_of_row(rows, n_local, rows // n_local)
    grads = ret_ref[:, width:].astype(F32)
    high = jnp.where(owner, grads[:, 0:1], 0.0).astype(BF)
    low = jnp.where(owner, grads[:, 1:2], 0.0).astype(BF)
    by_expert = dot(pick, high, ROWS) + dot(pick, low, ROWS)
    base = (1 + lax.div(lax.axis_index("group"), 2) * n_local).astype(F32)
    lane = lax.broadcasted_iota(jnp.int32, meta.shape, 1)
    tail = jnp.zeros(meta.shape, F32)
    for k in range(top):
        hit = matches(meta, k, base, n_local) & (meta[:, SLOT + k : SLOT + k + 1] < CAP)
        value = jnp.sum(jnp.where(hit, by_expert, 0.0), axis=1, keepdims=True)
        tail = jnp.where(lane == k, value / meta[:, GATE + k : GATE + k + 1], tail)
    tail = tail.astype(BF)
    block = outs[0].shape[0]
    for m, out in enumerate(outs):
        out[:, :width] = total[m * block : (m + 1) * block]
        out[:, width:] = tail[m * block : (m + 1) * block]


def finish_kernel(b0, b1, b2, b3, tokens_ref, gates_ref):
    half = tokens_ref.shape[1] // 2
    first = lax.rem(lax.axis_index("group"), 2) == 0
    own = b0[...].astype(F32) + b2[...].astype(F32)
    other = b1[:, :half].astype(F32) + b3[:, :half].astype(F32)
    mine = own[:, :half]
    tokens_ref[:, :half] = jnp.where(first, mine, other).astype(BF)
    tokens_ref[:, half:] = jnp.where(first, other, mine).astype(BF)
    lane = lax.broadcasted_iota(jnp.int32, (gates_ref.shape[0], META), 1)
    row = lax.broadcasted_iota(jnp.int32, (gates_ref.shape[0], META), 0)
    turn = jnp.where(lane == row, 1.0, 0.0).astype(BF)
    gates_ref[...] = dot(turn, own[:, half:].astype(BF), LAST).astype(BF)


def shape(*dims, dtype=BF):
    return jax.ShapeDtypeStruct(dims, dtype)


def shards(
    x_q,
    x_scale,
    cotangent,
    gates,
    experts,
    replicas,
    slots,
    w_gate_q,
    w_up_q,
    w_down_q,
    gate_scales,
    up_scales,
    down_scales,
):
    n_group = lax.axis_size("group")
    n_local = lax.axis_size("local")
    tok, width = x_q.shape
    top = experts.shape[1]
    half = width // 2
    hidden = w_gate_q.shape[2]
    column = n_group * tok
    rows = n_local * n_group * 4
    kept = 2 * CAP
    wide = half + META

    def across(block, apart):
        return lax.ppermute(block, "group", [(i, i ^ apart) for i in range(n_group)])

    def spread(block):
        return lax.all_to_all(block, "local", split_axis=0, concat_axis=0, tiled=True)

    same_x, other_x, same_dy, other_dy = call(
        prepare_kernel,
        (shape(tok, wide), shape(tok, wide), shape(tok, half), shape(tok, half)),
        (x_q, x_scale, cotangent, experts.T, replicas.T, slots.T, gates.T),
        limit=63,
        moved=tok * width * 8,
        grid=(1,),
        in_specs=[whole(tok, width), whole(*x_scale.shape), whole(tok, width)]
        + [whole(top, tok)] * 4,
        out_specs=[whole(tok, wide)] * 2 + [whole(tok, half)] * 2,
    )
    near_x = [same_x, across(other_x, 1), across(same_x, 2), across(other_x, 3)]
    near_dy = [same_dy, across(other_dy, 1), across(same_dy, 2), across(other_dy, 3)]
    packed_x, pick, gated, column_meta = call(
        functools.partial(pack_x_kernel, n_local, top, rows // n_local),
        (shape(rows, wide), shape(rows, column), shape(rows, column), shape(column, META)),
        tuple(near_x),
        limit=LIMIT,
        flops=2 * rows * column * wide,
        moved=2 * rows * wide,
        in_specs=[VMEM] * 4,
        out_specs=[HBM] + [VMEM] * 3,
        scratch_shapes=[pltpu.VMEM((column, wide), BF), pltpu.VMEM((rows, wide), BF), SEMS((4,))],
    )
    packed_dy = call(
        pack_dy_kernel,
        shape(rows, half),
        (gated, *near_dy),
        limit=LIMIT,
        flops=2 * rows * column * half,
        moved=2 * rows * half,
        in_specs=[VMEM] * 5,
        out_specs=HBM,
        scratch_shapes=[pltpu.VMEM((column, half), BF), pltpu.VMEM((rows, half), BF), SEMS((4,))],
    )
    got_x = spread(packed_x)
    got_x, packed_dy = lax.optimization_barrier((got_x, packed_dy))
    got_dy = spread(packed_dy)

    weights = [w[:, 0, :] for w in (w_gate_q, w_up_q, w_down_q)]
    scales = [s[:, 0, :].T for s in (gate_scales, up_scales, down_scales)]
    cols = 256
    steps = hidden // cols
    raw = pltpu.VMEM((half, hidden), BF)
    send_a, slot_of = call(
        functools.partial(forward_kernel, n_local, top, cols),
        (shape(kept, hidden), shape(kept, rows)),
        (scales[0], got_x, weights[0]),
        limit=LIMIT_FORWARD,
        flops=2 * kept * half * hidden,
        moved=2 * half * hidden + 4 * rows * half,
        in_specs=[SMEM, HBM, HBM],
        out_specs=[VMEM, VMEM],
        scratch_shapes=[pltpu.VMEM((rows, half), BF), pltpu.VMEM((rows, META), BF)]
        + [pltpu.VMEM((kept, half), BF), raw, pltpu.VMEM((half, cols), BF)]
        + [SEMS((4,)), SEMS((steps,)), SEMS],
    )
    their_a = across(send_a, 1)
    rows_x, send_b = call(
        functools.partial(project_kernel, cols),
        (shape(kept, half), shape(kept, hidden)),
        (scales[1], slot_of, got_x, weights[1]),
        limit=LIMIT_DOWN,
        flops=2 * kept * half * hidden,
        moved=2 * half * hidden + 4 * rows * half,
        in_specs=[SMEM, VMEM, HBM, HBM],
        out_specs=[HBM, VMEM],
        scratch_shapes=[
            pltpu.VMEM((rows, half), BF), pltpu.VMEM((kept, half), BF), raw,
            pltpu.VMEM((half, cols), BF), SEMS((4,)), SEMS((steps,)), SEMS,
        ],
    )
    their_a, send_b = lax.optimization_barrier((their_a, send_b))
    their_b = across(send_b, 1)
    rows_dy, send_dh = call(
        functools.partial(project_kernel, cols),
        (shape(kept, half), shape(kept, hidden)),
        (scales[2], slot_of, got_dy, weights[2]),
        limit=LIMIT_DOWN,
        flops=2 * kept * half * hidden,
        moved=2 * half * hidden + 4 * rows * half,
        in_specs=[SMEM, VMEM, HBM, HBM],
        out_specs=[HBM, VMEM],
        scratch_shapes=[
            pltpu.VMEM((rows, half), BF), pltpu.VMEM((kept, half), BF), raw,
            pltpu.VMEM((half, cols), BF), SEMS((4,)), SEMS((steps,)), SEMS,
        ],
    )
    their_dh = across(send_dh, 1)
    chunk = 1024
    parts = half // chunk
    factor, hid, both_w = call(
        functools.partial(factor_kernel, chunk),
        (shape(2, kept, hidden), shape(kept, hidden), shape(half, 2 * hidden)),
        (scales[0], scales[1], send_a, send_b, their_a, their_b, weights[0], weights[1]),
        limit=LIMIT_FACTOR,
        flops=16 * kept * hidden,
        moved=8 * half * hidden,
        in_specs=[SMEM, SMEM] + [VMEM] * 4 + [HBM, HBM],
        out_specs=[VMEM] * 3,
        scratch_shapes=[raw, raw, SEMS((parts,)), SEMS((parts,))],
    )
    d_ab, dx = call(
        functools.partial(backward_kernel, chunk),
        (shape(2, kept, hidden), shape(rows, wide)),
        (factor, hid, send_dh, their_dh, slot_of, both_w),
        limit=LIMIT_BACKWARD,
        flops=4 * rows * half * hidden,
        moved=4 * half * hidden + 2 * rows * half,
        in_specs=[VMEM] * 5 + [HBM],
        out_specs=[HBM, HBM],
        scratch_shapes=[
            pltpu.VMEM((2, kept, hidden), BF),
            pltpu.VMEM((rows, 2 * hidden), BF),
            pltpu.VMEM((kept, META), BF),
            pltpu.VMEM((half, 2 * hidden), BF),
            pltpu.VMEM((rows, wide), BF),
            SEMS((parts,)),
            SEMS((parts,)),
            SEMS,
            SEMS,
        ],
    )
    returned = spread(dx)
    grads = [
        dot(left, right, ROWS).astype(BF)
        for left, right in ((rows_x, d_ab[0]), (rows_x, d_ab[1]), (rows_dy, hid))
    ]
    returned, *grads = lax.optimization_barrier((returned, *grads))
    blocks = call(
        functools.partial(combine_kernel, n_local, top),
        tuple(shape(tok, wide) for _ in range(n_group)),
        (returned, pick, column_meta),
        flops=2 * rows * column * half,
        limit=24,
        moved=2 * rows * half,
        in_specs=[VMEM] * 3,
        out_specs=[VMEM] * n_group,
    )
    back = [blocks[0]] + [across(blocks[m], m) for m in range(1, n_group)]
    grad_tokens, grad_gates = call(
        finish_kernel,
        (shape(tok, width), shape(top, tok)),
        tuple(back),
        limit=24,
        moved=tok * width * 6,
        grid=(1,),
        in_specs=[whole(tok, wide)] * 4,
        out_specs=[whole(tok, width), whole(top, tok)],
    )
    return (
        grad_tokens,
        grad_gates.T,
        grads[0][:, None, :],
        grads[1][:, None, :],
        grads[2][:, None, :],
    )


def solution(mesh):
    by_token = P(("group", "local"), None)
    by_expert = P("group", "local", None)
    return jax.shard_map(
        shards,
        mesh=mesh,
        in_specs=(by_token,) * 7 + (by_expert,) * 6,
        out_specs=(by_token,) * 2 + (by_expert,) * 3,
        check_vma=False,
    )
```
